256 devices in a mesh: grp: 8 (over z_lo, core), dp: 32 (over z_hi, y, x).
Axes of the slice: x: 4, y: 4, z: 8 (z_hi: 2, z_lo: 4; z = z_hi * 4 + z_lo), core: 2. Of those that a mesh axis runs over, the one named last changes fastest.
Arguments:
- patches: bfloat16 [262144, 1152], P(('grp', 'dp')), may hold values from -180 to 180
- patch_counts: int32 [1024], P(('grp', 'dp')), may hold values from 64 to 256, as said below
- pack_offsets: int32 [1024], P(('grp', 'dp')), may hold values from 0 to 960, as said below
- norm_gain: float32 [1152], replicated, may hold values from 0.1 to 1.9
- mlp_in: bfloat16 [1152, 4304], P('dp'), may hold values from -0.1875 to 0.1875
- mlp_out: bfloat16 [4304, 1152], P(None, 'dp'), may hold values from -0.09375 to 0.09375
- probe_query: bfloat16 [1152], replicated, may hold values from -4 to 4
- key_weight: bfloat16 [1152, 1152], replicated, may hold values from -0.1875 to 0.1875
- value_weight: bfloat16 [1152, 1152], replicated, may hold values from -0.1875 to 0.1875
- out_weight: bfloat16 [1152, 1152], replicated, may hold values from -0.1875 to 0.1875
- text_embed: bfloat16 [1024, 1152], P(('grp', 'dp')), may hold values from -6 to 6
- pair_label: int32 [1024], replicated, may hold values from 0 to 511
- logit_scale: float32 [1], replicated, may hold values from 4 to 16
- logit_bias: float32 [1], replicated, may hold values from -4 to -1
Outputs:
- loss: float32 [], replicated
- image_grad: float32 [1024, 1152], P(('grp', 'dp'))
- text_grad: float32 [1024, 1152], P(('grp', 'dp'))
The draws below stay inside these ranges and needn't reach their ends.
Inputs may be any that keep to these rules, and one draw needn't show every extreme that they name: `patch_counts`: the counts of the 4 images of one device sum to 512. `pack_offsets`: the images held in one pack occupy disjoint rows that end by row 1024; in every group some pack is filled completely.
All inputs are finite; a program needn't handle non-finite values.
Results may differ from the reference program's by a relative error of at most 0.008.
The reference program's roundings to bfloat16 on the way count: a program that leaves them out, or rounds other values in their place, can miss the bound.
Values may be sent and summed in bfloat16 or wider, within the bound.
A program may use at most 128 MiB of HBM per device.

```python
import math
import jax
import jax.numpy as jnp
from jax import lax

D = 1152
HEAD_DIM = 72
FF = 4304
IMG_DEV = 4
SLOT = 256
PACK = 1024
IMAGES = 1024
N_GRP = 8
N_DP = 32


def layout(key):
    group_count = N_GRP
    dp_count = N_DP
    stride = dp_count // IMG_DEV
    pieces = jax.random.split(key, 6)
    hot_pack = jax.random.randint(pieces[0], (group_count, 1), 0, dp_count)
    paired = jax.random.randint(pieces[1], (group_count, dp_count, 2), SLOT // 4, 3 * SLOT // 4 + 1)
    regular = jnp.stack([paired[..., 0], SLOT - paired[..., 0], paired[..., 1], SLOT - paired[..., 1]], axis=-1)
    first_part = jax.random.randint(pieces[2], (group_count, dp_count), SLOT // 4, SLOT // 2 + 1)
    second_part = jax.random.randint(pieces[3], (group_count, dp_count), SLOT // 4, 3 * SLOT // 4 + 1 - first_part)
    third_part = SLOT - first_part - second_part
    triple = jnp.stack([first_part, second_part, third_part], axis=-1)
    places = jnp.arange(dp_count)[None, :]
    distance = (hot_pack - places) % dp_count
    is_hot = distance % stride == 0
    hot_slot = (distance // stride)[..., None]
    ordinal = jnp.arange(IMG_DEV)
    rank_index = jnp.clip(jnp.where(ordinal < hot_slot, ordinal, ordinal - 1), 0, 2)
    rank_index = jnp.broadcast_to(rank_index, (group_count, dp_count, IMG_DEV))
    spread_counts = jnp.take_along_axis(triple, rank_index, axis=-1)
    hot_counts = jnp.where(ordinal == hot_slot, SLOT, spread_counts)
    counts = jnp.where(is_hot[..., None], hot_counts, regular).astype(jnp.int32)
    held_counts = jnp.stack([jnp.roll(counts[:, :, ordinal_value], ordinal_value * stride, axis=1) for ordinal_value in range(IMG_DEV)], axis=-1)
    pack_keys = jax.random.split(pieces[4], group_count * dp_count)
    orders = jax.vmap(lambda single: jax.random.permutation(single, IMG_DEV))(pack_keys).reshape(group_count, dp_count, IMG_DEV)
    gap_weight = jax.random.randint(pieces[5], (group_count, dp_count, IMG_DEV + 1), 1, 101)
    leftover = PACK - jnp.sum(held_counts, axis=-1, keepdims=True)
    gap_rows = leftover * gap_weight // jnp.sum(gap_weight, axis=-1, keepdims=True)
    ordered = jnp.take_along_axis(held_counts, orders, axis=-1)
    begins = jnp.cumsum(gap_rows[..., :IMG_DEV] + ordered, axis=-1) - ordered
    offsets = jnp.sum(jnp.where(orders[..., :, None] == ordinal[None, None, None, :], begins[..., :, None], 0), axis=-2)
    return (counts.reshape(-1), offsets.reshape(-1).astype(jnp.int32))


def draw_patch_counts(key, part):
    counts, offsets = layout(key)
    return counts


def draw_pack_offsets(key, part):
    counts, offsets = layout(key)
    return offsets


def draw_patches(key, part):
    key = jax.random.fold_in(key, 3)
    row_count = N_GRP * N_DP * PACK
    pieces = jax.random.split(key, 1)
    values = jnp.clip(jax.random.normal(pieces[0], (row_count, D), jnp.float32), -6.0, 6.0)
    return values.astype(jnp.bfloat16)


def draw_text_embed(key, part):
    key = jax.random.fold_in(key, 5)
    pieces = jax.random.split(key, 3)
    row_scale = jnp.exp(jax.random.uniform(pieces[1], (IMAGES, 1), jnp.float32, 0.0, math.log(10.0)))
    column_scale = jnp.exp(jax.random.uniform(pieces[2], (1, D), jnp.float32, -1.15, 1.15))
    base = jnp.clip(jax.random.normal(pieces[0], (IMAGES, D), jnp.float32), -6.0, 6.0)
    return (0.03 * base * row_scale * column_scale).astype(jnp.bfloat16)


def with_ends(drawn, rng, low, high):
    dims = drawn.shape
    spot = [jax.random.randint(jax.random.fold_in(rng, axis), (), 0, dims[axis]) for axis in range(len(dims))]
    drawn = drawn.at[tuple(spot)].set(low)
    longest = dims.index(max(dims))
    spot[longest] = (spot[longest] + 1) % dims[longest]
    return drawn.at[tuple(spot)].set(high)


def level_of(rng, dims, cuts, smallest, largest):
    def one(axis_at, blocks):
        draws = jax.random.uniform(jax.random.fold_in(jax.random.fold_in(rng, 6), axis_at), (blocks,), jnp.float32, smallest / len(cuts), largest / len(cuts))
        return jnp.repeat(jnp.exp(draws), dims[axis_at] // blocks).reshape((-1,) + (1,) * (len(dims) - axis_at - 1))

    level = one(*cuts[0])
    for cut in cuts[1:]:
        level = level * one(*cut)
    return level


def noise(stream_key, extent, scale, bound, cuts=(), kind=jnp.bfloat16):
    loudness = level_of(stream_key, extent, cuts, -0.22, 0.18) if cuts else 1.0
    values = jax.random.normal(stream_key, extent, jnp.float32) * scale * loudness
    return jnp.minimum(jnp.maximum(values, -bound), bound).astype(kind)


def setup_inputs(seed: int = 0) -> dict:
    key_list = jax.random.split(jax.random.key(seed), 15)
    patches = draw_patches(jax.random.fold_in(key_list[14], 71), 0)
    patch_counts = draw_patch_counts(jax.random.fold_in(key_list[14], 71), 0)
    pack_offsets = draw_pack_offsets(jax.random.fold_in(key_list[14], 71), 0)
    norm_gain = jnp.clip(1.0 + 0.18 * jax.random.normal(key_list[3], (D,), jnp.float32), 0.1, 1.9)
    mlp_in = noise(key_list[4], (D, FF), D ** -0.5, 0.1875, ((0, 32),))
    mlp_out = noise(key_list[5], (FF, D), FF ** -0.5, 0.09375, ((1, 32),))
    probe_query = noise(key_list[6], (D,), 1.0, 4.0)
    key_weight = noise(key_list[7], (D, D), D ** -0.5, 0.1875)
    value_weight = noise(key_list[8], (D, D), D ** -0.5, 0.1875)
    out_weight = noise(key_list[9], (D, D), D ** -0.5, 0.1875)
    text_embed = draw_text_embed(jax.random.fold_in(key_list[14], 71), 0)
    pair_label = with_ends(jax.random.randint(key_list[11], (IMAGES,), 0, IMAGES // 2), jax.random.fold_in(key_list[11], 1), 0, (IMAGES // 2) - 1).astype(jnp.int32)
    logit_scale = jnp.clip(jnp.exp(jax.random.uniform(key_list[12], (1,), jnp.float32, math.log(4.0), math.log(16.0))), 4.0, 16.0)
    logit_bias = jnp.clip(jax.random.uniform(key_list[13], (1,), jnp.float32, -4.0, -1.0), -4.0, -1.0)
    return dict(patches=patches, patch_counts=patch_counts, pack_offsets=pack_offsets, norm_gain=norm_gain, mlp_in=mlp_in, mlp_out=mlp_out, probe_query=probe_query, key_weight=key_weight, value_weight=value_weight, out_weight=out_weight, text_embed=text_embed, pair_label=pair_label, logit_scale=logit_scale, logit_bias=logit_bias)


EPSILON = 1e-06

def feed_forward(patch_rows, norm_gain, mlp_in, mlp_out):
    widened = patch_rows.astype(jnp.float32)
    center = lax.optimization_barrier(jnp.mean(widened, axis=1, keepdims=True))
    spread = lax.optimization_barrier(jnp.mean(jnp.square(widened - center), axis=1, keepdims=True))
    normed = ((widened - center) * lax.rsqrt(spread + EPSILON) * norm_gain).astype(jnp.bfloat16)
    hidden = jnp.dot(normed, mlp_in, preferred_element_type=jnp.float32)
    active = jax.nn.gelu(hidden, approximate=True).astype(jnp.bfloat16)
    return (widened + jnp.dot(active, mlp_out, preferred_element_type=jnp.float32)).astype(jnp.bfloat16)

def head_keys(key_weight, probe_query):
    model_width = key_weight.shape[0]
    head_count = model_width // HEAD_DIM
    head_of_row = jnp.arange(model_width) // HEAD_DIM
    probe_block = jnp.where(head_of_row[:, None] == jnp.arange(head_count)[None, :], probe_query[:, None], jnp.zeros((), probe_query.dtype))
    return (jnp.dot(key_weight, probe_block, preferred_element_type=jnp.float32) / math.sqrt(HEAD_DIM)).astype(jnp.bfloat16)

def attend(states, member, head_key, value_weight, out_weight):
    row_count, model_width = states.shape
    image_count = member.shape[1]
    head_count = head_key.shape[1]
    scores = jnp.dot(states, head_key, preferred_element_type=jnp.float32)
    masked = jnp.where(member[:, :, None], scores[:, None, :], -1e+30)
    highest = lax.optimization_barrier(jnp.max(masked, axis=0))
    raised = jnp.exp(masked - highest[None])
    denominator = lax.optimization_barrier(jnp.sum(raised, axis=0))
    weights_low = (raised / denominator[None]).astype(jnp.bfloat16).reshape(row_count, image_count * head_count)
    mean_states = jnp.dot(weights_low.T, states, preferred_element_type=jnp.float32).astype(jnp.bfloat16)
    per_head = mean_states.reshape(image_count, head_count, model_width)
    head_values = jnp.einsum('khd,dhe->khe', per_head.astype(jnp.float32), value_weight.reshape(model_width, head_count, HEAD_DIM).astype(jnp.float32))
    mixed = head_values.astype(jnp.bfloat16).reshape(image_count, model_width)
    return jnp.dot(mixed, out_weight, preferred_element_type=jnp.float32)

def reference(patches, patch_counts, pack_offsets, norm_gain, mlp_in, mlp_out, probe_query, key_weight, value_weight, out_weight, text_embed, pair_label, logit_scale, logit_bias):
    head_key = head_keys(key_weight, probe_query)
    stride = N_DP // IMG_DEV
    slot_index = jnp.arange(IMG_DEV, dtype=jnp.int32)
    row_index = jnp.arange(2 * SLOT, dtype=jnp.int32)

    def pool_owner(owner_index):
        group_index = owner_index // N_DP
        place_index = owner_index % N_DP
        pack_index = group_index * N_DP + (place_index + slot_index * stride) % N_DP
        counts = lax.dynamic_slice_in_dim(patch_counts, (owner_index * IMG_DEV).astype(jnp.int32), IMG_DEV)
        offsets = pack_offsets[pack_index * IMG_DEV + slot_index]
        bounds_end = jnp.cumsum(counts)
        starts = bounds_end - counts
        segment = lax.optimization_barrier(jnp.sum((row_index[:, None] >= bounds_end[None, :]).astype(jnp.int32), axis=1))
        source = pack_index[segment] * PACK + offsets[segment] + row_index - starts[segment]
        gathered = jnp.take(patches, source.astype(jnp.int32), axis=0)
        states = feed_forward(gathered, norm_gain, mlp_in, mlp_out)
        member = segment[:, None] == slot_index[None, :]
        return attend(states, member, head_key, value_weight, out_weight)
    pooled = lax.map(pool_owner, jnp.arange(N_GRP * N_DP, dtype=jnp.int32)).reshape(IMAGES, -1)
    logit_mult = logit_scale[0]
    logit_shift = logit_bias[0]
    image_inv = lax.rsqrt(lax.optimization_barrier(jnp.sum(pooled * pooled, axis=1, keepdims=True)) + EPSILON)
    image_unit = pooled * image_inv
    image_low = image_unit.astype(jnp.bfloat16)
    text_wide = text_embed.astype(jnp.float32)
    text_inv = lax.rsqrt(lax.optimization_barrier(jnp.sum(text_wide * text_wide, axis=1, keepdims=True)) + EPSILON)
    text_unit = text_wide * text_inv
    text_low = text_unit.astype(jnp.bfloat16)
    logits = logit_mult * jnp.dot(image_low, text_low.T, preferred_element_type=jnp.float32) + logit_shift
    target_sign = jnp.where(pair_label[:, None] == pair_label[None, :], 1.0, -1.0).astype(jnp.float32)
    loss_value = jnp.sum(-jax.nn.log_sigmoid(target_sign * logits)) / IMAGES
    slope_low = (logit_mult * -target_sign * jax.nn.sigmoid(-target_sign * logits)).astype(jnp.bfloat16)
    image_push = jnp.dot(slope_low, text_low, preferred_element_type=jnp.float32)
    text_push = jnp.dot(slope_low.T, image_low, preferred_element_type=jnp.float32)
    image_grad = (image_push - image_unit * lax.optimization_barrier(jnp.sum(image_unit * image_push, axis=1, keepdims=True))) * image_inv
    text_grad = (text_push - text_unit * lax.optimization_barrier(jnp.sum(text_unit * text_push, axis=1, keepdims=True))) * text_inv
    return (loss_value, image_grad, text_grad)
```

```python
import math

import jax
import jax.numpy as jnp
from jax import lax
from jax.experimental import pallas as pl
from jax.experimental.pallas import tpu as pltpu
from jax.sharding import PartitionSpec as P

MESH = pl.DeviceIdType.MESH
F32 = jnp.float32
BF16 = jnp.bfloat16
I32 = jnp.int32

EPSILON = 1e-06
D = 1152
FF = 4304
HEAD_DIM = 72
HEADS = 16
PACK = 1024
TEXTS = 1024
SHARD = 36
SLOT_ROWS = 48
LANES = 128
CHUNKS = 17
HALF = CHUNKS * LANES
BLOCK = 4 * SHARD
GROUP = 4 * BLOCK
TILE = 256

LAG_A, LAG_B, LAG_C, LAG_D, LAG_E = 1, 2, 3, 4, 5
TICKS = CHUNKS + LAG_E

Z, A_MINUS, A_PLUS, A_FAR, B_MINUS, B_PLUS, B_FAR, SIB = range(8)

NT = (((1,), (1,)), ((), ()))


def gelu(hidden):
    c1 = math.sqrt(2.0 / math.pi)
    c2 = c1 * 0.044715
    inner = hidden * (c1 + c2 * (hidden * hidden))
    half = 0.5 * hidden
    return (half + half * jnp.tanh(inner)).astype(BF16)


def kernel(
    patches, counts, offsets, gain, win, woutt, probe, key_w, value_w, out_w, text, labels, scale, bias,
    loss_out, igrad_out, tgrad_out,
    xbuf, normed, acc, G, a2a_s, a2a_r, compact, T, line_f, tx_s, tx_r, ix_s, ix_r, PI, tcol,
    ps_s, ps_r, ig_s, ig_r, cn_s, cn_r, hk, kw, vw, ow, ilab, tlab, ls_s, ls_r,
    loc_sem, g_ss, g_rs, x_ss, x_rs, tx_ss, tx_rs, ty_ss, ty_rs, tz_ss, tz_rs, ts_ss, ts_rs,
    ix_ss, ix_rs, iy_ss, iy_rs, ps_ss, ps_rs, ig_ss, ig_rs, cn_ss, cn_rs,
    l1_ss, l1_rs, l2_ss, l2_rs, l3_ss, l3_rs,
):
    g = lax.axis_index("grp")
    d = lax.axis_index("dp")
    k = lax.rem(g, 2)
    zl = lax.div(g, 2)
    x = lax.rem(d, 4)
    y = lax.rem(lax.div(d, 4), 4)
    zh = lax.div(d, 16)
    z = zh * 4 + zl

    def dev(x_, y_, z_, k_):
        return (lax.rem(z_, 4) * 2 + k_, lax.div(z_, 4) * 16 + y_ * 4 + x_)

    def m4(v):
        return lax.rem(v, 4)

    def m8(v):
        return lax.rem(v, 8)

    sib = dev(x, y, z, 1 - k)
    xs = [dev(m4(x + i), y, z, k) for i in (1, 2, 3)]
    zs = [dev(x, y, m8(z + i), k) for i in range(1, 8)]
    group_dev = [(g, lax.rem(d + 8 * j, 32)) for j in range(4)]

    def rcopy(src, dst, ss, rs, to):
        return pltpu.make_async_remote_copy(
            src_ref=src, dst_ref=dst, send_sem=ss, recv_sem=rs, device_id=to, device_id_type=MESH
        )

    def wait_recv(ref, rs):
        rcopy(ref, ref, loc_sem.at[0], rs, sib).wait_recv()

    def wait_send(ref, ss):
        rcopy(ref, ref, ss, loc_sem.at[0], sib).wait_send()

    barrier = pltpu.get_barrier_semaphore()
    partners = list(xs) + list(zs) + [sib]
    for i in (1, 2, 3):
        for c_ in (0, 1):
            partners.append(dev(x, m4(y + i), z, c_))
    partners.append(dev(x, m4(y + 2), m8(z + 4), k))
    for p in partners:
        pl.semaphore_signal(barrier, inc=1, device_id=p, device_id_type=MESH)

    local = [
        pltpu.make_async_copy(patches, xbuf, loc_sem.at[1]),
        pltpu.make_async_copy(key_w, kw, loc_sem.at[2]),
        pltpu.make_async_copy(value_w, vw, loc_sem.at[3]),
        pltpu.make_async_copy(out_w, ow, loc_sem.at[4]),
    ]
    for cp in local:
        cp.start()

    source = k == zh

    @pl.when(source)
    def _():
        for part in range(4):
            shard = win if part < 2 else woutt
            if part % 2 == 0:
                a2a_s[part, 0:SHARD, :] = shard[:, 0:HALF]
            else:
                a2a_s[part, :, HALF - LANES:HALF] = jnp.zeros((SLOT_ROWS, LANES), BF16)
                a2a_s[part, 0:SHARD, 0:FF - HALF] = shard[:, HALF:FF]

    text_wide = text[...].astype(F32)
    text_inv = lax.rsqrt(jnp.sum(text_wide * text_wide, axis=1, keepdims=True) + EPSILON)
    text_unit = text_wide * text_inv
    tx_s[...] = jnp.zeros((16, D), BF16)
    tx_s[0:4, :] = text_unit.astype(BF16)
    for j in range(4):
        cn_s[j] = jnp.full((8, LANES), counts[j], I32)

    pl.semaphore_wait(barrier, len(partners))

    @pl.when(source)
    def _():
        for i in range(3):
            to_x = m4(x + i + 1)
            rcopy(a2a_s.at[to_x], a2a_r.at[x], x_ss.at[i], x_rs.at[x], xs[i]).start()
        a2a_r[x] = a2a_s[x]

    for i in range(3):
        rcopy(tx_s, tx_r.at[x], tx_ss.at[i], tx_rs.at[x], xs[i]).start()
    tx_r[x] = tx_s[...]
    for j in (1, 2, 3):
        rcopy(cn_s.at[j], cn_r.at[j], cn_ss.at[j], cn_rs.at[j], group_dev[j]).start()
    cn_r[0] = cn_s[0]

    a = jnp.where(k == 0, y, x)
    b = jnp.where(k == 0, x, y)

    def along(axis_is_a, step):
        move_y = jnp.where(k == 0, 1, 0) if axis_is_a else jnp.where(k == 0, 0, 1)
        return dev(m4(x + (1 - move_y) * step), m4(y + move_y * step), z, k)

    a_plus, a_minus = along(True, 1), along(True, 3)
    b_plus, b_minus = along(False, 1), along(False, 3)

    def a_block(c, at):
        return G.at[c, k, b, pl.ds(pl.multiple_of(at * BLOCK, 16), BLOCK), :]

    def b_group(c, at):
        return G.at[c, k, at]

    @pl.when(source)
    def _():
        for i in (1, 2, 3):
            s = m4(x + i)
            wait_recv(a2a_r.at[s], x_rs.at[s])
        for s in range(4):
            compact[s * SHARD:(s + 1) * SHARD, :] = a2a_r[s, 0:SHARD, :].astype(F32)
        for c in range(CHUNKS):
            G[c, k, b, pl.ds(pl.multiple_of(a * BLOCK, 16), BLOCK), :] = compact[
                :, c * LANES:(c + 1) * LANES
            ].astype(BF16)

    edge = jnp.logical_or(zl == 0, zl == 3)
    outward = jnp.where(zl == 3, 1, 7)
    z_to = dev(x, y, m8(z + jnp.where(source, outward, 8 - outward)), k)

    def t_block(zl_, k_, zh_):
        return T.at[zl_, k_, zh_]

    def z_parts(step):
        zz = m8(z + step)
        return m4(zz), lax.div(zz, 4)

    def text_ring(step):
        zl_, zh_ = z_parts(step)
        return T.at[zl_, k, zh_]

    z_plus, z_minus = zs[0], zs[6]
    own_t = pl.ds(pl.multiple_of(y * 16, 16), 16)

    def gather_line(received, wide):
        for s in range(4):
            wide[4 * s:4 * s + 4, :] = received[s, 0:4, :].astype(F32)
        return wide[...].astype(BF16)

    def label_cols(ids):
        rows = ids.shape[0]
        lanes = lax.broadcasted_iota(I32, (rows, TEXTS), 1)
        row = jnp.broadcast_to(labels[...].astype(F32), (rows, TEXTS))
        return jnp.sum(jnp.where(lanes == ids, row, 0.0), axis=1, keepdims=True)

    def tick(t, carry):
        @pl.when(t < CHUNKS)
        def _():
            c = t
            own = a_block(c, a)

            @pl.when(jnp.logical_not(source))
            def _():
                wait_recv(own, g_rs.at[Z, c])

            @pl.when(edge)
            def _():
                rcopy(own, own, g_ss.at[Z, c], g_rs.at[Z, c], z_to).start()

            rcopy(own, own, g_ss.at[A_MINUS, c], g_rs.at[A_MINUS, c], a_plus).start()
            rcopy(own, own, g_ss.at[A_PLUS, c], g_rs.at[A_PLUS, c], a_minus).start()

        @pl.when(jnp.logical_and(t >= LAG_A, t < CHUNKS + LAG_A))
        def _():
            c = t - LAG_A
            even = lax.rem(c, 2) == 0
            blk = a_block(c, m4(a + jnp.where(even, 3, 1)))
            wait_recv(blk, g_rs.at[jnp.where(even, A_MINUS, A_PLUS), c])
            to = tuple(jnp.where(even, p, m) for p, m in zip(a_plus, a_minus))
            rcopy(blk, blk, g_ss.at[A_FAR, c], g_rs.at[A_FAR, c], to).start()

        @pl.when(jnp.logical_and(t >= LAG_B, t < CHUNKS + LAG_B))
        def _():
            c = t - LAG_B
            even = lax.rem(c, 2) == 0
            wait_recv(a_block(c, m4(a + jnp.where(even, 1, 3))), g_rs.at[jnp.where(even, A_PLUS, A_MINUS), c])
            wait_recv(a_block(c, m4(a + 2)), g_rs.at[A_FAR, c])
            grp = b_group(c, b)
            rcopy(grp, grp, g_ss.at[B_MINUS, c], g_rs.at[B_MINUS, c], b_plus).start()
            rcopy(grp, grp, g_ss.at[B_PLUS, c], g_rs.at[B_PLUS, c], b_minus).start()

        @pl.when(jnp.logical_and(t >= LAG_C, t < CHUNKS + LAG_C))
        def _():
            c = t - LAG_C
            even = lax.rem(c, 2) == 0
            grp = b_group(c, m4(b + jnp.where(even, 3, 1)))
            wait_recv(grp, g_rs.at[jnp.where(even, B_MINUS, B_PLUS), c])
            to = tuple(jnp.where(even, p, m) for p, m in zip(b_plus, b_minus))
            rcopy(grp, grp, g_ss.at[B_FAR, c], g_rs.at[B_FAR, c], to).start()

        @pl.when(jnp.logical_and(t >= LAG_D, t < CHUNKS + LAG_D))
        def _():
            c = t - LAG_D
            even = lax.rem(c, 2) == 0
            wait_recv(b_group(c, m4(b + jnp.where(even, 1, 3))), g_rs.at[jnp.where(even, B_PLUS, B_MINUS), c])
            wait_recv(b_group(c, m4(b + 2)), g_rs.at[B_FAR, c])
            half = G.at[c, k]
            rcopy(half, half, g_ss.at[SIB, c], g_rs.at[SIB, c], sib).start()

        @pl.when(t == 0)
        def _():
            for i in (1, 2, 3):
                s = m4(x + i)
                wait_recv(tx_r.at[s], tx_rs.at[s])
            T[zl, k, zh, own_t, :] = gather_line(tx_r, line_f)
            blk = T.at[zl, k, zh, own_t, :]
            for i in (1, 2, 3):
                rcopy(blk, blk, ty_ss.at[i - 1], ty_rs.at[y], dev(x, m4(y + i), z, k)).start()

        @pl.when(t == 1)
        def _():
            for i in (1, 2, 3):
                yy = m4(y + i)
                wait_recv(T.at[zl, k, zh, pl.ds(pl.multiple_of(yy * 16, 16), 16), :], ty_rs.at[yy])
            blk = text_ring(0)
            rcopy(blk, blk, tz_ss.at[0, 0], tz_rs.at[0, 0], z_plus).start()
            rcopy(blk, blk, tz_ss.at[1, 0], tz_rs.at[1, 0], z_minus).start()

        for hop in (1, 2):

            @pl.when(t == 1 + 2 * hop)
            def _():
                low, high = text_ring(8 - hop), text_ring(hop)
                wait_recv(low, tz_rs.at[0, hop - 1])
                wait_recv(high, tz_rs.at[1, hop - 1])
                rcopy(low, low, tz_ss.at[0, hop], tz_rs.at[0, hop], z_plus).start()
                rcopy(high, high, tz_ss.at[1, hop], tz_rs.at[1, hop], z_minus).start()

        @pl.when(t == 7)
        def _():
            low, high = text_ring(5), text_ring(3)
            wait_recv(low, tz_rs.at[0, 2])
            wait_recv(high, tz_rs.at[1, 2])

            @pl.when(k == 0)
            def _():
                rcopy(low, low, tz_ss.at[0, 3], tz_rs.at[0, 3], z_plus).start()

            @pl.when(k == 1)
            def _():
                rcopy(high, high, tz_ss.at[0, 3], tz_rs.at[0, 3], z_minus).start()

        @pl.when(t == 9)
        def _():
            wait_recv(text_ring(4), tz_rs.at[0, 3])
            mine = T.at[:, k]
            rcopy(mine, mine, ts_ss.at[0], ts_rs.at[0], sib).start()

        @pl.when(t == 0)
        def _():
            local[0].wait()

        @pl.when(t < PACK // TILE)
        def _():
            sl = pl.ds(pl.multiple_of(t * TILE, TILE), TILE)
            wide = xbuf[sl, :].astype(F32)
            center = jnp.mean(wide, axis=1, keepdims=True)
            off = wide - center
            spread = jnp.mean(off * off, axis=1, keepdims=True)
            normed[sl, :] = (off * lax.rsqrt(spread + EPSILON) * gain[...]).astype(BF16)
            acc[sl, :] = wide

        @pl.when(t == 4)
        def _():
            local[1].wait()
            head_of = lax.div(lax.broadcasted_iota(I32, (HEADS, D), 1), HEAD_DIM)
            own_head = head_of == lax.broadcasted_iota(I32, (HEADS, D), 0)
            block = jnp.where(own_head, jnp.broadcast_to(probe[...].astype(F32), (HEADS, D)), 0.0)
            keys = lax.dot_general(block.astype(BF16), kw[...], NT, preferred_element_type=F32)
            hk[...] = (keys / math.sqrt(HEAD_DIM)).astype(BF16)

            pos = lax.broadcasted_iota(I32, (LANES, 1), 0)
            slot = lax.rem(pos, 4)
            px = lax.rem(lax.div(pos, 4), 4)
            py = lax.rem(lax.div(pos, 16), 4)
            pk = lax.div(pos, 64)
            owner = lax.rem(16 * zh + 4 * py + px + 32 - 8 * slot, 32)
            ids = 4 * ((2 * zl + pk) * 32 + owner) + slot
            hot = lax.broadcasted_iota(I32, (LANES, TEXTS), 1) == ids
            hot = jnp.where(hot, 1.0, 0.0).astype(BF16)
            lab = labels[...]
            high = lax.div(lab, 16)
            low = lab - 16 * high
            pair = jnp.where(
                lax.broadcasted_iota(I32, (16, TEXTS), 0) == 0,
                jnp.broadcast_to(high, (16, TEXTS)),
                jnp.broadcast_to(low, (16, TEXTS)),
            ).astype(F32).astype(BF16)
            rows = lax.dot_general(pair, hot, NT, preferred_element_type=F32)
            ilab[...] = jnp.broadcast_to(16.0 * rows[0:1, :] + rows[1:2, :], (8, LANES))
            tpos = lax.broadcasted_iota(I32, (64, 1), 0)
            tz = lax.div(tpos, 8)
            tid = m4(tz) * 256 + k * 128 + lax.div(tz, 4) * 64 + y * 16 + x * 4 + m4(tpos)
            tlab[...] = jnp.broadcast_to(label_cols(tid), (64, LANES))

        @pl.when(t >= LAG_E)
        def _():
            c = t - LAG_E
            wait_recv(G.at[c, 1 - k], g_rs.at[SIB, c])

            def part(p):
                pieces = [G[c, 0, p]]
                for yy in range(4):
                    pieces.append(G[c, 1, yy, p * BLOCK:(p + 1) * BLOCK, :])
                return jnp.concatenate(pieces, axis=0)

            w1 = jnp.concatenate([part(0), part(1)], axis=1)
            w2 = jnp.concatenate([part(2), part(3)], axis=1)
            for r in range(PACK // TILE):
                sl = slice(r * TILE, (r + 1) * TILE)
                hidden = jnp.dot(normed[sl, :], w1, preferred_element_type=F32)
                acc[sl, :] += lax.dot_general(gelu(hidden), w2, NT, preferred_element_type=F32)

        return carry

    lax.fori_loop(0, TICKS, tick, 0)

    states = normed
    states[...] = acc[...].astype(BF16)
    scores = lax.dot_general(hk[...], states[...], NT, preferred_element_type=F32)
    row = lax.broadcasted_iota(I32, (HEADS, PACK), 1)
    all_weights = []
    for j in range(4):
        if j > 0:
            wait_recv(cn_r.at[j], cn_rs.at[j])
        first = offsets[j]
        count = cn_r[j][0:1, 0:1]
        member = jnp.logical_and(row >= first, row < first + count)
        masked = jnp.where(member, scores, -1e30)
        highest = jnp.max(masked, axis=1, keepdims=True)
        raised = jnp.exp(masked - highest)
        all_weights.append(raised / jnp.sum(raised, axis=1, keepdims=True))
    weights = jnp.concatenate(all_weights, axis=0).astype(BF16)
    mean_states = jnp.dot(weights, states[...], preferred_element_type=F32).astype(BF16)
    local[2].wait()
    local[3].wait()
    full = jnp.dot(mean_states, vw[...], preferred_element_type=F32)
    head_of = lax.div(lax.broadcasted_iota(I32, (HEADS, D), 1), HEAD_DIM)
    own_head = head_of == lax.broadcasted_iota(I32, (HEADS, D), 0)
    values = [
        jnp.sum(jnp.where(own_head, full[HEADS * j:HEADS * (j + 1), :], 0.0), axis=0, keepdims=True)
        for j in range(4)
    ]
    mixed = jnp.concatenate(values + [jnp.zeros((12, D), F32)], axis=0).astype(BF16)
    pooled = jnp.dot(mixed, ow[...], preferred_element_type=F32)[0:8, :]
    image_inv = lax.rsqrt(jnp.sum(pooled * pooled, axis=1, keepdims=True) + EPSILON)
    image_unit = pooled * image_inv
    ix_s[...] = jnp.concatenate([image_unit, jnp.zeros((8, D), F32)], axis=0).astype(BF16)

    for i in range(3):
        rcopy(ix_s, ix_r.at[x], ix_ss.at[i], ix_rs.at[x], xs[i]).start()
    ix_r[x] = ix_s[...]

    mult = scale[0]
    shift = bias[0]

    wait_recv(T.at[:, 1 - k], ts_rs.at[0])
    texts = T[...].reshape(TEXTS, D)
    own_logits = mult * lax.dot_general(ix_s[...], texts, NT, preferred_element_type=F32) + shift
    slot = lax.broadcasted_iota(I32, (16, 1), 0)
    slot4 = m4(slot)
    own_ids = 4 * (g * 32 + lax.rem(d + 32 - 8 * slot4, 32)) + slot4
    own_lab = label_cols(own_ids)
    sign = jnp.where(own_lab == labels[...].astype(F32), 1.0, -1.0)
    signed = sign * own_logits
    terms = jnp.log1p(jnp.exp(-jnp.abs(signed))) + jnp.maximum(-signed, 0.0)
    terms = jnp.where(slot < 4, terms, 0.0)
    part_loss = jnp.sum(jnp.sum(terms, axis=1, keepdims=True), axis=0, keepdims=True)
    ls_s[0] = jnp.broadcast_to(part_loss, (8, LANES))
    for i in range(3):
        rcopy(ls_s.at[0], ls_r.at[0, x], l1_ss.at[i], l1_rs.at[x], xs[i]).start()
    ls_r[0, x] = ls_s[0]

    for i in (1, 2, 3):
        s = m4(x + i)
        wait_recv(ix_r.at[s], ix_rs.at[s])
    PI[k, own_t, :] = gather_line(ix_r, line_f)
    others = [(m4(y + i), c_) for i in (1, 2, 3) for c_ in (0, 1)]
    to_plane = [dev(x, yy, z, c_) for yy, c_ in others] + [sib]
    blk = PI.at[k, own_t, :]
    for i, to in enumerate(to_plane):
        rcopy(blk, blk, iy_ss.at[i], iy_rs.at[k, y], to).start()

    for i in (1, 2, 3):
        s = m4(x + i)
        wait_recv(ls_r.at[0, s], l1_rs.at[s])
    ls_s[1] = ls_r[0, 0] + ls_r[0, 1] + ls_r[0, 2] + ls_r[0, 3]
    me8 = k * 4 + y
    for i, to in enumerate(to_plane):
        rcopy(ls_s.at[1], ls_r.at[1, me8], l2_ss.at[i], l2_rs.at[me8], to).start()
    ls_r[1, me8] = ls_s[1]

    own_slope = (mult * -sign * jax.nn.sigmoid(-signed)).astype(BF16)
    image_push = jnp.dot(own_slope, texts, preferred_element_type=F32)[0:8, :]
    image_grad = (
        image_push - image_unit * jnp.sum(image_unit * image_push, axis=1, keepdims=True)
    ) * image_inv
    for j in range(4):
        ig_s[j] = image_grad[j:j + 1, :]
    for j in (1, 2, 3):
        rcopy(ig_s.at[j], ig_r.at[j], ig_ss.at[j], ig_rs.at[j], group_dev[4 - j]).start()
    ig_r[0] = ig_s[0]

    for zz in range(8):
        block = T[zz % 4, k, zz // 4, own_t, :].astype(F32)
        mine = jnp.zeros((4, D), F32)
        for s in range(4):
            mine = mine + jnp.where(x == s, 1.0, 0.0) * block[4 * s:4 * s + 4, :]
        tcol[8 * zz:8 * zz + 4, :] = mine
        tcol[8 * zz + 4:8 * zz + 8, :] = jnp.zeros((4, D), F32)

    for yy, c_ in others + [(y, 1 - k)]:
        wait_recv(PI.at[c_, pl.ds(pl.multiple_of(yy * 16, 16), 16), :], iy_rs.at[c_, yy])
    plane = PI[...].reshape(LANES, D)
    plane_logits = mult * lax.dot_general(
        tcol[...].astype(BF16), plane, NT, preferred_element_type=F32
    ) + shift
    plane_sign = jnp.where(tlab[...] == ilab[0:1, :], 1.0, -1.0)
    plane_slope = (mult * -plane_sign * jax.nn.sigmoid(-plane_sign * plane_logits)).astype(BF16)
    push = jnp.dot(plane_slope, plane, preferred_element_type=F32)
    for zz in range(8):
        ps_s[zz] = push[8 * zz:8 * zz + 8, :]
    for i in range(7):
        to_z = m8(z + i + 1)
        rcopy(ps_s.at[to_z], ps_r.at[z], ps_ss.at[i], ps_rs.at[z], zs[i]).start()
    ps_r[z] = ps_s[z]

    for yy, c_ in others + [(y, 1 - k)]:
        wait_recv(ls_r.at[1, c_ * 4 + yy], l2_rs.at[c_ * 4 + yy])
    total = ls_r[1, 0]
    for i in range(1, 8):
        total = total + ls_r[1, i]
    ls_s[2] = total
    for i in range(7):
        rcopy(ls_s.at[2], ls_r.at[2, z], l3_ss.at[i], l3_rs.at[z], zs[i]).start()
    ls_r[2, z] = ls_s[2]

    for j in (1, 2, 3):
        wait_recv(ig_r.at[j], ig_rs.at[j])
    for j in range(4):
        igrad_out[j:j + 1, :] = ig_r[j]

    for i in range(1, 8):
        zz = m8(z + i)
        wait_recv(ps_r.at[zz], ps_rs.at[zz])
    text_push = ps_r[0]
    for i in range(1, 8):
        text_push = text_push + ps_r[i]
    text_push = text_push[0:4, :]
    tgrad_out[...] = (
        text_push - text_unit * jnp.sum(text_unit * text_push, axis=1, keepdims=True)
    ) * text_inv

    for i in range(1, 8):
        zz = m8(z + i)
        wait_recv(ls_r.at[2, zz], l3_rs.at[zz])
    total = ls_r[2, 0]
    for i in range(1, 8):
        total = total + ls_r[2, i]
    loss_out[...] = total[0:1, 0:1] / float(TEXTS)

    def drain(c, carry):
        own = a_block(c, a)

        @pl.when(edge)
        def _():
            wait_send(own, g_ss.at[Z, c])

        for kind in (A_MINUS, A_PLUS, A_FAR):
            wait_send(own, g_ss.at[kind, c])
        for kind in (B_MINUS, B_PLUS, B_FAR):
            wait_send(b_group(c, b), g_ss.at[kind, c])
        wait_send(G.at[c, k], g_ss.at[SIB, c])
        return carry

    lax.fori_loop(0, CHUNKS, drain, 0)

    @pl.when(source)
    def _():
        for i in range(3):
            wait_send(a2a_s.at[0], x_ss.at[i])

    for i in range(3):
        wait_send(tx_s, tx_ss.at[i])
        wait_send(T.at[zl, k, zh, own_t, :], ty_ss.at[i])
        wait_send(ix_s, ix_ss.at[i])
        wait_send(ls_s.at[0], l1_ss.at[i])
        wait_send(cn_s.at[i + 1], cn_ss.at[i + 1])
        wait_send(ig_s.at[i + 1], ig_ss.at[i + 1])
        wait_send(text_ring(0), tz_ss.at[0, i])
        wait_send(text_ring(0), tz_ss.at[1, i])
    wait_send(text_ring(0), tz_ss.at[0, 3])
    wait_send(T.at[:, k], ts_ss.at[0])
    for i in range(7):
        wait_send(PI.at[k, own_t, :], iy_ss.at[i])
        wait_send(ls_s.at[1], l2_ss.at[i])
        wait_send(ps_s.at[0], ps_ss.at[i])
        wait_send(ls_s.at[2], l3_ss.at[i])


def per_device(
    patches, patch_counts, pack_offsets, norm_gain, mlp_in, mlp_out, probe_query, key_weight,
    value_weight, out_weight, text_embed, pair_label, logit_scale, logit_bias,
):
    vmem = pl.BlockSpec(memory_space=pltpu.VMEM)
    smem = pl.BlockSpec(memory_space=pltpu.SMEM)
    anywhere = pl.BlockSpec(memory_space=pl.ANY)
    dma = pltpu.SemaphoreType.DMA
    loss, image_grad, text_grad = pl.pallas_call(
        kernel,
        out_shape=(
            jax.ShapeDtypeStruct((1, 1), F32),
            jax.ShapeDtypeStruct((4, D), F32),
            jax.ShapeDtypeStruct((4, D), F32),
        ),
        in_specs=[
            anywhere, smem, smem, vmem, vmem, vmem, vmem, anywhere, anywhere, anywhere, vmem, vmem, smem, smem,
        ],
        out_specs=(vmem, vmem, vmem),
        scratch_shapes=[
            pltpu.VMEM((PACK, D), BF16),
            pltpu.VMEM((PACK, D), BF16),
            pltpu.VMEM((PACK, D), F32),
            pltpu.VMEM((CHUNKS, 2, 4, GROUP, LANES), BF16),
            pltpu.VMEM((4, SLOT_ROWS, HALF), BF16),
            pltpu.VMEM((4, SLOT_ROWS, HALF), BF16),
            pltpu.VMEM((BLOCK, HALF), F32),
            pltpu.VMEM((4, 2, 2, 64, D), BF16),
            pltpu.VMEM((16, D), F32),
            pltpu.VMEM((16, D), BF16),
            pltpu.VMEM((4, 16, D), BF16),
            pltpu.VMEM((16, D), BF16),
            pltpu.VMEM((4, 16, D), BF16),
            pltpu.VMEM((2, 64, D), BF16),
            pltpu.VMEM((64, D), F32),
            pltpu.VMEM((8, 8, D), F32),
            pltpu.VMEM((8, 8, D), F32),
            pltpu.VMEM((4, 1, D), F32),
            pltpu.VMEM((4, 1, D), F32),
            pltpu.VMEM((4, 8, LANES), I32),
            pltpu.VMEM((4, 8, LANES), I32),
            pltpu.VMEM((HEADS, D), BF16),
            pltpu.VMEM((D, D), BF16),
            pltpu.VMEM((D, D), BF16),
            pltpu.VMEM((D, D), BF16),
            pltpu.VMEM((8, LANES), F32),
            pltpu.VMEM((64, LANES), F32),
            pltpu.VMEM((3, 8, LANES), F32),
            pltpu.VMEM((3, 8, 8, LANES), F32),
            dma((5,)),
            dma((8, CHUNKS)), dma((8, CHUNKS)),
            dma((3,)), dma((4,)),
            dma((3,)), dma((4,)),
            dma((3,)), dma((4,)),
            dma((2, 4)), dma((2, 4)),
            dma((1,)), dma((1,)),
            dma((3,)), dma((4,)),
            dma((7,)), dma((2, 4)),
            dma((7,)), dma((8,)),
            dma((4,)), dma((4,)),
            dma((4,)), dma((4,)),
            dma((3,)), dma((4,)),
            dma((7,)), dma((8,)),
            dma((7,)), dma((8,)),
        ],
        compiler_params=pltpu.CompilerParams(
            collective_id=0, has_side_effects=True, vmem_limit_bytes=62 * 2**20
        ),
        cost_estimate=pl.CostEstimate(
            flops=4 * PACK * D * FF, bytes_accessed=12 * 2**20, transcendentals=PACK * FF
        ),
        name="pooled_loss",
    )(
        patches, patch_counts, pack_offsets, norm_gain.reshape(1, D), mlp_in, mlp_out.T,
        probe_query.reshape(1, D), key_weight, value_weight, out_weight, text_embed,
        pair_label.reshape(1, TEXTS), logit_scale, logit_bias,
    )
    return loss.reshape(()), image_grad, text_grad


def solution(mesh):
    placed = (
        P(("grp", "dp"), None), P(("grp", "dp")), P(("grp", "dp")), P(), P("dp", None), P(None, "dp"),
        P(), P(), P(), P(), P(("grp", "dp"), None), P(), P(), P(),
    )
    return jax.shard_map(
        per_device,
        mesh=mesh,
        in_specs=placed,
        out_specs=(P(), P(("grp", "dp"), None), P(("grp", "dp"), None)),
        check_vma=False,
    )
```

```python
import math

import jax
import jax.numpy as jnp
from jax import lax
from jax.experimental import pallas as pl
from jax.experimental.pallas import tpu as pltpu
from jax.sharding import PartitionSpec as P

MESH = pl.DeviceIdType.MESH
F32 = jnp.float32
BF16 = jnp.bfloat16
I32 = jnp.int32

EPSILON = 1e-06
D = 1152
FF = 4304
HEAD_DIM = 72
HEADS = 16
PACK = 1024
TEXTS = 1024
SHARD = 36
SLOT_ROWS = 48
LANES = 128
CHUNKS = 17
HALF = CHUNKS * LANES
BLOCK = 4 * SHARD
GROUP = 4 * BLOCK
TILE = 256

LAG_A, LAG_B, LAG_C, LAG_D, LAG_E = 2, 4, 6, 8, 9

SHARED = 3
GATHERED = CHUNKS - SHARED
TICKS = GATHERED + LAG_E
HANDED_TICKS = (14, 17, 20)
TWO_AT = (15, 18, 21)
TEXT_TICKS = (4, 7, 11, 15, 18, 21)

Z, A_MINUS, A_PLUS, A_FAR, B_MINUS, B_PLUS, B_FAR, SIB, HAND = range(9)

NT = (((1,), (1,)), ((), ()))


def gelu(hidden):
    c1 = math.sqrt(2.0 / math.pi)
    c2 = c1 * 0.044715
    inner = hidden * (c1 + c2 * (hidden * hidden))
    half = 0.5 * hidden
    return (half + half * jnp.tanh(inner)).astype(BF16)


def kernel(
    patches, counts, offsets, gain, win, woutt, probe, key_w, value_w, out_w, text, labels, scale, bias,
    loss_out, igrad_out, tgrad_out,
    xbuf, normed, acc, act, G, own_blocks, a2a_s, a2a_r, compact, T, line_f, tx_s, tx_r, ix_s, ix_r, PI, tcol,
    ps_s, ps_r, ig_s, ig_r, cn_s, cn_r, hk, kw, vw, ow, ilab, tlab, ls_s, ls_r,
    loc_sem, g_ss, g_rs, x_ss, x_rs, tx_ss, tx_rs, ty_ss, ty_rs, tz_ss, tz_rs, ts_ss, ts_rs,
    ix_ss, ix_rs, iy_ss, iy_rs, ps_ss, ps_rs, ig_ss, ig_rs, cn_ss, cn_rs,
    l1_ss, l1_rs, l2_ss, l2_rs, l3_ss, l3_rs,
):
    g = lax.axis_index("grp")
    d = lax.axis_index("dp")
    k = lax.rem(g, 2)
    zl = lax.div(g, 2)
    x = lax.rem(d, 4)
    y = lax.rem(lax.div(d, 4), 4)
    zh = lax.div(d, 16)
    z = zh * 4 + zl

    def dev(x_, y_, z_, k_):
        return (lax.rem(z_, 4) * 2 + k_, lax.div(z_, 4) * 16 + y_ * 4 + x_)

    def m4(v):
        return lax.rem(v, 4)

    def m8(v):
        return lax.rem(v, 8)

    sib = dev(x, y, z, 1 - k)
    xs = [dev(m4(x + i), y, z, k) for i in (1, 2, 3)]
    zs = [dev(x, y, m8(z + i), k) for i in range(1, 8)]
    group_dev = [(g, lax.rem(d + 8 * j, 32)) for j in range(4)]

    def rcopy(src, dst, ss, rs, to):
        return pltpu.make_async_remote_copy(
            src_ref=src, dst_ref=dst, send_sem=ss, recv_sem=rs, device_id=to, device_id_type=MESH
        )

    def wait_recv(ref, rs):
        rcopy(ref, ref, loc_sem.at[0], rs, sib).wait_recv()

    def wait_send(ref, ss):
        rcopy(ref, ref, ss, loc_sem.at[0], sib).wait_send()

    barrier = pltpu.get_barrier_semaphore()
    partners = list(xs) + list(zs) + [sib]
    for i in (1, 2, 3):
        for c_ in (0, 1):
            partners.append(dev(x, m4(y + i), z, c_))
    partners.append(dev(x, m4(y + 2), m8(z + 4), k))
    for p in partners:
        pl.semaphore_signal(barrier, inc=1, device_id=p, device_id_type=MESH)

    local = [
        pltpu.make_async_copy(patches, xbuf, loc_sem.at[1]),
        pltpu.make_async_copy(key_w, kw, loc_sem.at[2]),
        pltpu.make_async_copy(value_w, vw, loc_sem.at[3]),
        pltpu.make_async_copy(out_w, ow, loc_sem.at[4]),
    ]
    for cp in local:
        cp.start()

    source = k == zh

    @pl.when(source)
    def _():
        for part in range(4):
            shard = win if part < 2 else woutt
            if part % 2 == 0:
                a2a_s[part, 0:SHARD, :] = shard[:, 0:HALF]
            else:
                a2a_s[part, :, HALF - LANES:HALF] = jnp.zeros((SLOT_ROWS, LANES), BF16)
                a2a_s[part, 0:SHARD, 0:FF - HALF] = shard[:, HALF:FF]

    text_wide = text[...].astype(F32)
    text_inv = lax.rsqrt(jnp.sum(text_wide * text_wide, axis=1, keepdims=True) + EPSILON)
    text_unit = text_wide * text_inv
    tx_s[...] = jnp.zeros((16, D), BF16)
    tx_s[0:4, :] = text_unit.astype(BF16)
    for j in range(4):
        cn_s[j] = jnp.full((8, LANES), counts[j], I32)

    pl.semaphore_wait(barrier, len(partners))

    @pl.when(source)
    def _():
        for i in range(3):
            to_x = m4(x + i + 1)
            rcopy(a2a_s.at[to_x], a2a_r.at[x], x_ss.at[i], x_rs.at[x], xs[i]).start()
        a2a_r[x] = a2a_s[x]

    for i in range(3):
        rcopy(tx_s, tx_r.at[x], tx_ss.at[i], tx_rs.at[x], xs[i]).start()
    tx_r[x] = tx_s[...]
    for j in (1, 2, 3):
        rcopy(cn_s.at[j], cn_r.at[j], cn_ss.at[j], cn_rs.at[j], group_dev[j]).start()
    cn_r[0] = cn_s[0]

    a = jnp.where(k == 0, y, x)
    b = jnp.where(k == 0, x, y)

    def along(axis_is_a, step):
        move_y = jnp.where(k == 0, 1, 0) if axis_is_a else jnp.where(k == 0, 0, 1)
        return dev(m4(x + (1 - move_y) * step), m4(y + move_y * step), z, k)

    a_plus, a_minus = along(True, 1), along(True, 3)
    b_plus, b_minus = along(False, 1), along(False, 3)

    def a_block(c, at):
        return G.at[c, k, b, pl.ds(pl.multiple_of(at * BLOCK, 16), BLOCK), :]

    def b_group(c, at):
        return G.at[c, k, at]

    @pl.when(source)
    def _():
        for i in (1, 2, 3):
            s = m4(x + i)
            wait_recv(a2a_r.at[s], x_rs.at[s])
        for s in range(4):
            compact[s * SHARD:(s + 1) * SHARD, :] = a2a_r[s, 0:SHARD, :].astype(F32)
        for c in range(CHUNKS):
            own_blocks[c] = compact[:, c * LANES:(c + 1) * LANES].astype(BF16)

    edge = jnp.logical_or(zl == 0, zl == 3)
    outward = jnp.where(zl == 3, 1, 7)
    z_to = dev(x, y, m8(z + jnp.where(source, outward, 8 - outward)), k)

    def t_block(zl_, k_, zh_):
        return T.at[zl_, k_, zh_]

    def z_parts(step):
        zz = m8(z + step)
        return m4(zz), lax.div(zz, 4)

    def text_ring(step):
        zl_, zh_ = z_parts(step)
        return T.at[zl_, k, zh_]

    z_plus, z_minus = zs[0], zs[6]
    own_t = pl.ds(pl.multiple_of(y * 16, 16), 16)

    def gather_line(received, wide):
        for s in range(4):
            wide[4 * s:4 * s + 4, :] = received[s, 0:4, :].astype(F32)
        return wide[...].astype(BF16)

    def label_cols(ids):
        rows = ids.shape[0]
        lanes = lax.broadcasted_iota(I32, (rows, TEXTS), 1)
        row = jnp.broadcast_to(labels[...].astype(F32), (rows, TEXTS))
        return jnp.sum(jnp.where(lanes == ids, row, 0.0), axis=1, keepdims=True)

    parity = lax.rem(zl, 2)
    hand_to = tuple(jnp.where(k == 0, p, m) for p, m in zip(z_plus, z_minus))

    def gathered(i):
        return jnp.where(i < SHARED, 2 * i + parity, i + SHARED)

    def part(c, p):
        pieces = [G[c, 0, p]]
        for yy in range(4):
            pieces.append(G[c, 1, yy, p * BLOCK:(p + 1) * BLOCK, :])
        return jnp.concatenate(pieces, axis=0)

    def w1_of(c):
        return jnp.concatenate([part(c, 0), part(c, 1)], axis=1)

    def w2_of(c):
        return jnp.concatenate([part(c, 2), part(c, 3)], axis=1)

    def tick(t, carry):
        for q in range(2):

            @pl.when(2 * t + q < CHUNKS)
            def _():
                c = 2 * t + q
                own = own_blocks.at[c]

                @pl.when(jnp.logical_not(source))
                def _():
                    wait_recv(own, g_rs.at[Z, c])

                @pl.when(edge)
                def _():
                    rcopy(own, own, g_ss.at[Z, c], g_rs.at[Z, c], z_to).start()

        @pl.when(t < GATHERED)
        def _():
            c = gathered(t)
            own = own_blocks.at[c]
            there = a_block(c, a)
            rcopy(own, there, g_ss.at[A_MINUS, c], g_rs.at[A_MINUS, c], a_plus).start()
            rcopy(own, there, g_ss.at[A_PLUS, c], g_rs.at[A_PLUS, c], a_minus).start()
            there[...] = own[...]

        @pl.when(jnp.logical_and(t >= LAG_A, t < GATHERED + LAG_A))
        def _():
            even = lax.rem(t - LAG_A, 2) == 0
            c = gathered(t - LAG_A)
            blk = a_block(c, m4(a + jnp.where(even, 3, 1)))
            wait_recv(blk, g_rs.at[jnp.where(even, A_MINUS, A_PLUS), c])
            to = tuple(jnp.where(even, p, m) for p, m in zip(a_plus, a_minus))
            rcopy(blk, blk, g_ss.at[A_FAR, c], g_rs.at[A_FAR, c], to).start()

        @pl.when(jnp.logical_and(t >= LAG_C, t < GATHERED + LAG_C))
        def _():
            even = lax.rem(t - LAG_C, 2) == 0
            c = gathered(t - LAG_C)
            grp = b_group(c, m4(b + jnp.where(even, 3, 1)))
            wait_recv(grp, g_rs.at[jnp.where(even, B_MINUS, B_PLUS), c])
            to = tuple(jnp.where(even, p, m) for p, m in zip(b_plus, b_minus))
            rcopy(grp, grp, g_ss.at[B_FAR, c], g_rs.at[B_FAR, c], to).start()

        @pl.when(jnp.logical_and(t >= LAG_B, t < GATHERED + LAG_B))
        def _():
            even = lax.rem(t - LAG_B, 2) == 0
            c = gathered(t - LAG_B)
            wait_recv(a_block(c, m4(a + jnp.where(even, 1, 3))), g_rs.at[jnp.where(even, A_PLUS, A_MINUS), c])
            wait_recv(a_block(c, m4(a + 2)), g_rs.at[A_FAR, c])
            grp = b_group(c, b)
            rcopy(grp, grp, g_ss.at[B_MINUS, c], g_rs.at[B_MINUS, c], b_plus).start()
            rcopy(grp, grp, g_ss.at[B_PLUS, c], g_rs.at[B_PLUS, c], b_minus).start()

        @pl.when(jnp.logical_and(t >= LAG_D, t < GATHERED + LAG_D))
        def _():
            even = lax.rem(t - LAG_D, 2) == 0
            i = t - LAG_D
            c = gathered(i)
            wait_recv(b_group(c, m4(b + jnp.where(even, 1, 3))), g_rs.at[jnp.where(even, B_PLUS, B_MINUS), c])
            wait_recv(b_group(c, m4(b + 2)), g_rs.at[B_FAR, c])
            half = G.at[c, k]
            rcopy(half, half, g_ss.at[SIB, c], g_rs.at[SIB, c], sib).start()

            @pl.when(i < SHARED)
            def _():
                rcopy(half, half, g_ss.at[HAND, c], g_rs.at[HAND, c], hand_to).start()

        for j, at in enumerate(HANDED_TICKS):

            @pl.when(t == at)
            def _():
                c = 2 * j + 1 - parity
                half = G.at[c, k]
                wait_recv(half, g_rs.at[HAND, c])
                rcopy(half, half, g_ss.at[SIB, c], g_rs.at[SIB, c], sib).start()

        @pl.when(t == TEXT_TICKS[0])
        def _():
            for i in (1, 2, 3):
                s = m4(x + i)
                wait_recv(tx_r.at[s], tx_rs.at[s])
            T[zl, k, zh, own_t, :] = gather_line(tx_r, line_f)
            blk = T.at[zl, k, zh, own_t, :]
            for i in (1, 2, 3):
                rcopy(blk, blk, ty_ss.at[i - 1], ty_rs.at[y], dev(x, m4(y + i), z, k)).start()

        @pl.when(t == TEXT_TICKS[1])
        def _():
            for i in (1, 2, 3):
                yy = m4(y + i)
                wait_recv(T.at[zl, k, zh, pl.ds(pl.multiple_of(yy * 16, 16), 16), :], ty_rs.at[yy])
            blk = text_ring(0)
            rcopy(blk, blk, tz_ss.at[0, 0], tz_rs.at[0, 0], z_plus).start()
            rcopy(blk, blk, tz_ss.at[1, 0], tz_rs.at[1, 0], z_minus).start()

        for hop in (1, 2):

            @pl.when(t == TEXT_TICKS[1 + hop])
            def _():
                low, high = text_ring(8 - hop), text_ring(hop)
                wait_recv(low, tz_rs.at[0, hop - 1])
                wait_recv(high, tz_rs.at[1, hop - 1])
                rcopy(low, low, tz_ss.at[0, hop], tz_rs.at[0, hop], z_plus).start()
                rcopy(high, high, tz_ss.at[1, hop], tz_rs.at[1, hop], z_minus).start()

        @pl.when(t == TEXT_TICKS[4])
        def _():
            low, high = text_ring(5), text_ring(3)
            wait_recv(low, tz_rs.at[0, 2])
            wait_recv(high, tz_rs.at[1, 2])

            @pl.when(k == 0)
            def _():
                rcopy(low, low, tz_ss.at[0, 3], tz_rs.at[0, 3], z_plus).start()

            @pl.when(k == 1)
            def _():
                rcopy(high, high, tz_ss.at[0, 3], tz_rs.at[0, 3], z_minus).start()

        @pl.when(t == TEXT_TICKS[5])
        def _():
            wait_recv(text_ring(4), tz_rs.at[0, 3])
            mine = T.at[:, k]
            rcopy(mine, mine, ts_ss.at[0], ts_rs.at[0], sib).start()

        @pl.when(t == 0)
        def _():
            local[0].wait()

        @pl.when(t < PACK // TILE)
        def _():
            sl = pl.ds(pl.multiple_of(t * TILE, TILE), TILE)
            wide = xbuf[sl, :].astype(F32)
            center = jnp.mean(wide, axis=1, keepdims=True)
            off = wide - center
            spread = jnp.mean(off * off, axis=1, keepdims=True)
            normed[sl, :] = (off * lax.rsqrt(spread + EPSILON) * gain[...]).astype(BF16)
            acc[sl, :] = wide
            act[sl, :] = jnp.zeros((TILE, 2 * LANES), BF16)

        @pl.when(t == 4)
        def _():
            local[1].wait()
            head_of = lax.div(lax.broadcasted_iota(I32, (HEADS, D), 1), HEAD_DIM)
            own_head = head_of == lax.broadcasted_iota(I32, (HEADS, D), 0)
            block = jnp.where(own_head, jnp.broadcast_to(probe[...].astype(F32), (HEADS, D)), 0.0)
            keys = lax.dot_general(block.astype(BF16), kw[...], NT, preferred_element_type=F32)
            hk[...] = (keys / math.sqrt(HEAD_DIM)).astype(BF16)

            pos = lax.broadcasted_iota(I32, (LANES, 1), 0)
            slot = lax.rem(pos, 4)
            px = lax.rem(lax.div(pos, 4), 4)
            py = lax.rem(lax.div(pos, 16), 4)
            pk = lax.div(pos, 64)
            owner = lax.rem(16 * zh + 4 * py + px + 32 - 8 * slot, 32)
            ids = 4 * ((2 * zl + pk) * 32 + owner) + slot
            hot = lax.broadcasted_iota(I32, (LANES, TEXTS), 1) == ids
            hot = jnp.where(hot, 1.0, 0.0).astype(BF16)
            lab = labels[...]
            high = lax.div(lab, 16)
            low = lab - 16 * high
            pair = jnp.where(
                lax.broadcasted_iota(I32, (16, TEXTS), 0) == 0,
                jnp.broadcast_to(high, (16, TEXTS)),
                jnp.broadcast_to(low, (16, TEXTS)),
            ).astype(F32).astype(BF16)
            rows = lax.dot_general(pair, hot, NT, preferred_element_type=F32)
            ilab[...] = jnp.broadcast_to(16.0 * rows[0:1, :] + rows[1:2, :], (8, LANES))
            tpos = lax.broadcasted_iota(I32, (64, 1), 0)
            tz = lax.div(tpos, 8)
            tid = m4(tz) * 256 + k * 128 + lax.div(tz, 4) * 64 + y * 16 + x * 4 + m4(tpos)
            tlab[...] = jnp.broadcast_to(label_cols(tid), (64, LANES))

        def chunk_at(u):
            at = [tick_ - LAG_E + j + 1 for j, tick_ in enumerate(TWO_AT)]
            later = [jnp.where(u > v, 1, 0) for v in at]
            c = gathered(u - sum(later))
            for j, v in enumerate(at):
                c = jnp.where(u == v, 2 * j + 1 - parity, c)
            return c

        @pl.when(jnp.logical_and(t >= LAG_E, t < GATHERED + LAG_E))
        def _():
            first = t - LAG_E + sum(jnp.where(t > v, 1, 0) for v in TWO_AT)
            many = 1 + sum(jnp.where(t == v, 1, 0) for v in TWO_AT)

            def one(n, carry):
                u = first + n
                c = chunk_at(u)
                before = chunk_at(jnp.maximum(u - 1, 0))
                wait_recv(G.at[c, 1 - k], g_rs.at[SIB, c])
                w1, w2 = w1_of(c), w2_of(before)
                for r in range(PACK // TILE):
                    sl = slice(r * TILE, (r + 1) * TILE)
                    old = act[sl, :]
                    hidden = jnp.dot(normed[sl, :], w1, preferred_element_type=F32)
                    acc[sl, :] += lax.dot_general(old, w2, NT, preferred_element_type=F32)
                    act[sl, :] = gelu(hidden)
                return carry

            lax.fori_loop(0, many, one, 0)

        return carry

    lax.fori_loop(0, TICKS, tick, 0)

    states = normed
    w2 = w2_of(CHUNKS - 1)
    score_tiles = []
    for r in range(PACK // TILE):
        sl = slice(r * TILE, (r + 1) * TILE)
        mixed = lax.dot_general(act[sl, :], w2, NT, preferred_element_type=F32)
        low = (acc[sl, :] + mixed).astype(BF16)
        states[sl, :] = low
        score_tiles.append(lax.dot_general(hk[...], low, NT, preferred_element_type=F32))
    scores = jnp.concatenate(score_tiles, axis=1)
    row = lax.broadcasted_iota(I32, (HEADS, PACK), 1)
    all_weights = []
    for j in range(4):
        if j > 0:
            wait_recv(cn_r.at[j], cn_rs.at[j])
        first = offsets[j]
        count = cn_r[j][0:1, 0:1]
        member = jnp.logical_and(row >= first, row < first + count)
        masked = jnp.where(member, scores, -1e30)
        highest = jnp.max(masked, axis=1, keepdims=True)
        raised = jnp.exp(masked - highest)
        all_weights.append(raised / jnp.sum(raised, axis=1, keepdims=True))
    weights = jnp.concatenate(all_weights, axis=0).astype(BF16)
    mean_states = jnp.dot(weights, states[...], preferred_element_type=F32).astype(BF16)
    local[2].wait()
    local[3].wait()
    full = jnp.dot(mean_states, vw[...], preferred_element_type=F32)
    head_of = lax.div(lax.broadcasted_iota(I32, (HEADS, D), 1), HEAD_DIM)
    own_head = head_of == lax.broadcasted_iota(I32, (HEADS, D), 0)
    values = [
        jnp.sum(jnp.where(own_head, full[HEADS * j:HEADS * (j + 1), :], 0.0), axis=0, keepdims=True)
        for j in range(4)
    ]
    mixed = jnp.concatenate(values + [jnp.zeros((12, D), F32)], axis=0).astype(BF16)
    pooled = jnp.dot(mixed, ow[...], preferred_element_type=F32)[0:8, :]
    image_inv = lax.rsqrt(jnp.sum(pooled * pooled, axis=1, keepdims=True) + EPSILON)
    image_unit = pooled * image_inv
    ix_s[...] = jnp.concatenate([image_unit, jnp.zeros((8, D), F32)], axis=0).astype(BF16)

    for i in range(3):
        rcopy(ix_s, ix_r.at[x], ix_ss.at[i], ix_rs.at[x], xs[i]).start()
    ix_r[x] = ix_s[...]

    mult = scale[0]
    shift = bias[0]

    wait_recv(T.at[:, 1 - k], ts_rs.at[0])
    texts = T[...].reshape(TEXTS, D)
    own_logits = mult * lax.dot_general(ix_s[...], texts, NT, preferred_element_type=F32) + shift
    slot = lax.broadcasted_iota(I32, (16, 1), 0)
    slot4 = m4(slot)
    own_ids = 4 * (g * 32 + lax.rem(d + 32 - 8 * slot4, 32)) + slot4
    own_lab = label_cols(own_ids)
    sign = jnp.where(own_lab == labels[...].astype(F32), 1.0, -1.0)
    signed = sign * own_logits
    terms = jnp.log1p(jnp.exp(-jnp.abs(signed))) + jnp.maximum(-signed, 0.0)
    terms = jnp.where(slot < 4, terms, 0.0)
    part_loss = jnp.sum(jnp.sum(terms, axis=1, keepdims=True), axis=0, keepdims=True)
    ls_s[0] = jnp.broadcast_to(part_loss, (8, LANES))
    for i in range(3):
        rcopy(ls_s.at[0], ls_r.at[0, x], l1_ss.at[i], l1_rs.at[x], xs[i]).start()
    ls_r[0, x] = ls_s[0]

    for i in (1, 2, 3):
        s = m4(x + i)
        wait_recv(ix_r.at[s], ix_rs.at[s])
    PI[k, own_t, :] = gather_line(ix_r, line_f)
    others = [(m4(y + i), c_) for i in (1, 2, 3) for c_ in (0, 1)]
    to_plane = [dev(x, yy, z, c_) for yy, c_ in others] + [sib]
    blk = PI.at[k, own_t, :]
    for i, to in enumerate(to_plane):
        rcopy(blk, blk, iy_ss.at[i], iy_rs.at[k, y], to).start()

    for i in (1, 2, 3):
        s = m4(x + i)
        wait_recv(ls_r.at[0, s], l1_rs.at[s])
    ls_s[1] = ls_r[0, 0] + ls_r[0, 1] + ls_r[0, 2] + ls_r[0, 3]
    me8 = k * 4 + y
    for i, to in enumerate(to_plane):
        rcopy(ls_s.at[1], ls_r.at[1, me8], l2_ss.at[i], l2_rs.at[me8], to).start()
    ls_r[1, me8] = ls_s[1]

    own_slope = (mult * -sign * jax.nn.sigmoid(-signed)).astype(BF16)
    image_push = jnp.dot(own_slope, texts, preferred_element_type=F32)[0:8, :]
    image_grad = (
        image_push - image_unit * jnp.sum(image_unit * image_push, axis=1, keepdims=True)
    ) * image_inv
    for j in range(4):
        ig_s[j] = image_grad[j:j + 1, :]
    for j in (1, 2, 3):
        rcopy(ig_s.at[j], ig_r.at[j], ig_ss.at[j], ig_rs.at[j], group_dev[4 - j]).start()
    ig_r[0] = ig_s[0]

    for zz in range(8):
        block = T[zz % 4, k, zz // 4, own_t, :].astype(F32)
        mine = jnp.zeros((4, D), F32)
        for s in range(4):
            mine = mine + jnp.where(x == s, 1.0, 0.0) * block[4 * s:4 * s + 4, :]
        tcol[8 * zz:8 * zz + 4, :] = mine
        tcol[8 * zz + 4:8 * zz + 8, :] = jnp.zeros((4, D), F32)

    for yy, c_ in others + [(y, 1 - k)]:
        wait_recv(PI.at[c_, pl.ds(pl.multiple_of(yy * 16, 16), 16), :], iy_rs.at[c_, yy])
    plane = PI[...].reshape(LANES, D)
    plane_logits = mult * lax.dot_general(
        tcol[...].astype(BF16), plane, NT, preferred_element_type=F32
    ) + shift
    plane_sign = jnp.where(tlab[...] == ilab[0:1, :], 1.0, -1.0)
    plane_slope = (mult * -plane_sign * jax.nn.sigmoid(-plane_sign * plane_logits)).astype(BF16)
    push = jnp.dot(plane_slope, plane, preferred_element_type=F32)
    for zz in range(8):
        ps_s[zz] = push[8 * zz:8 * zz + 8, :]
    for i in range(7):
        to_z = m8(z + i + 1)
        rcopy(ps_s.at[to_z], ps_r.at[z], ps_ss.at[i], ps_rs.at[z], zs[i]).start()
    ps_r[z] = ps_s[z]

    for yy, c_ in others + [(y, 1 - k)]:
        wait_recv(ls_r.at[1, c_ * 4 + yy], l2_rs.at[c_ * 4 + yy])
    total = ls_r[1, 0]
    for i in range(1, 8):
        total = total + ls_r[1, i]
    ls_s[2] = total
    for i in range(7):
        rcopy(ls_s.at[2], ls_r.at[2, z], l3_ss.at[i], l3_rs.at[z], zs[i]).start()
    ls_r[2, z] = ls_s[2]

    for j in (1, 2, 3):
        wait_recv(ig_r.at[j], ig_rs.at[j])
    for j in range(4):
        igrad_out[j:j + 1, :] = ig_r[j]

    for i in range(1, 8):
        zz = m8(z + i)
        wait_recv(ps_r.at[zz], ps_rs.at[zz])
    text_push = ps_r[0]
    for i in range(1, 8):
        text_push = text_push + ps_r[i]
    text_push = text_push[0:4, :]
    tgrad_out[...] = (
        text_push - text_unit * jnp.sum(text_unit * text_push, axis=1, keepdims=True)
    ) * text_inv

    for i in range(1, 8):
        zz = m8(z + i)
        wait_recv(ls_r.at[2, zz], l3_rs.at[zz])
    total = ls_r[2, 0]
    for i in range(1, 8):
        total = total + ls_r[2, i]
    loss_out[...] = total[0:1, 0:1] / float(TEXTS)

    def drain(c, carry):
        own = own_blocks.at[c]

        @pl.when(edge)
        def _():
            wait_send(own, g_ss.at[Z, c])

        wait_send(G.at[c, k], g_ss.at[SIB, c])

        @pl.when(c < GATHERED)
        def _():
            e = gathered(c)
            for kind in (A_MINUS, A_PLUS, A_FAR):
                wait_send(own, g_ss.at[kind, e])
            for kind in (B_MINUS, B_PLUS, B_FAR):
                wait_send(b_group(e, b), g_ss.at[kind, e])

            @pl.when(c < SHARED)
            def _():
                wait_send(G.at[e, k], g_ss.at[HAND, e])

        return carry

    lax.fori_loop(0, CHUNKS, drain, 0)

    @pl.when(source)
    def _():
        for i in range(3):
            wait_send(a2a_s.at[0], x_ss.at[i])

    for i in range(3):
        wait_send(tx_s, tx_ss.at[i])
        wait_send(T.at[zl, k, zh, own_t, :], ty_ss.at[i])
        wait_send(ix_s, ix_ss.at[i])
        wait_send(ls_s.at[0], l1_ss.at[i])
        wait_send(cn_s.at[i + 1], cn_ss.at[i + 1])
        wait_send(ig_s.at[i + 1], ig_ss.at[i + 1])
        wait_send(text_ring(0), tz_ss.at[0, i])
        wait_send(text_ring(0), tz_ss.at[1, i])
    wait_send(text_ring(0), tz_ss.at[0, 3])
    wait_send(T.at[:, k], ts_ss.at[0])
    for i in range(7):
        wait_send(PI.at[k, own_t, :], iy_ss.at[i])
        wait_send(ls_s.at[1], l2_ss.at[i])
        wait_send(ps_s.at[0], ps_ss.at[i])
        wait_send(ls_s.at[2], l3_ss.at[i])


def per_device(
    patches, patch_counts, pack_offsets, norm_gain, mlp_in, mlp_out, probe_query, key_weight,
    value_weight, out_weight, text_embed, pair_label, logit_scale, logit_bias,
):
    vmem = pl.BlockSpec(memory_space=pltpu.VMEM)
    smem = pl.BlockSpec(memory_space=pltpu.SMEM)
    anywhere = pl.BlockSpec(memory_space=pl.ANY)
    dma = pltpu.SemaphoreType.DMA
    loss, image_grad, text_grad = pl.pallas_call(
        kernel,
        out_shape=(
            jax.ShapeDtypeStruct((1, 1), F32),
            jax.ShapeDtypeStruct((4, D), F32),
            jax.ShapeDtypeStruct((4, D), F32),
        ),
        in_specs=[
            anywhere, smem, smem, vmem, vmem, vmem, vmem, anywhere, anywhere, anywhere, vmem, vmem, smem, smem,
        ],
        out_specs=(vmem, vmem, vmem),
        scratch_shapes=[
            pltpu.VMEM((PACK, D), BF16),
            pltpu.VMEM((PACK, D), BF16),
            pltpu.VMEM((PACK, D), F32),
            pltpu.VMEM((PACK, 2 * LANES), BF16),
            pltpu.VMEM((CHUNKS, 2, 4, GROUP, LANES), BF16),
            pltpu.VMEM((CHUNKS, BLOCK, LANES), BF16),
            pltpu.VMEM((4, SLOT_ROWS, HALF), BF16),
            pltpu.VMEM((4, SLOT_ROWS, HALF), BF16),
            pltpu.VMEM((BLOCK, HALF), F32),
            pltpu.VMEM((4, 2, 2, 64, D), BF16),
            pltpu.VMEM((16, D), F32),
            pltpu.VMEM((16, D), BF16),
            pltpu.VMEM((4, 16, D), BF16),
            pltpu.VMEM((16, D), BF16),
            pltpu.VMEM((4, 16, D), BF16),
            pltpu.VMEM((2, 64, D), BF16),
            pltpu.VMEM((64, D), F32),
            pltpu.VMEM((8, 8, D), F32),
            pltpu.VMEM((8, 8, D), F32),
            pltpu.VMEM((4, 1, D), F32),
            pltpu.VMEM((4, 1, D), F32),
            pltpu.VMEM((4, 8, LANES), I32),
            pltpu.VMEM((4, 8, LANES), I32),
            pltpu.VMEM((HEADS, D), BF16),
            pltpu.VMEM((D, D), BF16),
            pltpu.VMEM((D, D), BF16),
            pltpu.VMEM((D, D), BF16),
            pltpu.VMEM((8, LANES), F32),
            pltpu.VMEM((64, LANES), F32),
            pltpu.VMEM((3, 8, LANES), F32),
            pltpu.VMEM((3, 8, 8, LANES), F32),
            dma((5,)),
            dma((9, CHUNKS)), dma((9, CHUNKS)),
            dma((3,)), dma((4,)),
            dma((3,)), dma((4,)),
            dma((3,)), dma((4,)),
            dma((2, 4)), dma((2, 4)),
            dma((1,)), dma((1,)),
            dma((3,)), dma((4,)),
            dma((7,)), dma((2, 4)),
            dma((7,)), dma((8,)),
            dma((4,)), dma((4,)),
            dma((4,)), dma((4,)),
            dma((3,)), dma((4,)),
            dma((7,)), dma((8,)),
            dma((7,)), dma((8,)),
        ],
        compiler_params=pltpu.CompilerParams(
            collective_id=0, has_side_effects=True, vmem_limit_bytes=62 * 2**20
        ),
        cost_estimate=pl.CostEstimate(
            flops=4 * PACK * D * FF, bytes_accessed=12 * 2**20, transcendentals=PACK * FF
        ),
        name="pooled_loss",
    )(
        patches, patch_counts, pack_offsets, norm_gain.reshape(1, D), mlp_in, mlp_out.T,
        probe_query.reshape(1, D), key_weight, value_weight, out_weight, text_embed,
        pair_label.reshape(1, TEXTS), logit_scale, logit_bias,
    )
    return loss.reshape(()), image_grad, text_grad


def solution(mesh):
    placed = (
        P(("grp", "dp"), None), P(("grp", "dp")), P(("grp", "dp")), P(), P("dp", None), P(None, "dp"),
        P(), P(), P(), P(), P(("grp", "dp"), None), P(), P(), P(),
    )
    return jax.shard_map(
        per_device,
        mesh=mesh,
        in_specs=placed,
        out_specs=(P(), P(("grp", "dp"), None), P(("grp", "dp"), None)),
        check_vma=False,
    )
```

```python
import math

import jax
import jax.numpy as jnp
from jax import lax
from jax.experimental import pallas as pl
from jax.experimental.pallas import tpu as pltpu
from jax.sharding import PartitionSpec as P

MESH = pl.DeviceIdType.MESH
F32 = jnp.float32
BF16 = jnp.bfloat16
I32 = jnp.int32

EPSILON = 1e-06
D = 1152
FF = 4304
HEAD_DIM = 72
HEADS = 16
PACK = 1024
TEXTS = 1024
SHARD = 36
SLOT_ROWS = 48
LANES = 128
CHUNKS = 17
HALF = CHUNKS * LANES
BLOCK = 4 * SHARD
GROUP = 4 * BLOCK
TILE = 256

LAG_A, LAG_B, LAG_C, LAG_D, LAG_E = 2, 4, 6, 8, 9

SHARED = 3
GATHERED = CHUNKS - SHARED
TICKS = GATHERED + LAG_E
HANDED_TICKS = (14, 17, 20)
TWO_AT = (15, 18, 21)
TEXT_TICKS = (3, 6, 9, 12, 15, 18)
PIECES = ((0, 4), (4, 10), (10, 17))
PIECE_TICKS = (1, 4)

Z, A_MINUS, A_PLUS, A_FAR, B_MINUS, B_PLUS, B_FAR, SIB, HAND = range(9)

NT = (((1,), (1,)), ((), ()))


def gelu(hidden):
    c1 = math.sqrt(2.0 / math.pi)
    c2 = c1 * 0.044715
    inner = hidden * (c1 + c2 * (hidden * hidden))
    half = 0.5 * hidden
    return (half + half * jnp.tanh(inner)).astype(BF16)


def kernel(
    patches, counts, offsets, gain, win_hbm, woutt_hbm, probe, key_w, value_w, out_w, text, labels, scale, bias,
    loss_out, igrad_out, tgrad_out,
    xbuf, normed, acc, act, G, own_blocks, win, woutt, a2a_s, a2a_r, compact, T, line_f, tx_s, tx_r, ix_s, ix_r, line_i, PI, tcol,
    ps_s, ps_r, ig_s, ig_r, cn_s, cn_r, hk, kw, vw, ow, ilab, tlab, ls_s, ls_r,
    loc_sem, g_ss, g_rs, x_ss, x_rs, tx_ss, tx_rs, ty_ss, ty_rs, tz_ss, tz_rs, ts_ss, ts_rs,
    ix_ss, ix_rs, iy_ss, iy_rs, ps_ss, ps_rs, ig_ss, ig_rs, cn_ss, cn_rs,
    l1_ss, l1_rs, l2_ss, l2_rs, l3_ss, l3_rs,
):
    g = lax.axis_index("grp")
    d = lax.axis_index("dp")
    k = lax.rem(g, 2)
    zl = lax.div(g, 2)
    x = lax.rem(d, 4)
    y = lax.rem(lax.div(d, 4), 4)
    zh = lax.div(d, 16)
    z = zh * 4 + zl

    def dev(x_, y_, z_, k_):
        return (lax.rem(z_, 4) * 2 + k_, lax.div(z_, 4) * 16 + y_ * 4 + x_)

    def m4(v):
        return lax.rem(v, 4)

    def m8(v):
        return lax.rem(v, 8)

    sib = dev(x, y, z, 1 - k)
    xs = [dev(m4(x + i), y, z, k) for i in (1, 2, 3)]
    zs = [dev(x, y, m8(z + i), k) for i in range(1, 8)]
    group_dev = [(g, lax.rem(d + 8 * j, 32)) for j in range(4)]

    def rcopy(src, dst, ss, rs, to):
        return pltpu.make_async_remote_copy(
            src_ref=src, dst_ref=dst, send_sem=ss, recv_sem=rs, device_id=to, device_id_type=MESH
        )

    def wait_recv(ref, rs):
        rcopy(ref, ref, loc_sem.at[0], rs, sib).wait_recv()

    def wait_send(ref, ss):
        rcopy(ref, ref, ss, loc_sem.at[0], sib).wait_send()

    shards = [
        pltpu.make_async_copy(win_hbm, win, loc_sem.at[5]),
        pltpu.make_async_copy(woutt_hbm, woutt, loc_sem.at[6]),
    ]
    for cp in shards:
        cp.start()
    local = [
        pltpu.make_async_copy(patches, xbuf, loc_sem.at[1]),
        pltpu.make_async_copy(key_w, kw, loc_sem.at[2]),
        pltpu.make_async_copy(value_w, vw, loc_sem.at[3]),
        pltpu.make_async_copy(out_w, ow, loc_sem.at[4]),
    ]

    barrier = pltpu.get_barrier_semaphore()
    partners = list(xs) + list(zs) + [sib]
    for i in (1, 2, 3):
        for c_ in (0, 1):
            partners.append(dev(x, m4(y + i), z, c_))
    partners.append(dev(x, m4(y + 2), m8(z + 4), k))
    for p in partners:
        pl.semaphore_signal(barrier, inc=1, device_id=p, device_id_type=MESH)

    for cp in shards:
        cp.wait()
    local[0].start()

    source = k == zh

    @pl.when(source)
    def _():
        for part in range(4):
            shard = win if part < 2 else woutt
            if part % 2 == 0:
                a2a_s[part, 0:SHARD, :] = shard[:, 0:HALF]
            else:
                a2a_s[part, :, HALF - LANES:HALF] = jnp.zeros((SLOT_ROWS, LANES), BF16)
                a2a_s[part, 0:SHARD, 0:FF - HALF] = shard[:, HALF:FF]

    text_wide = text[...].astype(F32)
    text_inv = lax.rsqrt(jnp.sum(text_wide * text_wide, axis=1, keepdims=True) + EPSILON)
    text_unit = text_wide * text_inv
    tx_s[...] = jnp.zeros((16, D), BF16)
    tx_s[0:4, :] = text_unit.astype(BF16)
    for j in range(4):
        cn_s[j] = jnp.full((8, LANES), counts[j], I32)

    pl.semaphore_wait(barrier, len(partners))

    def piece_lanes(p):
        return slice(PIECES[p][0] * LANES, PIECES[p][1] * LANES)

    @pl.when(source)
    def _():
        for p in range(len(PIECES)):
            at = piece_lanes(p)
            for i in range(3):
                to_x = m4(x + i + 1)
                rcopy(
                    a2a_s.at[to_x, :, at], a2a_r.at[x, :, at], x_ss.at[p, i], x_rs.at[p, x], xs[i]
                ).start()
        a2a_r[x] = a2a_s[x]

    for i in range(3):
        rcopy(tx_s, tx_r.at[x], tx_ss.at[i], tx_rs.at[x], xs[i]).start()
    tx_r[x] = tx_s[...]
    for j in (1, 2, 3):
        rcopy(cn_s.at[j], cn_r.at[j], cn_ss.at[j], cn_rs.at[j], group_dev[j]).start()
    cn_r[0] = cn_s[0]

    a = jnp.where(k == 0, y, x)
    b = jnp.where(k == 0, x, y)

    def along(axis_is_a, step):
        move_y = jnp.where(k == 0, 1, 0) if axis_is_a else jnp.where(k == 0, 0, 1)
        return dev(m4(x + (1 - move_y) * step), m4(y + move_y * step), z, k)

    a_plus, a_minus = along(True, 1), along(True, 3)
    b_plus, b_minus = along(False, 1), along(False, 3)

    def a_block(c, at):
        return G.at[c, k, b, pl.ds(pl.multiple_of(at * BLOCK, 16), BLOCK), :]

    def b_group(c, at):
        return G.at[c, k, at]

    def take_piece(p):
        at = piece_lanes(p)
        for i in (1, 2, 3):
            s = m4(x + i)
            wait_recv(a2a_r.at[s, :, at], x_rs.at[p, s])
        for s in range(4):
            compact[s * SHARD:(s + 1) * SHARD, at] = a2a_r[s, 0:SHARD, at].astype(F32)
        for c in range(*PIECES[p]):
            own_blocks[c] = compact[:, c * LANES:(c + 1) * LANES].astype(BF16)

    @pl.when(source)
    def _():
        take_piece(0)

    edge = jnp.logical_or(zl == 0, zl == 3)
    outward = jnp.where(zl == 3, 1, 7)
    z_to = dev(x, y, m8(z + jnp.where(source, outward, 8 - outward)), k)

    def t_block(zl_, k_, zh_):
        return T.at[zl_, k_, zh_]

    def z_parts(step):
        zz = m8(z + step)
        return m4(zz), lax.div(zz, 4)

    def text_ring(step):
        zl_, zh_ = z_parts(step)
        return T.at[zl_, k, zh_]

    z_plus, z_minus = zs[0], zs[6]
    own_t = pl.ds(pl.multiple_of(y * 16, 16), 16)

    def gather_line(received, wide):
        for s in range(4):
            wide[4 * s:4 * s + 4, :] = received[s, 0:4, :].astype(F32)
        return wide[...].astype(BF16)

    def label_cols(ids):
        rows = ids.shape[0]
        lanes = lax.broadcasted_iota(I32, (rows, TEXTS), 1)
        row = jnp.broadcast_to(labels[...].astype(F32), (rows, TEXTS))
        return jnp.sum(jnp.where(lanes == ids, row, 0.0), axis=1, keepdims=True)

    parity = lax.rem(zl, 2)
    hand_to = tuple(jnp.where(k == 0, p, m) for p, m in zip(z_plus, z_minus))

    def gathered(i):
        return jnp.where(i < SHARED, 2 * i + parity, i + SHARED)

    def part(c, p):
        pieces = [G[c, 0, p]]
        for yy in range(4):
            pieces.append(G[c, 1, yy, p * BLOCK:(p + 1) * BLOCK, :])
        return jnp.concatenate(pieces, axis=0)

    def w1_of(c):
        return jnp.concatenate([part(c, 0), part(c, 1)], axis=1)

    def w2_of(c):
        return jnp.concatenate([part(c, 2), part(c, 3)], axis=1)

    def tick(t, carry):
        for p, at in enumerate(PIECE_TICKS):

            @pl.when(jnp.logical_and(source, t == at))
            def _():
                take_piece(p + 1)

        for q in range(2):

            @pl.when(2 * t + q < CHUNKS)
            def _():
                c = 2 * t + q
                own = own_blocks.at[c]

                @pl.when(jnp.logical_not(source))
                def _():
                    wait_recv(own, g_rs.at[Z, c])

                @pl.when(edge)
                def _():
                    rcopy(own, own, g_ss.at[Z, c], g_rs.at[Z, c], z_to).start()

        @pl.when(t < GATHERED)
        def _():
            c = gathered(t)
            own = own_blocks.at[c]
            there = a_block(c, a)
            rcopy(own, there, g_ss.at[A_MINUS, c], g_rs.at[A_MINUS, c], a_plus).start()
            rcopy(own, there, g_ss.at[A_PLUS, c], g_rs.at[A_PLUS, c], a_minus).start()
            there[...] = own[...]

        @pl.when(jnp.logical_and(t >= LAG_A, t < GATHERED + LAG_A))
        def _():
            even = lax.rem(t - LAG_A, 2) == 0
            c = gathered(t - LAG_A)
            blk = a_block(c, m4(a + jnp.where(even, 3, 1)))
            wait_recv(blk, g_rs.at[jnp.where(even, A_MINUS, A_PLUS), c])
            to = tuple(jnp.where(even, p, m) for p, m in zip(a_plus, a_minus))
            rcopy(blk, blk, g_ss.at[A_FAR, c], g_rs.at[A_FAR, c], to).start()

        @pl.when(jnp.logical_and(t >= LAG_C, t < GATHERED + LAG_C))
        def _():
            even = lax.rem(t - LAG_C, 2) == 0
            c = gathered(t - LAG_C)
            grp = b_group(c, m4(b + jnp.where(even, 3, 1)))
            wait_recv(grp, g_rs.at[jnp.where(even, B_MINUS, B_PLUS), c])
            to = tuple(jnp.where(even, p, m) for p, m in zip(b_plus, b_minus))
            rcopy(grp, grp, g_ss.at[B_FAR, c], g_rs.at[B_FAR, c], to).start()

        @pl.when(jnp.logical_and(t >= LAG_B, t < GATHERED + LAG_B))
        def _():
            even = lax.rem(t - LAG_B, 2) == 0
            c = gathered(t - LAG_B)
            wait_recv(a_block(c, m4(a + jnp.where(even, 1, 3))), g_rs.at[jnp.where(even, A_PLUS, A_MINUS), c])
            wait_recv(a_block(c, m4(a + 2)), g_rs.at[A_FAR, c])
            grp = b_group(c, b)
            rcopy(grp, grp, g_ss.at[B_MINUS, c], g_rs.at[B_MINUS, c], b_plus).start()
            rcopy(grp, grp, g_ss.at[B_PLUS, c], g_rs.at[B_PLUS, c], b_minus).start()

        @pl.when(jnp.logical_and(t >= LAG_D, t < GATHERED + LAG_D))
        def _():
            even = lax.rem(t - LAG_D, 2) == 0
            i = t - LAG_D
            c = gathered(i)
            wait_recv(b_group(c, m4(b + jnp.where(even, 1, 3))), g_rs.at[jnp.where(even, B_PLUS, B_MINUS), c])
            wait_recv(b_group(c, m4(b + 2)), g_rs.at[B_FAR, c])
            half = G.at[c, k]
            rcopy(half, half, g_ss.at[SIB, c], g_rs.at[SIB, c], sib).start()

            @pl.when(i < SHARED)
            def _():
                rcopy(half, half, g_ss.at[HAND, c], g_rs.at[HAND, c], hand_to).start()

        for j, at in enumerate(HANDED_TICKS):

            @pl.when(t == at)
            def _():
                c = 2 * j + 1 - parity
                half = G.at[c, k]
                wait_recv(half, g_rs.at[HAND, c])
                rcopy(half, half, g_ss.at[SIB, c], g_rs.at[SIB, c], sib).start()

        @pl.when(t == TEXT_TICKS[0])
        def _():
            for i in (1, 2, 3):
                s = m4(x + i)
                wait_recv(tx_r.at[s], tx_rs.at[s])
            T[zl, k, zh, own_t, :] = gather_line(tx_r, line_f)
            blk = T.at[zl, k, zh, own_t, :]
            for i in (1, 2, 3):
                rcopy(blk, blk, ty_ss.at[i - 1], ty_rs.at[y], dev(x, m4(y + i), z, k)).start()

        @pl.when(t == TEXT_TICKS[1])
        def _():
            for i in (1, 2, 3):
                yy = m4(y + i)
                wait_recv(T.at[zl, k, zh, pl.ds(pl.multiple_of(yy * 16, 16), 16), :], ty_rs.at[yy])
            blk = text_ring(0)
            rcopy(blk, blk, tz_ss.at[0, 0], tz_rs.at[0, 0], z_plus).start()
            rcopy(blk, blk, tz_ss.at[1, 0], tz_rs.at[1, 0], z_minus).start()

        for hop in (1, 2):

            @pl.when(t == TEXT_TICKS[1 + hop])
            def _():
                low, high = text_ring(8 - hop), text_ring(hop)
                wait_recv(low, tz_rs.at[0, hop - 1])
                wait_recv(high, tz_rs.at[1, hop - 1])
                rcopy(low, low, tz_ss.at[0, hop], tz_rs.at[0, hop], z_plus).start()
                rcopy(high, high, tz_ss.at[1, hop], tz_rs.at[1, hop], z_minus).start()

        @pl.when(t == TEXT_TICKS[4])
        def _():
            low, high = text_ring(5), text_ring(3)
            wait_recv(low, tz_rs.at[0, 2])
            wait_recv(high, tz_rs.at[1, 2])

            @pl.when(k == 0)
            def _():
                rcopy(low, low, tz_ss.at[0, 3], tz_rs.at[0, 3], z_plus).start()

            @pl.when(k == 1)
            def _():
                rcopy(high, high, tz_ss.at[0, 3], tz_rs.at[0, 3], z_minus).start()

        @pl.when(t == TEXT_TICKS[5])
        def _():
            wait_recv(text_ring(4), tz_rs.at[0, 3])
            mine = T.at[:, k]
            rcopy(mine, mine, ts_ss.at[0], ts_rs.at[0], sib).start()

        @pl.when(t == TEXT_TICKS[5] + 1)
        def _():
            for zz in range(8):
                block = T[zz % 4, k, zz // 4, own_t, :].astype(F32)
                mine = jnp.zeros((4, D), F32)
                for s in range(4):
                    mine = mine + jnp.where(x == s, 1.0, 0.0) * block[4 * s:4 * s + 4, :]
                tcol[8 * zz:8 * zz + 4, :] = mine
                tcol[8 * zz + 4:8 * zz + 8, :] = jnp.zeros((4, D), F32)

        @pl.when(t == 0)
        def _():
            local[1].start()

        @pl.when(t == 1)
        def _():
            local[0].wait()

        @pl.when(t == 8)
        def _():
            local[2].start()
            local[3].start()

        @pl.when(jnp.logical_and(t >= 1, t <= PACK // TILE))
        def _():
            sl = pl.ds(pl.multiple_of((t - 1) * TILE, TILE), TILE)
            wide = xbuf[sl, :].astype(F32)
            center = jnp.mean(wide, axis=1, keepdims=True)
            off = wide - center
            spread = jnp.mean(off * off, axis=1, keepdims=True)
            normed[sl, :] = (off * lax.rsqrt(spread + EPSILON) * gain[...].reshape(1, D)).astype(BF16)
            acc[sl, :] = wide
            act[sl, :] = jnp.zeros((TILE, 2 * LANES), BF16)

        @pl.when(t == 7)
        def _():
            local[1].wait()
            head_of = lax.div(lax.broadcasted_iota(I32, (HEADS, D), 1), HEAD_DIM)
            own_head = head_of == lax.broadcasted_iota(I32, (HEADS, D), 0)
            block = jnp.where(own_head, jnp.broadcast_to(probe[...].astype(F32).reshape(1, D), (HEADS, D)), 0.0)
            keys = lax.dot_general(block.astype(BF16), kw[...], NT, preferred_element_type=F32)
            hk[...] = (keys / math.sqrt(HEAD_DIM)).astype(BF16)

            pos = lax.broadcasted_iota(I32, (LANES, 1), 0)
            slot = lax.rem(pos, 4)
            px = lax.rem(lax.div(pos, 4), 4)
            py = lax.rem(lax.div(pos, 16), 4)
            pk = lax.div(pos, 64)
            owner = lax.rem(16 * zh + 4 * py + px + 32 - 8 * slot, 32)
            ids = 4 * ((2 * zl + pk) * 32 + owner) + slot
            hot = lax.broadcasted_iota(I32, (LANES, TEXTS), 1) == ids
            hot = jnp.where(hot, 1.0, 0.0).astype(BF16)
            lab = labels[...]
            high = lax.div(lab, 16)
            low = lab - 16 * high
            pair = jnp.where(
                lax.broadcasted_iota(I32, (16, TEXTS), 0) == 0,
                jnp.broadcast_to(high, (16, TEXTS)),
                jnp.broadcast_to(low, (16, TEXTS)),
            ).astype(F32).astype(BF16)
            rows = lax.dot_general(pair, hot, NT, preferred_element_type=F32)
            ilab[...] = jnp.broadcast_to(16.0 * rows[0:1, :] + rows[1:2, :], (8, LANES))
            tpos = lax.broadcasted_iota(I32, (64, 1), 0)
            tz = lax.div(tpos, 8)
            tid = m4(tz) * 256 + k * 128 + lax.div(tz, 4) * 64 + y * 16 + x * 4 + m4(tpos)
            tlab[...] = jnp.broadcast_to(label_cols(tid), (64, LANES))

        def chunk_at(u):
            at = [tick_ - LAG_E + j + 1 for j, tick_ in enumerate(TWO_AT)]
            later = [jnp.where(u > v, 1, 0) for v in at]
            c = gathered(u - sum(later))
            for j, v in enumerate(at):
                c = jnp.where(u == v, 2 * j + 1 - parity, c)
            return c

        @pl.when(jnp.logical_and(t >= LAG_E, t < GATHERED + LAG_E))
        def _():
            first = t - LAG_E + sum(jnp.where(t > v, 1, 0) for v in TWO_AT)
            many = 1 + sum(jnp.where(t == v, 1, 0) for v in TWO_AT)

            def one(n, carry):
                u = first + n
                c = chunk_at(u)
                before = chunk_at(jnp.maximum(u - 1, 0))
                wait_recv(G.at[c, 1 - k], g_rs.at[SIB, c])
                w1, w2 = w1_of(c), w2_of(before)
                for r in range(PACK // TILE):
                    sl = slice(r * TILE, (r + 1) * TILE)
                    old = act[sl, :]
                    hidden = jnp.dot(normed[sl, :], w1, preferred_element_type=F32)
                    acc[sl, :] += lax.dot_general(old, w2, NT, preferred_element_type=F32)
                    act[sl, :] = gelu(hidden)
                return carry

            lax.fori_loop(0, many, one, 0)

        return carry

    lax.fori_loop(0, TICKS, tick, 0)

    states = normed
    w2 = w2_of(CHUNKS - 1)
    score_tiles = []
    for r in range(PACK // TILE):
        sl = slice(r * TILE, (r + 1) * TILE)
        mixed = lax.dot_general(act[sl, :], w2, NT, preferred_element_type=F32)
        low = (acc[sl, :] + mixed).astype(BF16)
        states[sl, :] = low
        score_tiles.append(lax.dot_general(hk[...], low, NT, preferred_element_type=F32))
    scores = jnp.concatenate(score_tiles, axis=1)
    row = lax.broadcasted_iota(I32, (HEADS, PACK), 1)
    all_weights = []
    for j in range(4):
        if j > 0:
            wait_recv(cn_r.at[j], cn_rs.at[j])
        first = offsets[j]
        count = cn_r[j][0:1, 0:1]
        member = jnp.logical_and(row >= first, row < first + count)
        masked = jnp.where(member, scores, -1e30)
        highest = jnp.max(masked, axis=1, keepdims=True)
        raised = jnp.exp(masked - highest)
        all_weights.append(raised / jnp.sum(raised, axis=1, keepdims=True))
    weights = jnp.concatenate(all_weights, axis=0).astype(BF16)
    mean_states = jnp.dot(weights, states[...], preferred_element_type=F32).astype(BF16)
    local[2].wait()
    local[3].wait()
    full = jnp.dot(mean_states, vw[...], preferred_element_type=F32)
    head_of = lax.div(lax.broadcasted_iota(I32, (HEADS, D), 1), HEAD_DIM)
    own_head = head_of == lax.broadcasted_iota(I32, (HEADS, D), 0)
    values = [
        jnp.sum(jnp.where(own_head, full[HEADS * j:HEADS * (j + 1), :], 0.0), axis=0, keepdims=True)
        for j in range(4)
    ]
    mixed = jnp.concatenate(values + [jnp.zeros((12, D), F32)], axis=0).astype(BF16)
    pooled = jnp.dot(mixed, ow[...], preferred_element_type=F32)[0:8, :]
    image_inv = lax.rsqrt(jnp.sum(pooled * pooled, axis=1, keepdims=True) + EPSILON)
    image_unit = pooled * image_inv
    image_low = jnp.concatenate([image_unit, jnp.zeros((8, D), F32)], axis=0).astype(BF16)
    ix_s[...] = image_low[0:8].astype(F32)[0:4]

    for i in range(3):
        rcopy(ix_s, ix_r.at[x], ix_ss.at[i], ix_rs.at[x], xs[i]).start()
    ix_r[x] = ix_s[...]

    mult = scale[0]
    shift = bias[0]

    wait_recv(T.at[:, 1 - k], ts_rs.at[0])
    texts = T[...].reshape(TEXTS, D)
    own_logits = mult * lax.dot_general(image_low, texts, NT, preferred_element_type=F32) + shift
    slot = lax.broadcasted_iota(I32, (16, 1), 0)
    slot4 = m4(slot)
    own_ids = 4 * (g * 32 + lax.rem(d + 32 - 8 * slot4, 32)) + slot4
    own_lab = label_cols(own_ids)
    sign = jnp.where(own_lab == labels[...].astype(F32), 1.0, -1.0)
    signed = sign * own_logits
    terms = jnp.log1p(jnp.exp(-jnp.abs(signed))) + jnp.maximum(-signed, 0.0)
    terms = jnp.where(slot < 4, terms, 0.0)
    part_loss = jnp.sum(jnp.sum(terms, axis=1, keepdims=True), axis=0, keepdims=True)
    ls_s[0] = jnp.broadcast_to(part_loss, (8, LANES))
    for i in range(3):
        rcopy(ls_s.at[0], ls_r.at[0, x], l1_ss.at[i], l1_rs.at[x], xs[i]).start()
    ls_r[0, x] = ls_s[0]

    for i in (1, 2, 3):
        s = m4(x + i)
        wait_recv(ix_r.at[s], ix_rs.at[s])
    for s in range(4):
        line_i[4 * s:4 * s + 4, :] = ix_r[s]
    PI[k, own_t, :] = line_i[...].astype(BF16)
    others = [(m4(y + i), c_) for i in (1, 2, 3) for c_ in (0, 1)]
    to_plane = [dev(x, yy, z, c_) for yy, c_ in others] + [sib]
    blk = PI.at[k, own_t, :]
    for i, to in enumerate(to_plane):
        rcopy(blk, blk, iy_ss.at[i], iy_rs.at[k, y], to).start()

    for i in (1, 2, 3):
        s = m4(x + i)
        wait_recv(ls_r.at[0, s], l1_rs.at[s])
    ls_s[1] = ls_r[0, 0] + ls_r[0, 1] + ls_r[0, 2] + ls_r[0, 3]
    me8 = k * 4 + y
    for i, to in enumerate(to_plane):
        rcopy(ls_s.at[1], ls_r.at[1, me8], l2_ss.at[i], l2_rs.at[me8], to).start()
    ls_r[1, me8] = ls_s[1]

    own_slope = (mult * -sign * jax.nn.sigmoid(-signed)).astype(BF16)
    image_push = jnp.dot(own_slope, texts, preferred_element_type=F32)[0:8, :]
    image_grad = (
        image_push - image_unit * jnp.sum(image_unit * image_push, axis=1, keepdims=True)
    ) * image_inv
    for j in range(4):
        ig_s[j] = image_grad[j:j + 1, :]
    for j in (1, 2, 3):
        rcopy(ig_s.at[j], ig_r.at[j], ig_ss.at[j], ig_rs.at[j], group_dev[4 - j]).start()
    ig_r[0] = ig_s[0]

    for yy, c_ in others + [(y, 1 - k)]:
        wait_recv(PI.at[c_, pl.ds(pl.multiple_of(yy * 16, 16), 16), :], iy_rs.at[c_, yy])
    plane = PI[...].reshape(LANES, D)
    plane_logits = mult * lax.dot_general(
        tcol[...].astype(BF16), plane, NT, preferred_element_type=F32
    ) + shift
    plane_sign = jnp.where(tlab[...] == ilab[0:1, :], 1.0, -1.0)
    plane_slope = (mult * -plane_sign * jax.nn.sigmoid(-plane_sign * plane_logits)).astype(BF16)
    push = jnp.dot(plane_slope, plane, preferred_element_type=F32)
    for zz in range(8):
        ps_s[zz] = push[8 * zz:8 * zz + 4, :]
    for i in range(7):
        to_z = m8(z + i + 1)
        rcopy(ps_s.at[to_z], ps_r.at[z], ps_ss.at[i], ps_rs.at[z], zs[i]).start()
    ps_r[z] = ps_s[z]

    for yy, c_ in others + [(y, 1 - k)]:
        wait_recv(ls_r.at[1, c_ * 4 + yy], l2_rs.at[c_ * 4 + yy])
    total = ls_r[1, 0]
    for i in range(1, 8):
        total = total + ls_r[1, i]
    ls_s[2] = total
    for i in range(7):
        rcopy(ls_s.at[2], ls_r.at[2, z], l3_ss.at[i], l3_rs.at[z], zs[i]).start()
    ls_r[2, z] = ls_s[2]

    for j in (1, 2, 3):
        wait_recv(ig_r.at[j], ig_rs.at[j])
    for j in range(4):
        igrad_out[j:j + 1, :] = ig_r[j]

    def drain(c, carry):
        own = own_blocks.at[c]

        @pl.when(edge)
        def _():
            wait_send(own, g_ss.at[Z, c])

        wait_send(G.at[c, k], g_ss.at[SIB, c])

        @pl.when(c < GATHERED)
        def _():
            e = gathered(c)
            for kind in (A_MINUS, A_PLUS, A_FAR):
                wait_send(own, g_ss.at[kind, e])
            for kind in (B_MINUS, B_PLUS, B_FAR):
                wait_send(b_group(e, b), g_ss.at[kind, e])

            @pl.when(c < SHARED)
            def _():
                wait_send(G.at[e, k], g_ss.at[HAND, e])

        return carry

    lax.fori_loop(0, CHUNKS, drain, 0)

    @pl.when(source)
    def _():
        for p in range(len(PIECES)):
            for i in range(3):
                wait_send(a2a_s.at[0, :, piece_lanes(p)], x_ss.at[p, i])

    for i in range(3):
        wait_send(tx_s, tx_ss.at[i])
        wait_send(T.at[zl, k, zh, own_t, :], ty_ss.at[i])
        wait_send(ix_s, ix_ss.at[i])
        wait_send(ls_s.at[0], l1_ss.at[i])
        wait_send(cn_s.at[i + 1], cn_ss.at[i + 1])
        wait_send(ig_s.at[i + 1], ig_ss.at[i + 1])
        wait_send(text_ring(0), tz_ss.at[0, i])
        wait_send(text_ring(0), tz_ss.at[1, i])
    wait_send(text_ring(0), tz_ss.at[0, 3])
    wait_send(T.at[:, k], ts_ss.at[0])
    for i in range(1, 8):
        zz = m8(z + i)
        wait_recv(ps_r.at[zz], ps_rs.at[zz])
    text_push = ps_r[0]
    for i in range(1, 8):
        text_push = text_push + ps_r[i]
    tgrad_out[...] = (
        text_push - text_unit * jnp.sum(text_unit * text_push, axis=1, keepdims=True)
    ) * text_inv

    for i in range(1, 8):
        zz = m8(z + i)
        wait_recv(ls_r.at[2, zz], l3_rs.at[zz])
    total = ls_r[2, 0]
    for i in range(1, 8):
        total = total + ls_r[2, i]
    loss_out[...] = total[0:1, 0:1] / float(TEXTS)

    for i in range(7):
        wait_send(PI.at[k, own_t, :], iy_ss.at[i])
        wait_send(ls_s.at[1], l2_ss.at[i])
        wait_send(ps_s.at[0], ps_ss.at[i])
        wait_send(ls_s.at[2], l3_ss.at[i])


def per_device(
    patches, patch_counts, pack_offsets, norm_gain, mlp_in, mlp_out, probe_query, key_weight,
    value_weight, out_weight, text_embed, pair_label, logit_scale, logit_bias,
):
    vmem = pl.BlockSpec(memory_space=pltpu.VMEM)
    smem = pl.BlockSpec(memory_space=pltpu.SMEM)
    anywhere = pl.BlockSpec(memory_space=pl.ANY)
    dma = pltpu.SemaphoreType.DMA
    loss, image_grad, text_grad = pl.pallas_call(
        kernel,
        out_shape=(
            jax.ShapeDtypeStruct((1, 1), F32),
            jax.ShapeDtypeStruct((4, D), F32),
            jax.ShapeDtypeStruct((4, D), F32),
        ),
        in_specs=[
            anywhere, smem, smem, vmem, anywhere, anywhere, vmem, anywhere, anywhere, anywhere, vmem, vmem, smem, smem,
        ],
        out_specs=(vmem, vmem, vmem),
        scratch_shapes=[
            pltpu.VMEM((PACK, D), BF16),
            pltpu.VMEM((PACK, D), BF16),
            pltpu.VMEM((PACK, D), F32),
            pltpu.VMEM((PACK, 2 * LANES), BF16),
            pltpu.VMEM((CHUNKS, 2, 4, GROUP, LANES), BF16),
            pltpu.VMEM((CHUNKS, BLOCK, LANES), BF16),
            pltpu.VMEM((SHARD, FF), BF16),
            pltpu.VMEM((SHARD, FF), BF16),
            pltpu.VMEM((4, SLOT_ROWS, HALF), BF16),
            pltpu.VMEM((4, SLOT_ROWS, HALF), BF16),
            pltpu.VMEM((BLOCK, HALF), F32),
            pltpu.VMEM((4, 2, 2, 64, D), BF16),
            pltpu.VMEM((16, D), F32),
            pltpu.VMEM((16, D), BF16),
            pltpu.VMEM((4, 16, D), BF16),
            pltpu.VMEM((4, D), F32),
            pltpu.VMEM((4, 4, D), F32),
            pltpu.VMEM((16, D), F32),
            pltpu.VMEM((2, 64, D), BF16),
            pltpu.VMEM((64, D), F32),
            pltpu.VMEM((8, 4, D), F32),
            pltpu.VMEM((8, 4, D), F32),
            pltpu.VMEM((4, 1, D), F32),
            pltpu.VMEM((4, 1, D), F32),
            pltpu.VMEM((4, 8, LANES), I32),
            pltpu.VMEM((4, 8, LANES), I32),
            pltpu.VMEM((HEADS, D), BF16),
            pltpu.VMEM((D, D), BF16),
            pltpu.VMEM((D, D), BF16),
            pltpu.VMEM((D, D), BF16),
            pltpu.VMEM((8, LANES), F32),
            pltpu.VMEM((64, LANES), F32),
            pltpu.VMEM((3, 8, LANES), F32),
            pltpu.VMEM((3, 8, 8, LANES), F32),
            dma((7,)),
            dma((9, CHUNKS)), dma((9, CHUNKS)),
            dma((3, 3)), dma((3, 4)),
            dma((3,)), dma((4,)),
            dma((3,)), dma((4,)),
            dma((2, 4)), dma((2, 4)),
            dma((1,)), dma((1,)),
            dma((3,)), dma((4,)),
            dma((7,)), dma((2, 4)),
            dma((7,)), dma((8,)),
            dma((4,)), dma((4,)),
            dma((4,)), dma((4,)),
            dma((3,)), dma((4,)),
            dma((7,)), dma((8,)),
            dma((7,)), dma((8,)),
        ],
        compiler_params=pltpu.CompilerParams(
            collective_id=0, has_side_effects=True, vmem_limit_bytes=62 * 2**20
        ),
        cost_estimate=pl.CostEstimate(
            flops=4 * PACK * D * FF, bytes_accessed=12 * 2**20, transcendentals=PACK * FF
        ),
        name="pooled_loss",
    )(
        patches, patch_counts, pack_offsets, norm_gain, mlp_in, mlp_out.T,
        probe_query, key_weight, value_weight, out_weight, text_embed,
        pair_label.reshape(1, TEXTS), logit_scale, logit_bias,
    )
    return loss.reshape(()), image_grad, text_grad


def solution(mesh):
    placed = (
        P(("grp", "dp"), None), P(("grp", "dp")), P(("grp", "dp")), P(), P("dp", None), P(None, "dp"),
        P(), P(), P(), P(), P(("grp", "dp"), None), P(), P(), P(),
    )
    return jax.shard_map(
        per_device,
        mesh=mesh,
        in_specs=placed,
        out_specs=(P(), P(("grp", "dp"), None), P(("grp", "dp"), None)),
        check_vma=False,
    )
```

```python
import math

import jax
import jax.numpy as jnp
from jax import lax
from jax.experimental import pallas as pl
from jax.experimental.pallas import tpu as pltpu
from jax.sharding import PartitionSpec as P

MESH = pl.DeviceIdType.MESH
F32 = jnp.float32
BF16 = jnp.bfloat16
I32 = jnp.int32

EPSILON = 1e-06
D = 1152
FF = 4304
HEAD_DIM = 72
HEADS = 16
PACK = 1024
TEXTS = 1024
SHARD = 36
SLOT_ROWS = 48
LANES = 128
CHUNKS = 17
HALF = CHUNKS * LANES
BLOCK = 4 * SHARD
GROUP = 4 * BLOCK
TILE = 256
PLANE = 32

LAG_A, LAG_B, LAG_C, LAG_D, LAG_E = 3, 6, 9, 12, 13

SHARED = 3
GATHERED = CHUNKS - SHARED
TICKS = GATHERED + LAG_E
HANDED_TICKS = (18, 21, 24)
TWO_AT = (19, 22, 25)
TEXT_TICKS = (5, 9, 13, 17, 21, 24)
PIECES = ((0, 4), (4, 10), (10, 17))
PIECE_TICKS = (1, 4)

Z, A_MINUS, A_PLUS, A_FAR, B_MINUS, B_PLUS, B_FAR, SIB, HAND = range(9)

NT = (((1,), (1,)), ((), ()))


def gelu(hidden):
    c1 = math.sqrt(2.0 / math.pi)
    c2 = c1 * 0.044715
    inner = hidden * (c1 + c2 * (hidden * hidden))
    half = 0.5 * hidden
    return (half + half * jnp.tanh(inner)).astype(BF16)


def kernel(
    patches, counts, offsets, gain, win_hbm, woutt_hbm, probe, key_w, value_w, out_w, text, labels, scale, bias,
    loss_out, grads_out,
    xbuf, normed, acc, act, G, own_blocks, win, woutt, a2a_s, a2a_r, compact, T, line_f, tx_s, tx_r, ix_s, ix_r, plane_f, tcol,
    ps_s, ps_r, ig_s, ig_r, cn_s, cn_r, hk, kw, vw, ow, ilab, tlab, ls_s, ls_r,
    loc_sem, g_ss, g_rs, x_ss, x_rs, tx_ss, tx_rs, ty_ss, ty_rs, tz_ss, tz_rs, ts_ss, ts_rs,
    ix_ss, ix_rs, ps_ss, ps_rs, ig_ss, ig_rs, cn_ss, cn_rs,
    l1_ss, l1_rs, l2_ss, l2_rs, l3_ss, l3_rs,
):
    g = lax.axis_index("grp")
    d = lax.axis_index("dp")
    k = lax.rem(g, 2)
    zl = lax.div(g, 2)
    x = lax.rem(d, 4)
    y = lax.rem(lax.div(d, 4), 4)
    zh = lax.div(d, 16)
    z = zh * 4 + zl

    def dev(x_, y_, z_, k_):
        return (lax.rem(z_, 4) * 2 + k_, lax.div(z_, 4) * 16 + y_ * 4 + x_)

    def m4(v):
        return lax.rem(v, 4)

    def m8(v):
        return lax.rem(v, 8)

    sib = dev(x, y, z, 1 - k)
    xs = [dev(m4(x + i), y, z, k) for i in (1, 2, 3)]
    zs = [dev(x, y, m8(z + i), k) for i in range(1, 8)]
    group_dev = [(g, lax.rem(d + 8 * j, 32)) for j in range(4)]

    def rcopy(src, dst, ss, rs, to):
        return pltpu.make_async_remote_copy(
            src_ref=src, dst_ref=dst, send_sem=ss, recv_sem=rs, device_id=to, device_id_type=MESH
        )

    def wait_recv(ref, rs):
        rcopy(ref, ref, loc_sem.at[0], rs, sib).wait_recv()

    def wait_send(ref, ss):
        rcopy(ref, ref, ss, loc_sem.at[0], sib).wait_send()

    shards = [
        pltpu.make_async_copy(win_hbm, win, loc_sem.at[5]),
        pltpu.make_async_copy(woutt_hbm, woutt, loc_sem.at[6]),
    ]
    for cp in shards:
        cp.start()
    local = [
        pltpu.make_async_copy(patches, xbuf, loc_sem.at[1]),
        pltpu.make_async_copy(key_w, kw, loc_sem.at[2]),
        pltpu.make_async_copy(value_w, vw, loc_sem.at[3]),
        pltpu.make_async_copy(out_w, ow, loc_sem.at[4]),
    ]

    barrier = pltpu.get_barrier_semaphore()
    place = k * 16 + y * 4 + x

    def in_plane(q):
        return dev(m4(q), m4(lax.div(q, 4)), z, lax.div(q, 16))

    def greet(i, carry):
        q = lax.rem(place + i, PLANE)
        pl.semaphore_signal(barrier, inc=1, device_id=in_plane(q), device_id_type=MESH)
        return carry

    lax.fori_loop(1, PLANE, greet, 0)
    partners = list(zs) + [dev(x, m4(y + 2), m8(z + 4), k)]
    for p in partners:
        pl.semaphore_signal(barrier, inc=1, device_id=p, device_id_type=MESH)

    for cp in shards:
        cp.wait()
    local[0].start()

    source = k == zh

    @pl.when(source)
    def _():
        for part in range(4):
            shard = win if part < 2 else woutt
            if part % 2 == 0:
                a2a_s[part, 0:SHARD, :] = shard[:, 0:HALF]
            else:
                a2a_s[part, :, HALF - LANES:HALF] = jnp.zeros((SLOT_ROWS, LANES), BF16)
                a2a_s[part, 0:SHARD, 0:FF - HALF] = shard[:, HALF:FF]

    text_wide = text[...].astype(F32)
    text_inv = lax.rsqrt(jnp.sum(text_wide * text_wide, axis=1, keepdims=True) + EPSILON)
    text_unit = text_wide * text_inv
    tx_s[...] = jnp.zeros((16, D), BF16)
    tx_s[0:4, :] = text_unit.astype(BF16)
    for j in range(4):
        cn_s[j] = jnp.full((8, LANES), counts[j], I32)

    pl.semaphore_wait(barrier, PLANE - 1 + len(partners))

    def piece_lanes(p):
        return slice(PIECES[p][0] * LANES, PIECES[p][1] * LANES)

    @pl.when(source)
    def _():
        for p in range(len(PIECES)):
            at = piece_lanes(p)
            for i in range(3):
                to_x = m4(x + i + 1)
                rcopy(
                    a2a_s.at[to_x, :, at], a2a_r.at[x, :, at], x_ss.at[p, i], x_rs.at[p, x], xs[i]
                ).start()
        a2a_r[x] = a2a_s[x]

    for i in range(3):
        rcopy(tx_s, tx_r.at[x], tx_ss.at[i], tx_rs.at[x], xs[i]).start()
    tx_r[x] = tx_s[...]
    for j in (1, 2, 3):
        rcopy(cn_s.at[j], cn_r.at[j], cn_ss.at[j], cn_rs.at[j], group_dev[j]).start()
    cn_r[0] = cn_s[0]

    a = jnp.where(k == 0, y, x)
    b = jnp.where(k == 0, x, y)

    def along(axis_is_a, step):
        move_y = jnp.where(k == 0, 1, 0) if axis_is_a else jnp.where(k == 0, 0, 1)
        return dev(m4(x + (1 - move_y) * step), m4(y + move_y * step), z, k)

    a_plus, a_minus = along(True, 1), along(True, 3)
    b_plus, b_minus = along(False, 1), along(False, 3)

    def a_block(c, at):
        return G.at[c, k, b, pl.ds(pl.multiple_of(at * BLOCK, 16), BLOCK), :]

    def b_group(c, at):
        return G.at[c, k, at]

    def take_piece(p):
        at = piece_lanes(p)
        for i in (1, 2, 3):
            s = m4(x + i)
            wait_recv(a2a_r.at[s, :, at], x_rs.at[p, s])
        for s in range(4):
            compact[s * SHARD:(s + 1) * SHARD, at] = a2a_r[s, 0:SHARD, at].astype(F32)
        for c in range(*PIECES[p]):
            own_blocks[c] = compact[:, c * LANES:(c + 1) * LANES].astype(BF16)

    @pl.when(source)
    def _():
        take_piece(0)

    edge = jnp.logical_or(zl == 0, zl == 3)
    outward = jnp.where(zl == 3, 1, 7)
    z_to = dev(x, y, m8(z + jnp.where(source, outward, 8 - outward)), k)

    def t_block(zl_, k_, zh_):
        return T.at[zl_, k_, zh_]

    def z_parts(step):
        zz = m8(z + step)
        return m4(zz), lax.div(zz, 4)

    def text_ring(step):
        zl_, zh_ = z_parts(step)
        return T.at[zl_, k, zh_]

    z_plus, z_minus = zs[0], zs[6]
    own_t = pl.ds(pl.multiple_of(y * 16, 16), 16)

    def gather_line(received, wide):
        for s in range(4):
            wide[4 * s:4 * s + 4, :] = received[s, 0:4, :].astype(F32)
        return wide[...].astype(BF16)

    def label_cols(ids):
        rows = ids.shape[0]
        lanes = lax.broadcasted_iota(I32, (rows, TEXTS), 1)
        row = jnp.broadcast_to(labels[...].astype(F32), (rows, TEXTS))
        return jnp.sum(jnp.where(lanes == ids, row, 0.0), axis=1, keepdims=True)

    parity = lax.rem(zl, 2)
    hand_to = tuple(jnp.where(k == 0, p, m) for p, m in zip(z_plus, z_minus))

    def gathered(i):
        return jnp.where(i < SHARED, 2 * i + parity, i + SHARED)

    def part(c, p):
        pieces = [G[c, 0, p]]
        for yy in range(4):
            pieces.append(G[c, 1, yy, p * BLOCK:(p + 1) * BLOCK, :])
        return jnp.concatenate(pieces, axis=0)

    def w1_of(c):
        return jnp.concatenate([part(c, 0), part(c, 1)], axis=1)

    def w2_of(c):
        return jnp.concatenate([part(c, 2), part(c, 3)], axis=1)

    def chunk_at(u):
        at = [tick_ - LAG_E + j + 1 for j, tick_ in enumerate(TWO_AT)]
        later = [jnp.where(u > v, 1, 0) for v in at]
        c = gathered(u - sum(later))
        for j, v in enumerate(at):
            c = jnp.where(u == v, 2 * j + 1 - parity, c)
        return c

    def tick(t, carry):
        for p, at in enumerate(PIECE_TICKS):

            @pl.when(jnp.logical_and(source, t == at))
            def _():
                take_piece(p + 1)

        for q in range(2):

            @pl.when(2 * t + q < CHUNKS)
            def _():
                c = 2 * t + q
                own = own_blocks.at[c]

                @pl.when(jnp.logical_not(source))
                def _():
                    wait_recv(own, g_rs.at[Z, c])

                @pl.when(edge)
                def _():
                    rcopy(own, own, g_ss.at[Z, c], g_rs.at[Z, c], z_to).start()

        @pl.when(t < GATHERED)
        def _():
            c = gathered(t)
            own = own_blocks.at[c]
            there = a_block(c, a)
            rcopy(own, there, g_ss.at[A_MINUS, c], g_rs.at[A_MINUS, c], a_plus).start()
            rcopy(own, there, g_ss.at[A_PLUS, c], g_rs.at[A_PLUS, c], a_minus).start()
            there[...] = own[...]

        @pl.when(jnp.logical_and(t >= LAG_A, t < GATHERED + LAG_A))
        def _():
            even = lax.rem(t - LAG_A, 2) == 0
            c = gathered(t - LAG_A)
            blk = a_block(c, m4(a + jnp.where(even, 3, 1)))
            wait_recv(blk, g_rs.at[jnp.where(even, A_MINUS, A_PLUS), c])
            to = tuple(jnp.where(even, p, m) for p, m in zip(a_plus, a_minus))
            rcopy(blk, blk, g_ss.at[A_FAR, c], g_rs.at[A_FAR, c], to).start()

        @pl.when(jnp.logical_and(t >= LAG_C, t < GATHERED + LAG_C))
        def _():
            even = lax.rem(t - LAG_C, 2) == 0
            c = gathered(t - LAG_C)
            grp = b_group(c, m4(b + jnp.where(even, 3, 1)))
            wait_recv(grp, g_rs.at[jnp.where(even, B_MINUS, B_PLUS), c])
            to = tuple(jnp.where(even, p, m) for p, m in zip(b_plus, b_minus))
            rcopy(grp, grp, g_ss.at[B_FAR, c], g_rs.at[B_FAR, c], to).start()

        @pl.when(jnp.logical_and(t >= LAG_B, t < GATHERED + LAG_B))
        def _():
            even = lax.rem(t - LAG_B, 2) == 0
            c = gathered(t - LAG_B)
            wait_recv(a_block(c, m4(a + jnp.where(even, 1, 3))), g_rs.at[jnp.where(even, A_PLUS, A_MINUS), c])
            wait_recv(a_block(c, m4(a + 2)), g_rs.at[A_FAR, c])
            grp = b_group(c, b)
            rcopy(grp, grp, g_ss.at[B_MINUS, c], g_rs.at[B_MINUS, c], b_plus).start()
            rcopy(grp, grp, g_ss.at[B_PLUS, c], g_rs.at[B_PLUS, c], b_minus).start()

        @pl.when(jnp.logical_and(t >= LAG_D, t < GATHERED + LAG_D))
        def _():
            even = lax.rem(t - LAG_D, 2) == 0
            i = t - LAG_D
            c = gathered(i)
            wait_recv(b_group(c, m4(b + jnp.where(even, 1, 3))), g_rs.at[jnp.where(even, B_PLUS, B_MINUS), c])
            wait_recv(b_group(c, m4(b + 2)), g_rs.at[B_FAR, c])
            half = G.at[c, k]
            rcopy(half, half, g_ss.at[SIB, c], g_rs.at[SIB, c], sib).start()

            @pl.when(i < SHARED)
            def _():
                rcopy(half, half, g_ss.at[HAND, c], g_rs.at[HAND, c], hand_to).start()

        for j, at in enumerate(HANDED_TICKS):

            @pl.when(t == at)
            def _():
                c = 2 * j + 1 - parity
                half = G.at[c, k]
                wait_recv(half, g_rs.at[HAND, c])
                rcopy(half, half, g_ss.at[SIB, c], g_rs.at[SIB, c], sib).start()

        @pl.when(t == TEXT_TICKS[0])
        def _():
            for i in (1, 2, 3):
                s = m4(x + i)
                wait_recv(tx_r.at[s], tx_rs.at[s])
            T[zl, k, zh, own_t, :] = gather_line(tx_r, line_f)
            blk = T.at[zl, k, zh, own_t, :]
            for i in (1, 2, 3):
                rcopy(blk, blk, ty_ss.at[i - 1], ty_rs.at[y], dev(x, m4(y + i), z, k)).start()

        @pl.when(t == TEXT_TICKS[1])
        def _():
            for i in (1, 2, 3):
                yy = m4(y + i)
                wait_recv(T.at[zl, k, zh, pl.ds(pl.multiple_of(yy * 16, 16), 16), :], ty_rs.at[yy])
            blk = text_ring(0)
            rcopy(blk, blk, tz_ss.at[0, 0], tz_rs.at[0, 0], z_plus).start()
            rcopy(blk, blk, tz_ss.at[1, 0], tz_rs.at[1, 0], z_minus).start()

        for hop in (1, 2):

            @pl.when(t == TEXT_TICKS[1 + hop])
            def _():
                low, high = text_ring(8 - hop), text_ring(hop)
                wait_recv(low, tz_rs.at[0, hop - 1])
                wait_recv(high, tz_rs.at[1, hop - 1])
                rcopy(low, low, tz_ss.at[0, hop], tz_rs.at[0, hop], z_plus).start()
                rcopy(high, high, tz_ss.at[1, hop], tz_rs.at[1, hop], z_minus).start()

        @pl.when(t == TEXT_TICKS[4])
        def _():
            low, high = text_ring(5), text_ring(3)
            wait_recv(low, tz_rs.at[0, 2])
            wait_recv(high, tz_rs.at[1, 2])

            @pl.when(k == 0)
            def _():
                rcopy(low, low, tz_ss.at[0, 3], tz_rs.at[0, 3], z_plus).start()

            @pl.when(k == 1)
            def _():
                rcopy(high, high, tz_ss.at[0, 3], tz_rs.at[0, 3], z_minus).start()

        @pl.when(t == TEXT_TICKS[5])
        def _():
            wait_recv(text_ring(4), tz_rs.at[0, 3])
            mine = T.at[:, k]
            rcopy(mine, mine, ts_ss.at[0], ts_rs.at[0], sib).start()

        @pl.when(t == TEXT_TICKS[5] + 1)
        def _():
            for zz in range(8):
                block = T[zz % 4, k, zz // 4, own_t, :].astype(F32)
                mine = jnp.zeros((4, D), F32)
                for s in range(4):
                    mine = mine + jnp.where(x == s, 1.0, 0.0) * block[4 * s:4 * s + 4, :]
                tcol[8 * zz:8 * zz + 4, :] = mine
                tcol[8 * zz + 4:8 * zz + 8, :] = jnp.zeros((4, D), F32)

        @pl.when(t == 0)
        def _():
            local[1].start()

        @pl.when(t == 1)
        def _():
            local[0].wait()

        @pl.when(t == 8)
        def _():
            local[2].start()
            local[3].start()

        @pl.when(jnp.logical_and(t >= 1, t <= PACK // TILE))
        def _():
            sl = pl.ds(pl.multiple_of((t - 1) * TILE, TILE), TILE)
            wide = xbuf[sl, :].astype(F32)
            center = jnp.mean(wide, axis=1, keepdims=True)
            off = wide - center
            spread = jnp.mean(off * off, axis=1, keepdims=True)
            normed[sl, :] = (off * lax.rsqrt(spread + EPSILON) * gain[...].reshape(1, D)).astype(BF16)
            acc[sl, :] = wide
            act[sl, :] = jnp.zeros((TILE, 2 * LANES), BF16)

        @pl.when(t == 7)
        def _():
            local[1].wait()
            head_of = lax.div(lax.broadcasted_iota(I32, (HEADS, D), 1), HEAD_DIM)
            own_head = head_of == lax.broadcasted_iota(I32, (HEADS, D), 0)
            block = jnp.where(own_head, jnp.broadcast_to(probe[...].astype(F32).reshape(1, D), (HEADS, D)), 0.0)
            keys = lax.dot_general(block.astype(BF16), kw[...], NT, preferred_element_type=F32)
            hk[...] = (keys / math.sqrt(HEAD_DIM)).astype(BF16)

            pos = lax.broadcasted_iota(I32, (LANES, 1), 0)
            slot = lax.rem(pos, 4)
            px = lax.rem(lax.div(pos, 4), 4)
            py = lax.rem(lax.div(pos, 16), 4)
            pk = lax.div(pos, 64)
            owner = lax.rem(16 * zh + 4 * py + px + 32 - 8 * slot, 32)
            ids = 4 * ((2 * zl + pk) * 32 + owner) + slot
            hot = lax.broadcasted_iota(I32, (LANES, TEXTS), 1) == ids
            hot = jnp.where(hot, 1.0, 0.0).astype(BF16)
            lab = labels[...]
            high = lax.div(lab, 16)
            low = lab - 16 * high
            pair = jnp.where(
                lax.broadcasted_iota(I32, (16, TEXTS), 0) == 0,
                jnp.broadcast_to(high, (16, TEXTS)),
                jnp.broadcast_to(low, (16, TEXTS)),
            ).astype(F32).astype(BF16)
            rows = lax.dot_general(pair, hot, NT, preferred_element_type=F32)
            ilab[...] = jnp.broadcast_to(16.0 * rows[0:1, :] + rows[1:2, :], (8, LANES))
            tpos = lax.broadcasted_iota(I32, (64, 1), 0)
            tz = lax.div(tpos, 8)
            tid = m4(tz) * 256 + k * 128 + lax.div(tz, 4) * 64 + y * 16 + x * 4 + m4(tpos)
            tlab[...] = jnp.broadcast_to(label_cols(tid), (64, LANES))

        @pl.when(jnp.logical_and(t >= LAG_E, t < GATHERED + LAG_E))
        def _():
            first = t - LAG_E + sum(jnp.where(t > v, 1, 0) for v in TWO_AT)
            many = 1 + sum(jnp.where(t == v, 1, 0) for v in TWO_AT)

            def one(n, carry):
                u = first + n
                c = chunk_at(u)
                before = chunk_at(jnp.maximum(u - 1, 0))
                wait_recv(G.at[c, 1 - k], g_rs.at[SIB, c])
                w1, w2 = w1_of(c), w2_of(before)
                for r in range(PACK // TILE):
                    sl = slice(r * TILE, (r + 1) * TILE)
                    old = act[sl, :]
                    hidden = jnp.dot(normed[sl, :], w1, preferred_element_type=F32)
                    acc[sl, :] += lax.dot_general(old, w2, NT, preferred_element_type=F32)
                    act[sl, :] = gelu(hidden)
                return carry

            lax.fori_loop(0, many, one, 0)

        return carry

    lax.fori_loop(0, TICKS, tick, 0)

    states = normed
    w2 = w2_of(chunk_at(CHUNKS - 1))
    score_tiles = []
    for r in range(PACK // TILE):
        sl = slice(r * TILE, (r + 1) * TILE)
        mixed = lax.dot_general(act[sl, :], w2, NT, preferred_element_type=F32)
        low = (acc[sl, :] + mixed).astype(BF16)
        states[sl, :] = low
        score_tiles.append(lax.dot_general(hk[...], low, NT, preferred_element_type=F32))
    scores = jnp.concatenate(score_tiles, axis=1)
    row = lax.broadcasted_iota(I32, (HEADS, PACK), 1)
    all_weights = []
    for j in range(4):
        if j > 0:
            wait_recv(cn_r.at[j], cn_rs.at[j])
        first = offsets[j]
        count = cn_r[j][0:1, 0:1]
        member = jnp.logical_and(row >= first, row < first + count)
        masked = jnp.where(member, scores, -1e30)
        highest = jnp.max(masked, axis=1, keepdims=True)
        raised = jnp.exp(masked - highest)
        all_weights.append(raised / jnp.sum(raised, axis=1, keepdims=True))
    weights = jnp.concatenate(all_weights, axis=0).astype(BF16)
    mean_states = jnp.dot(weights, states[...], preferred_element_type=F32).astype(BF16)
    local[2].wait()
    local[3].wait()
    full = jnp.dot(mean_states, vw[...], preferred_element_type=F32)
    head_of = lax.div(lax.broadcasted_iota(I32, (HEADS, D), 1), HEAD_DIM)
    own_head = head_of == lax.broadcasted_iota(I32, (HEADS, D), 0)
    values = [
        jnp.sum(jnp.where(own_head, full[HEADS * j:HEADS * (j + 1), :], 0.0), axis=0, keepdims=True)
        for j in range(4)
    ]
    mixed = jnp.concatenate(values + [jnp.zeros((12, D), F32)], axis=0).astype(BF16)
    pooled = jnp.dot(mixed, ow[...], preferred_element_type=F32)[0:8, :]
    image_inv = lax.rsqrt(jnp.sum(pooled * pooled, axis=1, keepdims=True) + EPSILON)
    image_unit = pooled * image_inv
    image_low = jnp.concatenate([image_unit, jnp.zeros((8, D), F32)], axis=0).astype(BF16)
    ix_s[...] = image_unit[0:4].astype(BF16)

    def send_images(i, carry):
        q = lax.rem(place + i, PLANE)
        rcopy(ix_s, ix_r.at[place], ix_ss.at[i], ix_rs.at[place], in_plane(q)).start()
        return carry

    lax.fori_loop(1, PLANE, send_images, 0)
    ix_r[place] = ix_s[...]

    mult = scale[0]
    shift = bias[0]

    wait_recv(T.at[:, 1 - k], ts_rs.at[0])
    texts = T[...].reshape(TEXTS, D)
    own_logits = mult * lax.dot_general(image_low, texts, NT, preferred_element_type=F32) + shift
    slot = lax.broadcasted_iota(I32, (16, 1), 0)
    slot4 = m4(slot)
    own_ids = 4 * (g * 32 + lax.rem(d + 32 - 8 * slot4, 32)) + slot4
    own_lab = label_cols(own_ids)
    sign = jnp.where(own_lab == labels[...].astype(F32), 1.0, -1.0)
    signed = sign * own_logits
    terms = jnp.log1p(jnp.exp(-jnp.abs(signed))) + jnp.maximum(-signed, 0.0)
    terms = jnp.where(slot < 4, terms, 0.0)
    part_loss = jnp.sum(jnp.sum(terms, axis=1, keepdims=True), axis=0, keepdims=True)
    ls_s[0] = jnp.broadcast_to(part_loss, (8, LANES))
    for i in range(3):
        rcopy(ls_s.at[0], ls_r.at[0, x], l1_ss.at[i], l1_rs.at[x], xs[i]).start()
    ls_r[0, x] = ls_s[0]

    others = [(m4(y + i), c_) for i in (1, 2, 3) for c_ in (0, 1)]
    to_plane = [dev(x, yy, z, c_) for yy, c_ in others] + [sib]

    own_slope = (mult * -sign * jax.nn.sigmoid(-signed)).astype(BF16)
    image_push = jnp.dot(own_slope, texts, preferred_element_type=F32)[0:8, :]
    image_grad = (
        image_push - image_unit * jnp.sum(image_unit * image_push, axis=1, keepdims=True)
    ) * image_inv
    for j in range(4):
        ig_s[j] = image_grad[j:j + 1, :]
    for j in (1, 2, 3):
        rcopy(ig_s.at[j], ig_r.at[j], ig_ss.at[j], ig_rs.at[j], group_dev[4 - j]).start()
    ig_r[0] = ig_s[0]

    for i in (1, 2, 3):
        s = m4(x + i)
        wait_recv(ls_r.at[0, s], l1_rs.at[s])
    ls_s[1] = ls_r[0, 0] + ls_r[0, 1] + ls_r[0, 2] + ls_r[0, 3]
    me8 = k * 4 + y
    for i, to in enumerate(to_plane):
        rcopy(ls_s.at[1], ls_r.at[1, me8], l2_ss.at[i], l2_rs.at[me8], to).start()
    ls_r[1, me8] = ls_s[1]

    def take_images(i, carry):
        q = lax.rem(place + i, PLANE)
        wait_recv(ix_r.at[q], ix_rs.at[q])
        return carry

    lax.fori_loop(1, PLANE, take_images, 0)
    for q in range(PLANE):
        plane_f[4 * q:4 * q + 4, :] = ix_r[q].astype(F32)
    plane = plane_f[...].astype(BF16)
    plane_logits = mult * lax.dot_general(
        tcol[...].astype(BF16), plane, NT, preferred_element_type=F32
    ) + shift
    plane_sign = jnp.where(tlab[...] == ilab[0:1, :], 1.0, -1.0)
    plane_slope = (mult * -plane_sign * jax.nn.sigmoid(-plane_sign * plane_logits)).astype(BF16)
    push = jnp.dot(plane_slope, plane, preferred_element_type=F32)
    for zz in range(8):
        ps_s[zz] = push[8 * zz:8 * zz + 4, :]
    for i in range(7):
        to_z = m8(z + i + 1)
        rcopy(ps_s.at[to_z], ps_r.at[z], ps_ss.at[i], ps_rs.at[z], zs[i]).start()
    ps_r[z] = ps_s[z]

    for yy, c_ in others + [(y, 1 - k)]:
        wait_recv(ls_r.at[1, c_ * 4 + yy], l2_rs.at[c_ * 4 + yy])
    total = ls_r[1, 0]
    for i in range(1, 8):
        total = total + ls_r[1, i]
    ls_s[2] = total
    for i in range(7):
        rcopy(ls_s.at[2], ls_r.at[2, z], l3_ss.at[i], l3_rs.at[z], zs[i]).start()
    ls_r[2, z] = ls_s[2]

    for j in (1, 2, 3):
        wait_recv(ig_r.at[j], ig_rs.at[j])
    for j in range(4):
        grads_out[j:j + 1, :] = ig_r[j]

    def drain(c, carry):
        own = own_blocks.at[c]

        @pl.when(edge)
        def _():
            wait_send(own, g_ss.at[Z, c])

        wait_send(G.at[c, k], g_ss.at[SIB, c])

        @pl.when(c < GATHERED)
        def _():
            e = gathered(c)
            for kind in (A_MINUS, A_PLUS, A_FAR):
                wait_send(own, g_ss.at[kind, e])
            for kind in (B_MINUS, B_PLUS, B_FAR):
                wait_send(b_group(e, b), g_ss.at[kind, e])

            @pl.when(c < SHARED)
            def _():
                wait_send(G.at[e, k], g_ss.at[HAND, e])

        return carry

    lax.fori_loop(0, CHUNKS, drain, 0)

    @pl.when(source)
    def _():
        for p in range(len(PIECES)):
            for i in range(3):
                wait_send(a2a_s.at[0, :, piece_lanes(p)], x_ss.at[p, i])

    for i in range(3):
        wait_send(tx_s, tx_ss.at[i])
        wait_send(T.at[zl, k, zh, own_t, :], ty_ss.at[i])
        wait_send(ls_s.at[0], l1_ss.at[i])
        wait_send(cn_s.at[i + 1], cn_ss.at[i + 1])
        wait_send(ig_s.at[i + 1], ig_ss.at[i + 1])
        wait_send(text_ring(0), tz_ss.at[0, i])
        wait_send(text_ring(0), tz_ss.at[1, i])
    wait_send(text_ring(0), tz_ss.at[0, 3])
    wait_send(T.at[:, k], ts_ss.at[0])
    for i in range(1, 8):
        zz = m8(z + i)
        wait_recv(ps_r.at[zz], ps_rs.at[zz])
    text_push = ps_r[0]
    for i in range(1, 8):
        text_push = text_push + ps_r[i]
    grads_out[4:8, :] = (
        text_push - text_unit * jnp.sum(text_unit * text_push, axis=1, keepdims=True)
    ) * text_inv

    for i in range(1, 8):
        zz = m8(z + i)
        wait_recv(ls_r.at[2, zz], l3_rs.at[zz])
    total = ls_r[2, 0]
    for i in range(1, 8):
        total = total + ls_r[2, i]
    loss_out[...] = total[0:1, 0:1] / float(TEXTS)

    def sent_images(i, carry):
        wait_send(ix_s, ix_ss.at[i])
        return carry

    lax.fori_loop(1, PLANE, sent_images, 0)
    for i in range(7):
        wait_send(ls_s.at[1], l2_ss.at[i])
        wait_send(ps_s.at[0], ps_ss.at[i])
        wait_send(ls_s.at[2], l3_ss.at[i])


def per_device(
    patches, patch_counts, pack_offsets, norm_gain, mlp_in, mlp_out, probe_query, key_weight,
    value_weight, out_weight, text_embed, pair_label, logit_scale, logit_bias,
):
    vmem = pl.BlockSpec(memory_space=pltpu.VMEM)
    smem = pl.BlockSpec(memory_space=pltpu.SMEM)
    anywhere = pl.BlockSpec(memory_space=pl.ANY)
    dma = pltpu.SemaphoreType.DMA
    loss, grads = pl.pallas_call(
        kernel,
        out_shape=(
            jax.ShapeDtypeStruct((1, 1), F32),
            jax.ShapeDtypeStruct((8, D), F32),
        ),
        in_specs=[
            anywhere, smem, smem, vmem, anywhere, anywhere, vmem, anywhere, anywhere, anywhere, vmem, vmem, smem, smem,
        ],
        out_specs=(vmem, vmem),
        scratch_shapes=[
            pltpu.VMEM((PACK, D), BF16),
            pltpu.VMEM((PACK, D), BF16),
            pltpu.VMEM((PACK, D), F32),
            pltpu.VMEM((PACK, 2 * LANES), BF16),
            pltpu.VMEM((CHUNKS, 2, 4, GROUP, LANES), BF16),
            pltpu.VMEM((CHUNKS, BLOCK, LANES), BF16),
            pltpu.VMEM((SHARD, FF), BF16),
            pltpu.VMEM((SHARD, FF), BF16),
            pltpu.VMEM((4, SLOT_ROWS, HALF), BF16),
            pltpu.VMEM((4, SLOT_ROWS, HALF), BF16),
            pltpu.VMEM((BLOCK, HALF), F32),
            pltpu.VMEM((4, 2, 2, 64, D), BF16),
            pltpu.VMEM((16, D), F32),
            pltpu.VMEM((16, D), BF16),
            pltpu.VMEM((4, 16, D), BF16),
            pltpu.VMEM((4, D), BF16),
            pltpu.VMEM((PLANE, 4, D), BF16),
            pltpu.VMEM((LANES, D), F32),
            pltpu.VMEM((64, D), F32),
            pltpu.VMEM((8, 4, D), F32),
            pltpu.VMEM((8, 4, D), F32),
            pltpu.VMEM((4, 1, D), F32),
            pltpu.VMEM((4, 1, D), F32),
            pltpu.VMEM((4, 8, LANES), I32),
            pltpu.VMEM((4, 8, LANES), I32),
            pltpu.VMEM((HEADS, D), BF16),
            pltpu.VMEM((D, D), BF16),
            pltpu.VMEM((D, D), BF16),
            pltpu.VMEM((D, D), BF16),
            pltpu.VMEM((8, LANES), F32),
            pltpu.VMEM((64, LANES), F32),
            pltpu.VMEM((3, 8, LANES), F32),
            pltpu.VMEM((3, 8, 8, LANES), F32),
            dma((7,)),
            dma((9, CHUNKS)), dma((9, CHUNKS)),
            dma((3, 3)), dma((3, 4)),
            dma((3,)), dma((4,)),
            dma((3,)), dma((4,)),
            dma((2, 4)), dma((2, 4)),
            dma((1,)), dma((1,)),
            dma((PLANE,)), dma((PLANE,)),
            dma((7,)), dma((8,)),
            dma((4,)), dma((4,)),
            dma((4,)), dma((4,)),
            dma((3,)), dma((4,)),
            dma((7,)), dma((8,)),
            dma((7,)), dma((8,)),
        ],
        compiler_params=pltpu.CompilerParams(
            collective_id=0, has_side_effects=True, vmem_limit_bytes=62 * 2**20
        ),
        cost_estimate=pl.CostEstimate(
            flops=4 * PACK * D * FF, bytes_accessed=12 * 2**20, transcendentals=PACK * FF
        ),
        name="pooled_loss",
    )(
        patches, patch_counts, pack_offsets, norm_gain, mlp_in, mlp_out.T,
        probe_query, key_weight, value_weight, out_weight, text_embed,
        pair_label.reshape(1, TEXTS), logit_scale, logit_bias,
    )
    return loss.reshape(()), grads[0:4], grads[4:8]


def solution(mesh):
    placed = (
        P(("grp", "dp"), None), P(("grp", "dp")), P(("grp", "dp")), P(), P("dp", None), P(None, "dp"),
        P(), P(), P(), P(), P(("grp", "dp"), None), P(), P(), P(),
    )
    return jax.shard_map(
        per_device,
        mesh=mesh,
        in_specs=placed,
        out_specs=(P(), P(("grp", "dp"), None), P(("grp", "dp"), None)),
        check_vma=False,
    )
```

```python
import math

import jax
import jax.numpy as jnp
from jax import lax
from jax.experimental import pallas as pl
from jax.experimental.pallas import tpu as pltpu
from jax.sharding import PartitionSpec as P

MESH = pl.DeviceIdType.MESH
F32 = jnp.float32
BF16 = jnp.bfloat16
I32 = jnp.int32

EPSILON = 1e-06
D = 1152
FF = 4304
HEAD_DIM = 72
HEADS = 16
PACK = 1024
TEXTS = 1024
SHARD = 36
SLOT_ROWS = 48
LANES = 128
CHUNKS = 17
HALF = CHUNKS * LANES
BLOCK = 4 * SHARD
GROUP = 4 * BLOCK
TILE = 256
PLANE = 32

LAG_A, LAG_B, LAG_C, LAG_D, LAG_E = 3, 6, 9, 12, 13

SHARED = 3
SHARED_AT = (0, 3, 7)
GATHERED = CHUNKS - SHARED
TICKS = GATHERED + LAG_E
HANDED_TICKS = (17, 20, 23)
TWO_AT = (18, 21, 24)
TEXT_TICKS = (5, 9, 13, 17, 21, 24)
PIECES = ((0, 4), (4, 8), (8, 17))
PIECE_TICKS = (1, 2)

Z, A_MINUS, A_PLUS, A_FAR, B_MINUS, B_PLUS, B_FAR, SIB, HAND = range(9)

NT = (((1,), (1,)), ((), ()))


def gelu(hidden):
    c1 = math.sqrt(2.0 / math.pi)
    c2 = c1 * 0.044715
    inner = hidden * (c1 + c2 * (hidden * hidden))
    half = 0.5 * hidden
    return (half + half * jnp.tanh(inner)).astype(BF16)


def kernel(
    patches, counts, offsets, gain, win_hbm, woutt_hbm, probe, key_w, value_w, out_w, text, labels, scale, bias,
    loss_out, grads_out,
    xbuf, normed, acc, act, G, own_blocks, win, woutt, a2a_s, a2a_r, compact, T, line_f, tx_s, tx_r, ix_s, ix_r, plane_f, tcol,
    ps_s, ps_r, ig_s, ig_r, cn_s, cn_r, hk, kw, vw, ow, ilab, tlab, ls_s, ls_r,
    loc_sem, g_ss, g_rs, x_ss, x_rs, tx_ss, tx_rs, ty_ss, ty_rs, tz_ss, tz_rs, ts_ss, ts_rs,
    ix_ss, ix_rs, ps_ss, ps_rs, ig_ss, ig_rs, cn_ss, cn_rs,
    l1_ss, l1_rs, l2_ss, l2_rs, l3_ss, l3_rs,
):
    g = lax.axis_index("grp")
    d = lax.axis_index("dp")
    k = lax.rem(g, 2)
    zl = lax.div(g, 2)
    x = lax.rem(d, 4)
    y = lax.rem(lax.div(d, 4), 4)
    zh = lax.div(d, 16)
    z = zh * 4 + zl

    def dev(x_, y_, z_, k_):
        return (lax.rem(z_, 4) * 2 + k_, lax.div(z_, 4) * 16 + y_ * 4 + x_)

    def m4(v):
        return lax.rem(v, 4)

    def m8(v):
        return lax.rem(v, 8)

    sib = dev(x, y, z, 1 - k)
    xs = [dev(m4(x + i), y, z, k) for i in (1, 2, 3)]
    zs = [dev(x, y, m8(z + i), k) for i in range(1, 8)]
    group_dev = [(g, lax.rem(d + 8 * j, 32)) for j in range(4)]

    def rcopy(src, dst, ss, rs, to):
        return pltpu.make_async_remote_copy(
            src_ref=src, dst_ref=dst, send_sem=ss, recv_sem=rs, device_id=to, device_id_type=MESH
        )

    def wait_recv(ref, rs):
        rcopy(ref, ref, loc_sem.at[0], rs, sib).wait_recv()

    def wait_send(ref, ss):
        rcopy(ref, ref, ss, loc_sem.at[0], sib).wait_send()

    shards = [
        pltpu.make_async_copy(win_hbm, win, loc_sem.at[5]),
        pltpu.make_async_copy(woutt_hbm, woutt, loc_sem.at[6]),
    ]
    for cp in shards:
        cp.start()
    local = [
        pltpu.make_async_copy(patches, xbuf, loc_sem.at[1]),
        pltpu.make_async_copy(key_w, kw, loc_sem.at[2]),
        pltpu.make_async_copy(value_w, vw, loc_sem.at[3]),
        pltpu.make_async_copy(out_w, ow, loc_sem.at[4]),
    ]

    barrier = pltpu.get_barrier_semaphore()
    place = k * 16 + y * 4 + x

    def in_plane(q):
        return dev(m4(q), m4(lax.div(q, 4)), z, lax.div(q, 16))

    def greet(i, carry):
        q = lax.rem(place + i, PLANE)
        pl.semaphore_signal(barrier, inc=1, device_id=in_plane(q), device_id_type=MESH)
        return carry

    lax.fori_loop(1, PLANE, greet, 0)
    partners = list(zs) + [dev(x, m4(y + 2), m8(z + 4), k)]
    for p in partners:
        pl.semaphore_signal(barrier, inc=1, device_id=p, device_id_type=MESH)

    for cp in shards:
        cp.wait()
    local[0].start()

    source = k == zh

    @pl.when(source)
    def _():
        for part in range(4):
            shard = win if part < 2 else woutt
            if part % 2 == 0:
                a2a_s[part, 0:SHARD, :] = shard[:, 0:HALF]
            else:
                a2a_s[part, :, HALF - LANES:HALF] = jnp.zeros((SLOT_ROWS, LANES), BF16)
                a2a_s[part, 0:SHARD, 0:FF - HALF] = shard[:, HALF:FF]

    text_wide = text[...].astype(F32)
    text_inv = lax.rsqrt(jnp.sum(text_wide * text_wide, axis=1, keepdims=True) + EPSILON)
    text_unit = text_wide * text_inv
    tx_s[...] = jnp.zeros((16, D), BF16)
    tx_s[0:4, :] = text_unit.astype(BF16)
    for j in range(4):
        cn_s[j] = jnp.full((8, LANES), counts[j], I32)

    pl.semaphore_wait(barrier, PLANE - 1 + len(partners))

    def piece_lanes(p):
        return slice(PIECES[p][0] * LANES, PIECES[p][1] * LANES)

    @pl.when(source)
    def _():
        for p in range(len(PIECES)):
            at = piece_lanes(p)
            for i in range(3):
                to_x = m4(x + i + 1)
                rcopy(
                    a2a_s.at[to_x, :, at], a2a_r.at[x, :, at], x_ss.at[p, i], x_rs.at[p, x], xs[i]
                ).start()
        a2a_r[x] = a2a_s[x]

    for i in range(3):
        rcopy(tx_s, tx_r.at[x], tx_ss.at[i], tx_rs.at[x], xs[i]).start()
    tx_r[x] = tx_s[...]
    for j in (1, 2, 3):
        rcopy(cn_s.at[j], cn_r.at[j], cn_ss.at[j], cn_rs.at[j], group_dev[j]).start()
    cn_r[0] = cn_s[0]

    a = jnp.where(k == 0, y, x)
    b = jnp.where(k == 0, x, y)

    def along(axis_is_a, step):
        move_y = jnp.where(k == 0, 1, 0) if axis_is_a else jnp.where(k == 0, 0, 1)
        return dev(m4(x + (1 - move_y) * step), m4(y + move_y * step), z, k)

    a_plus, a_minus = along(True, 1), along(True, 3)
    b_plus, b_minus = along(False, 1), along(False, 3)

    def a_block(c, at):
        return G.at[c, k, b, pl.ds(pl.multiple_of(at * BLOCK, 16), BLOCK), :]

    def b_group(c, at):
        return G.at[c, k, at]

    def take_piece(p):
        at = piece_lanes(p)
        for i in (1, 2, 3):
            s = m4(x + i)
            wait_recv(a2a_r.at[s, :, at], x_rs.at[p, s])
        for s in range(4):
            compact[s * SHARD:(s + 1) * SHARD, at] = a2a_r[s, 0:SHARD, at].astype(F32)
        for c in range(*PIECES[p]):
            own_blocks[c] = compact[:, c * LANES:(c + 1) * LANES].astype(BF16)

    @pl.when(source)
    def _():
        take_piece(0)

    edge = jnp.logical_or(zl == 0, zl == 3)
    outward = jnp.where(zl == 3, 1, 7)
    z_to = dev(x, y, m8(z + jnp.where(source, outward, 8 - outward)), k)

    def t_block(zl_, k_, zh_):
        return T.at[zl_, k_, zh_]

    def z_parts(step):
        zz = m8(z + step)
        return m4(zz), lax.div(zz, 4)

    def text_ring(step):
        zl_, zh_ = z_parts(step)
        return T.at[zl_, k, zh_]

    z_plus, z_minus = zs[0], zs[6]
    own_t = pl.ds(pl.multiple_of(y * 16, 16), 16)

    def gather_line(received, wide):
        for s in range(4):
            wide[4 * s:4 * s + 4, :] = received[s, 0:4, :].astype(F32)
        return wide[...].astype(BF16)

    def label_cols(ids):
        rows = ids.shape[0]
        lanes = lax.broadcasted_iota(I32, (rows, TEXTS), 1)
        row = jnp.broadcast_to(labels[...].astype(F32), (rows, TEXTS))
        return jnp.sum(jnp.where(lanes == ids, row, 0.0), axis=1, keepdims=True)

    parity = lax.rem(zl, 2)
    hand_to = tuple(jnp.where(k == 0, p, m) for p, m in zip(z_plus, z_minus))

    def gathered(i):
        c = i + 2 * SHARED - sum(jnp.where(i > at, 1, 0) for at in SHARED_AT)
        for j, at in enumerate(SHARED_AT):
            c = jnp.where(i == at, 2 * j + parity, c)
        return c

    def part(c, p):
        pieces = [G[c, 0, p]]
        for yy in range(4):
            pieces.append(G[c, 1, yy, p * BLOCK:(p + 1) * BLOCK, :])
        return jnp.concatenate(pieces, axis=0)

    def w1_of(c):
        return jnp.concatenate([part(c, 0), part(c, 1)], axis=1)

    def w2_of(c):
        return jnp.concatenate([part(c, 2), part(c, 3)], axis=1)

    def chunk_at(u):
        at = [tick_ - LAG_E + j + 1 for j, tick_ in enumerate(TWO_AT)]
        later = [jnp.where(u > v, 1, 0) for v in at]
        c = gathered(u - sum(later))
        for j, v in enumerate(at):
            c = jnp.where(u == v, 2 * j + 1 - parity, c)
        return c

    def tick(t, carry):
        for p, at in enumerate(PIECE_TICKS):

            @pl.when(jnp.logical_and(source, t == at))
            def _():
                take_piece(p + 1)

        for q in range(4):

            @pl.when(4 * t + q < CHUNKS)
            def _():
                c = 4 * t + q
                own = own_blocks.at[c]

                @pl.when(jnp.logical_not(source))
                def _():
                    wait_recv(own, g_rs.at[Z, c])

                @pl.when(edge)
                def _():
                    rcopy(own, own, g_ss.at[Z, c], g_rs.at[Z, c], z_to).start()

        @pl.when(t < GATHERED)
        def _():
            c = gathered(t)
            own = own_blocks.at[c]
            there = a_block(c, a)
            rcopy(own, there, g_ss.at[A_MINUS, c], g_rs.at[A_MINUS, c], a_plus).start()
            rcopy(own, there, g_ss.at[A_PLUS, c], g_rs.at[A_PLUS, c], a_minus).start()
            there[...] = own[...]

        @pl.when(jnp.logical_and(t >= LAG_A, t < GATHERED + LAG_A))
        def _():
            even = lax.rem(t - LAG_A, 2) == 0
            c = gathered(t - LAG_A)
            blk = a_block(c, m4(a + jnp.where(even, 3, 1)))
            wait_recv(blk, g_rs.at[jnp.where(even, A_MINUS, A_PLUS), c])
            to = tuple(jnp.where(even, p, m) for p, m in zip(a_plus, a_minus))
            rcopy(blk, blk, g_ss.at[A_FAR, c], g_rs.at[A_FAR, c], to).start()

        @pl.when(jnp.logical_and(t >= LAG_C, t < GATHERED + LAG_C))
        def _():
            even = lax.rem(t - LAG_C, 2) == 0
            c = gathered(t - LAG_C)
            grp = b_group(c, m4(b + jnp.where(even, 3, 1)))
            wait_recv(grp, g_rs.at[jnp.where(even, B_MINUS, B_PLUS), c])
            to = tuple(jnp.where(even, p, m) for p, m in zip(b_plus, b_minus))
            rcopy(grp, grp, g_ss.at[B_FAR, c], g_rs.at[B_FAR, c], to).start()

        @pl.when(jnp.logical_and(t >= LAG_B, t < GATHERED + LAG_B))
        def _():
            even = lax.rem(t - LAG_B, 2) == 0
            c = gathered(t - LAG_B)
            wait_recv(a_block(c, m4(a + jnp.where(even, 1, 3))), g_rs.at[jnp.where(even, A_PLUS, A_MINUS), c])
            wait_recv(a_block(c, m4(a + 2)), g_rs.at[A_FAR, c])
            grp = b_group(c, b)
            rcopy(grp, grp, g_ss.at[B_MINUS, c], g_rs.at[B_MINUS, c], b_plus).start()
            rcopy(grp, grp, g_ss.at[B_PLUS, c], g_rs.at[B_PLUS, c], b_minus).start()

        @pl.when(jnp.logical_and(t >= LAG_D, t < GATHERED + LAG_D))
        def _():
            even = lax.rem(t - LAG_D, 2) == 0
            i = t - LAG_D
            c = gathered(i)
            wait_recv(b_group(c, m4(b + jnp.where(even, 1, 3))), g_rs.at[jnp.where(even, B_PLUS, B_MINUS), c])
            wait_recv(b_group(c, m4(b + 2)), g_rs.at[B_FAR, c])
            half = G.at[c, k]
            rcopy(half, half, g_ss.at[SIB, c], g_rs.at[SIB, c], sib).start()

            @pl.when(sum(jnp.where(i == at, 1, 0) for at in SHARED_AT) == 1)
            def _():
                rcopy(half, half, g_ss.at[HAND, c], g_rs.at[HAND, c], hand_to).start()

        for j, at in enumerate(HANDED_TICKS):

            @pl.when(t == at)
            def _():
                c = 2 * j + 1 - parity
                half = G.at[c, k]
                wait_recv(half, g_rs.at[HAND, c])
                rcopy(half, half, g_ss.at[SIB, c], g_rs.at[SIB, c], sib).start()

        @pl.when(t == TEXT_TICKS[0])
        def _():
            for i in (1, 2, 3):
                s = m4(x + i)
                wait_recv(tx_r.at[s], tx_rs.at[s])
            T[zl, k, zh, own_t, :] = gather_line(tx_r, line_f)
            blk = T.at[zl, k, zh, own_t, :]
            for i in (1, 2, 3):
                rcopy(blk, blk, ty_ss.at[i - 1], ty_rs.at[y], dev(x, m4(y + i), z, k)).start()

        @pl.when(t == TEXT_TICKS[1])
        def _():
            for i in (1, 2, 3):
                yy = m4(y + i)
                wait_recv(T.at[zl, k, zh, pl.ds(pl.multiple_of(yy * 16, 16), 16), :], ty_rs.at[yy])
            blk = text_ring(0)
            rcopy(blk, blk, tz_ss.at[0, 0], tz_rs.at[0, 0], z_plus).start()
            rcopy(blk, blk, tz_ss.at[1, 0], tz_rs.at[1, 0], z_minus).start()

        for hop in (1, 2):

            @pl.when(t == TEXT_TICKS[1 + hop])
            def _():
                low, high = text_ring(8 - hop), text_ring(hop)
                wait_recv(low, tz_rs.at[0, hop - 1])
                wait_recv(high, tz_rs.at[1, hop - 1])
                rcopy(low, low, tz_ss.at[0, hop], tz_rs.at[0, hop], z_plus).start()
                rcopy(high, high, tz_ss.at[1, hop], tz_rs.at[1, hop], z_minus).start()

        @pl.when(t == TEXT_TICKS[4])
        def _():
            low, high = text_ring(5), text_ring(3)
            wait_recv(low, tz_rs.at[0, 2])
            wait_recv(high, tz_rs.at[1, 2])

            @pl.when(k == 0)
            def _():
                rcopy(low, low, tz_ss.at[0, 3], tz_rs.at[0, 3], z_plus).start()

            @pl.when(k == 1)
            def _():
                rcopy(high, high, tz_ss.at[0, 3], tz_rs.at[0, 3], z_minus).start()

        @pl.when(t == TEXT_TICKS[5])
        def _():
            wait_recv(text_ring(4), tz_rs.at[0, 3])
            mine = T.at[:, k]
            rcopy(mine, mine, ts_ss.at[0], ts_rs.at[0], sib).start()

        @pl.when(t == TEXT_TICKS[5] + 1)
        def _():
            for zz in range(8):
                block = T[zz % 4, k, zz // 4, own_t, :].astype(F32)
                mine = jnp.zeros((4, D), F32)
                for s in range(4):
                    mine = mine + jnp.where(x == s, 1.0, 0.0) * block[4 * s:4 * s + 4, :]
                tcol[8 * zz:8 * zz + 4, :] = mine
                tcol[8 * zz + 4:8 * zz + 8, :] = jnp.zeros((4, D), F32)

        @pl.when(t == 0)
        def _():
            local[1].start()

        @pl.when(t == 1)
        def _():
            local[0].wait()

        @pl.when(t == 8)
        def _():
            local[2].start()
            local[3].start()

        @pl.when(jnp.logical_and(t >= 1, t <= PACK // TILE))
        def _():
            sl = pl.ds(pl.multiple_of((t - 1) * TILE, TILE), TILE)
            wide = xbuf[sl, :].astype(F32)
            center = jnp.mean(wide, axis=1, keepdims=True)
            off = wide - center
            spread = jnp.mean(off * off, axis=1, keepdims=True)
            normed[sl, :] = (off * lax.rsqrt(spread + EPSILON) * gain[...].reshape(1, D)).astype(BF16)
            acc[sl, :] = wide
            act[sl, :] = jnp.zeros((TILE, 2 * LANES), BF16)

        @pl.when(t == 7)
        def _():
            local[1].wait()
            head_of = lax.div(lax.broadcasted_iota(I32, (HEADS, D), 1), HEAD_DIM)
            own_head = head_of == lax.broadcasted_iota(I32, (HEADS, D), 0)
            block = jnp.where(own_head, jnp.broadcast_to(probe[...].astype(F32).reshape(1, D), (HEADS, D)), 0.0)
            keys = lax.dot_general(block.astype(BF16), kw[...], NT, preferred_element_type=F32)
            hk[...] = (keys / math.sqrt(HEAD_DIM)).astype(BF16)

            pos = lax.broadcasted_iota(I32, (LANES, 1), 0)
            slot = lax.rem(pos, 4)
            px = lax.rem(lax.div(pos, 4), 4)
            py = lax.rem(lax.div(pos, 16), 4)
            pk = lax.div(pos, 64)
            owner = lax.rem(16 * zh + 4 * py + px + 32 - 8 * slot, 32)
            ids = 4 * ((2 * zl + pk) * 32 + owner) + slot
            hot = lax.broadcasted_iota(I32, (LANES, TEXTS), 1) == ids
            hot = jnp.where(hot, 1.0, 0.0).astype(BF16)
            lab = labels[...]
            high = lax.div(lab, 16)
            low = lab - 16 * high
            pair = jnp.where(
                lax.broadcasted_iota(I32, (16, TEXTS), 0) == 0,
                jnp.broadcast_to(high, (16, TEXTS)),
                jnp.broadcast_to(low, (16, TEXTS)),
            ).astype(F32).astype(BF16)
            rows = lax.dot_general(pair, hot, NT, preferred_element_type=F32)
            ilab[...] = jnp.broadcast_to(16.0 * rows[0:1, :] + rows[1:2, :], (8, LANES))
            tpos = lax.broadcasted_iota(I32, (64, 1), 0)
            tz = lax.div(tpos, 8)
            tid = m4(tz) * 256 + k * 128 + lax.div(tz, 4) * 64 + y * 16 + x * 4 + m4(tpos)
            tlab[...] = jnp.broadcast_to(label_cols(tid), (64, LANES))

        @pl.when(jnp.logical_and(t >= LAG_E, t < GATHERED + LAG_E))
        def _():
            first = t - LAG_E + sum(jnp.where(t > v, 1, 0) for v in TWO_AT)
            many = 1 + sum(jnp.where(t == v, 1, 0) for v in TWO_AT)

            def one(n, carry):
                u = first + n
                c = chunk_at(u)
                before = chunk_at(jnp.maximum(u - 1, 0))
                wait_recv(G.at[c, 1 - k], g_rs.at[SIB, c])
                w1, w2 = w1_of(c), w2_of(before)
                for r in range(PACK // TILE):
                    sl = slice(r * TILE, (r + 1) * TILE)
                    old = act[sl, :]
                    hidden = jnp.dot(normed[sl, :], w1, preferred_element_type=F32)
                    acc[sl, :] += lax.dot_general(old, w2, NT, preferred_element_type=F32)
                    act[sl, :] = gelu(hidden)
                return carry

            lax.fori_loop(0, many, one, 0)

        return carry

    lax.fori_loop(0, TICKS, tick, 0)

    states = normed
    w2 = w2_of(chunk_at(CHUNKS - 1))
    score_tiles = []
    for r in range(PACK // TILE):
        sl = slice(r * TILE, (r + 1) * TILE)
        mixed = lax.dot_general(act[sl, :], w2, NT, preferred_element_type=F32)
        low = (acc[sl, :] + mixed).astype(BF16)
        states[sl, :] = low
        score_tiles.append(lax.dot_general(hk[...], low, NT, preferred_element_type=F32))
    scores = jnp.concatenate(score_tiles, axis=1)
    row = lax.broadcasted_iota(I32, (HEADS, PACK), 1)
    all_weights = []
    for j in range(4):
        if j > 0:
            wait_recv(cn_r.at[j], cn_rs.at[j])
        first = offsets[j]
        count = cn_r[j][0:1, 0:1]
        member = jnp.logical_and(row >= first, row < first + count)
        masked = jnp.where(member, scores, -1e30)
        highest = jnp.max(masked, axis=1, keepdims=True)
        raised = jnp.exp(masked - highest)
        all_weights.append(raised / jnp.sum(raised, axis=1, keepdims=True))
    weights = jnp.concatenate(all_weights, axis=0).astype(BF16)
    mean_states = jnp.dot(weights, states[...], preferred_element_type=F32).astype(BF16)
    local[2].wait()
    local[3].wait()
    full = jnp.dot(mean_states, vw[...], preferred_element_type=F32)
    head_of = lax.div(lax.broadcasted_iota(I32, (HEADS, D), 1), HEAD_DIM)
    own_head = head_of == lax.broadcasted_iota(I32, (HEADS, D), 0)
    values = [
        jnp.sum(jnp.where(own_head, full[HEADS * j:HEADS * (j + 1), :], 0.0), axis=0, keepdims=True)
        for j in range(4)
    ]
    mixed = jnp.concatenate(values + [jnp.zeros((12, D), F32)], axis=0).astype(BF16)
    pooled = jnp.dot(mixed, ow[...], preferred_element_type=F32)[0:8, :]
    image_inv = lax.rsqrt(jnp.sum(pooled * pooled, axis=1, keepdims=True) + EPSILON)
    image_unit = pooled * image_inv
    image_low = jnp.concatenate([image_unit, jnp.zeros((8, D), F32)], axis=0).astype(BF16)
    ix_s[...] = image_unit[0:4].astype(BF16)

    def send_images(i, carry):
        q = lax.rem(place + i, PLANE)
        rcopy(ix_s, ix_r.at[place], ix_ss.at[i], ix_rs.at[place], in_plane(q)).start()
        return carry

    lax.fori_loop(1, PLANE, send_images, 0)
    ix_r[place] = ix_s[...]

    mult = scale[0]
    shift = bias[0]

    wait_recv(T.at[:, 1 - k], ts_rs.at[0])
    texts = T[...].reshape(TEXTS, D)
    own_logits = mult * lax.dot_general(image_low, texts, NT, preferred_element_type=F32) + shift
    slot = lax.broadcasted_iota(I32, (16, 1), 0)
    slot4 = m4(slot)
    own_ids = 4 * (g * 32 + lax.rem(d + 32 - 8 * slot4, 32)) + slot4
    own_lab = label_cols(own_ids)
    sign = jnp.where(own_lab == labels[...].astype(F32), 1.0, -1.0)
    signed = sign * own_logits
    terms = jnp.log1p(jnp.exp(-jnp.abs(signed))) + jnp.maximum(-signed, 0.0)
    terms = jnp.where(slot < 4, terms, 0.0)
    part_loss = jnp.sum(jnp.sum(terms, axis=1, keepdims=True), axis=0, keepdims=True)
    ls_s[0] = jnp.broadcast_to(part_loss, (8, LANES))
    for i in range(3):
        rcopy(ls_s.at[0], ls_r.at[0, x], l1_ss.at[i], l1_rs.at[x], xs[i]).start()
    ls_r[0, x] = ls_s[0]

    others = [(m4(y + i), c_) for i in (1, 2, 3) for c_ in (0, 1)]
    to_plane = [dev(x, yy, z, c_) for yy, c_ in others] + [sib]

    own_slope = (mult * -sign * jax.nn.sigmoid(-signed)).astype(BF16)
    image_push = jnp.dot(own_slope, texts, preferred_element_type=F32)[0:8, :]
    image_grad = (
        image_push - image_unit * jnp.sum(image_unit * image_push, axis=1, keepdims=True)
    ) * image_inv
    for j in range(4):
        ig_s[j] = image_grad[j:j + 1, :]
    for j in (1, 2, 3):
        rcopy(ig_s.at[j], ig_r.at[j], ig_ss.at[j], ig_rs.at[j], group_dev[4 - j]).start()
    ig_r[0] = ig_s[0]

    for i in (1, 2, 3):
        s = m4(x + i)
        wait_recv(ls_r.at[0, s], l1_rs.at[s])
    ls_s[1] = ls_r[0, 0] + ls_r[0, 1] + ls_r[0, 2] + ls_r[0, 3]
    me8 = k * 4 + y
    for i, to in enumerate(to_plane):
        rcopy(ls_s.at[1], ls_r.at[1, me8], l2_ss.at[i], l2_rs.at[me8], to).start()
    ls_r[1, me8] = ls_s[1]

    def take_images(i, carry):
        q = lax.rem(place + i, PLANE)
        wait_recv(ix_r.at[q], ix_rs.at[q])
        return carry

    lax.fori_loop(1, PLANE, take_images, 0)
    for q in range(PLANE):
        plane_f[4 * q:4 * q + 4, :] = ix_r[q].astype(F32)
    plane = plane_f[...].astype(BF16)
    plane_logits = mult * lax.dot_general(
        tcol[...].astype(BF16), plane, NT, preferred_element_type=F32
    ) + shift
    plane_sign = jnp.where(tlab[...] == ilab[0:1, :], 1.0, -1.0)
    plane_slope = (mult * -plane_sign * jax.nn.sigmoid(-plane_sign * plane_logits)).astype(BF16)
    push = jnp.dot(plane_slope, plane, preferred_element_type=F32)
    for zz in range(8):
        ps_s[zz] = push[8 * zz:8 * zz + 4, :]
    for i in range(7):
        to_z = m8(z + i + 1)
        rcopy(ps_s.at[to_z], ps_r.at[z], ps_ss.at[i], ps_rs.at[z], zs[i]).start()
    ps_r[z] = ps_s[z]

    for yy, c_ in others + [(y, 1 - k)]:
        wait_recv(ls_r.at[1, c_ * 4 + yy], l2_rs.at[c_ * 4 + yy])
    total = ls_r[1, 0]
    for i in range(1, 8):
        total = total + ls_r[1, i]
    ls_s[2] = total
    for i in range(7):
        rcopy(ls_s.at[2], ls_r.at[2, z], l3_ss.at[i], l3_rs.at[z], zs[i]).start()
    ls_r[2, z] = ls_s[2]

    for j in (1, 2, 3):
        wait_recv(ig_r.at[j], ig_rs.at[j])
    for j in range(4):
        grads_out[j:j + 1, :] = ig_r[j]

    def drain(c, carry):
        own = own_blocks.at[c]

        @pl.when(edge)
        def _():
            wait_send(own, g_ss.at[Z, c])

        wait_send(G.at[c, k], g_ss.at[SIB, c])

        @pl.when(c < GATHERED)
        def _():
            e = gathered(c)
            for kind in (A_MINUS, A_PLUS, A_FAR):
                wait_send(own, g_ss.at[kind, e])
            for kind in (B_MINUS, B_PLUS, B_FAR):
                wait_send(b_group(e, b), g_ss.at[kind, e])

            @pl.when(c < SHARED)
            def _():
                wait_send(G.at[e, k], g_ss.at[HAND, 2 * c + parity])

        return carry

    lax.fori_loop(0, CHUNKS, drain, 0)

    @pl.when(source)
    def _():
        for p in range(len(PIECES)):
            for i in range(3):
                wait_send(a2a_s.at[0, :, piece_lanes(p)], x_ss.at[p, i])

    for i in range(3):
        wait_send(tx_s, tx_ss.at[i])
        wait_send(T.at[zl, k, zh, own_t, :], ty_ss.at[i])
        wait_send(ls_s.at[0], l1_ss.at[i])
        wait_send(cn_s.at[i + 1], cn_ss.at[i + 1])
        wait_send(ig_s.at[i + 1], ig_ss.at[i + 1])
        wait_send(text_ring(0), tz_ss.at[0, i])
        wait_send(text_ring(0), tz_ss.at[1, i])
    wait_send(text_ring(0), tz_ss.at[0, 3])
    wait_send(T.at[:, k], ts_ss.at[0])
    for i in range(1, 8):
        zz = m8(z + i)
        wait_recv(ps_r.at[zz], ps_rs.at[zz])
    text_push = ps_r[0]
    for i in range(1, 8):
        text_push = text_push + ps_r[i]
    grads_out[4:8, :] = (
        text_push - text_unit * jnp.sum(text_unit * text_push, axis=1, keepdims=True)
    ) * text_inv

    for i in range(1, 8):
        zz = m8(z + i)
        wait_recv(ls_r.at[2, zz], l3_rs.at[zz])
    total = ls_r[2, 0]
    for i in range(1, 8):
        total = total + ls_r[2, i]
    loss_out[...] = total[0:1, 0:1] / float(TEXTS)

    def sent_images(i, carry):
        wait_send(ix_s, ix_ss.at[i])
        return carry

    lax.fori_loop(1, PLANE, sent_images, 0)
    for i in range(7):
        wait_send(ls_s.at[1], l2_ss.at[i])
        wait_send(ps_s.at[0], ps_ss.at[i])
        wait_send(ls_s.at[2], l3_ss.at[i])


def per_device(
    patches, patch_counts, pack_offsets, norm_gain, mlp_in, mlp_out, probe_query, key_weight,
    value_weight, out_weight, text_embed, pair_label, logit_scale, logit_bias,
):
    vmem = pl.BlockSpec(memory_space=pltpu.VMEM)
    smem = pl.BlockSpec(memory_space=pltpu.SMEM)
    anywhere = pl.BlockSpec(memory_space=pl.ANY)
    dma = pltpu.SemaphoreType.DMA
    loss, grads = pl.pallas_call(
        kernel,
        out_shape=(
            jax.ShapeDtypeStruct((1, 1), F32),
            jax.ShapeDtypeStruct((8, D), F32),
        ),
        in_specs=[
            anywhere, smem, smem, vmem, anywhere, anywhere, vmem, anywhere, anywhere, anywhere, vmem, vmem, smem, smem,
        ],
        out_specs=(vmem, vmem),
        scratch_shapes=[
            pltpu.VMEM((PACK, D), BF16),
            pltpu.VMEM((PACK, D), BF16),
            pltpu.VMEM((PACK, D), F32),
            pltpu.VMEM((PACK, 2 * LANES), BF16),
            pltpu.VMEM((CHUNKS, 2, 4, GROUP, LANES), BF16),
            pltpu.VMEM((CHUNKS, BLOCK, LANES), BF16),
            pltpu.VMEM((SHARD, FF), BF16),
            pltpu.VMEM((SHARD, FF), BF16),
            pltpu.VMEM((4, SLOT_ROWS, HALF), BF16),
            pltpu.VMEM((4, SLOT_ROWS, HALF), BF16),
            pltpu.VMEM((BLOCK, HALF), F32),
            pltpu.VMEM((4, 2, 2, 64, D), BF16),
            pltpu.VMEM((16, D), F32),
            pltpu.VMEM((16, D), BF16),
            pltpu.VMEM((4, 16, D), BF16),
            pltpu.VMEM((4, D), BF16),
            pltpu.VMEM((PLANE, 4, D), BF16),
            pltpu.VMEM((LANES, D), F32),
            pltpu.VMEM((64, D), F32),
            pltpu.VMEM((8, 4, D), F32),
            pltpu.VMEM((8, 4, D), F32),
            pltpu.VMEM((4, 1, D), F32),
            pltpu.VMEM((4, 1, D), F32),
            pltpu.VMEM((4, 8, LANES), I32),
            pltpu.VMEM((4, 8, LANES), I32),
            pltpu.VMEM((HEADS, D), BF16),
            pltpu.VMEM((D, D), BF16),
            pltpu.VMEM((D, D), BF16),
            pltpu.VMEM((D, D), BF16),
            pltpu.VMEM((8, LANES), F32),
            pltpu.VMEM((64, LANES), F32),
            pltpu.VMEM((3, 8, LANES), F32),
            pltpu.VMEM((3, 8, 8, LANES), F32),
            dma((7,)),
            dma((9, CHUNKS)), dma((9, CHUNKS)),
            dma((3, 3)), dma((3, 4)),
            dma((3,)), dma((4,)),
            dma((3,)), dma((4,)),
            dma((2, 4)), dma((2, 4)),
            dma((1,)), dma((1,)),
            dma((PLANE,)), dma((PLANE,)),
            dma((7,)), dma((8,)),
            dma((4,)), dma((4,)),
            dma((4,)), dma((4,)),
            dma((3,)), dma((4,)),
            dma((7,)), dma((8,)),
            dma((7,)), dma((8,)),
        ],
        compiler_params=pltpu.CompilerParams(
            collective_id=0, has_side_effects=True, vmem_limit_bytes=62 * 2**20
        ),
        cost_estimate=pl.CostEstimate(
            flops=4 * PACK * D * FF, bytes_accessed=12 * 2**20, transcendentals=PACK * FF
        ),
        name="pooled_loss",
    )(
        patches, patch_counts, pack_offsets, norm_gain, mlp_in, mlp_out.T,
        probe_query, key_weight, value_weight, out_weight, text_embed,
        pair_label.reshape(1, TEXTS), logit_scale, logit_bias,
    )
    return loss.reshape(()), grads[0:4], grads[4:8]


def solution(mesh):
    placed = (
        P(("grp", "dp"), None), P(("grp", "dp")), P(("grp", "dp")), P(), P("dp", None), P(None, "dp"),
        P(), P(), P(), P(), P(("grp", "dp"), None), P(), P(), P(),
    )
    return jax.shard_map(
        per_device,
        mesh=mesh,
        in_specs=placed,
        out_specs=(P(), P(("grp", "dp"), None), P(("grp", "dp"), None)),
        check_vma=False,
    )
```

```python
import math

import jax
import jax.numpy as jnp
from jax import lax
from jax.experimental import pallas as pl
from jax.experimental.pallas import tpu as pltpu
from jax.sharding import PartitionSpec as P

MESH = pl.DeviceIdType.MESH
F32 = jnp.float32
BF16 = jnp.bfloat16
I32 = jnp.int32

EPSILON = 1e-06
D = 1152
FF = 4304
HEAD_DIM = 72
HEADS = 16
PACK = 1024
TEXTS = 1024
SHARD = 36
SLOT_ROWS = 36
LANES = 128
CHUNKS = 17
HALF = CHUNKS * LANES
BLOCK = 4 * SHARD
GROUP = 4 * BLOCK
TILE = 256
PLANE = 32

LAG_A, LAG_B, LAG_C, LAG_D, LAG_E = 3, 6, 9, 12, 13

SHARED = 3
SHARED_AT = (0, 3, 7)
GATHERED = CHUNKS - SHARED
TICKS = GATHERED + LAG_E
HANDED_TICKS = (17, 20, 23)
TWO_AT = (18, 21, 24)
TEXT_TICKS = (5, 9, 13, 17, 21, 24)
PIECES = ((0, 4), (4, 8), (8, 17))
PIECE_TICKS = (1, 2)

Z, A_MINUS, A_PLUS, A_FAR, B_MINUS, B_PLUS, B_FAR, SIB, HAND = range(9)

NT = (((1,), (1,)), ((), ()))


def gelu(hidden):
    c1 = math.sqrt(2.0 / math.pi)
    c2 = c1 * 0.044715
    inner = hidden * (c1 + c2 * (hidden * hidden))
    half = 0.5 * hidden
    return (half + half * jnp.tanh(inner)).astype(BF16)


def kernel(
    patches, counts, offsets, gain, win_hbm, woutt_hbm, probe, key_w, value_w, out_w, text, labels, scale, bias,
    loss_out, grads_out,
    xbuf, normed, acc, act, G, own_blocks, win, woutt, a2a_s, a2a_r, compact, T, line_f, tx_s, tx_r, ix_s, ix_r, plane_f, tcol,
    ps_s, ps_r, ig_s, ig_r, cn_s, cn_r, hk, kw, vw, ow, ilab, tlab, ls_s, ls_r,
    loc_sem, g_ss, g_rs, x_ss, x_rs, tx_ss, tx_rs, ty_ss, ty_rs, tz_ss, tz_rs, ts_ss, ts_rs,
    ix_ss, ix_rs, ps_ss, ps_rs, ig_ss, ig_rs, cn_ss, cn_rs,
    l1_ss, l1_rs, l2_ss, l2_rs, l3_ss, l3_rs,
):
    g = lax.axis_index("grp")
    d = lax.axis_index("dp")
    k = lax.rem(g, 2)
    zl = lax.div(g, 2)
    x = lax.rem(d, 4)
    y = lax.rem(lax.div(d, 4), 4)
    zh = lax.div(d, 16)
    z = zh * 4 + zl

    def dev(x_, y_, z_, k_):
        return (lax.rem(z_, 4) * 2 + k_, lax.div(z_, 4) * 16 + y_ * 4 + x_)

    def m4(v):
        return lax.rem(v, 4)

    def m8(v):
        return lax.rem(v, 8)

    sib = dev(x, y, z, 1 - k)
    xs = [dev(m4(x + i), y, z, k) for i in (1, 2, 3)]
    zs = [dev(x, y, m8(z + i), k) for i in range(1, 8)]
    group_dev = [(g, lax.rem(d + 8 * j, 32)) for j in range(4)]

    def rcopy(src, dst, ss, rs, to):
        return pltpu.make_async_remote_copy(
            src_ref=src, dst_ref=dst, send_sem=ss, recv_sem=rs, device_id=to, device_id_type=MESH
        )

    def wait_recv(ref, rs):
        rcopy(ref, ref, loc_sem.at[0], rs, sib).wait_recv()

    def wait_send(ref, ss):
        rcopy(ref, ref, ss, loc_sem.at[0], sib).wait_send()

    shards = [
        pltpu.make_async_copy(win_hbm, win, loc_sem.at[5]),
        pltpu.make_async_copy(woutt_hbm, woutt, loc_sem.at[6]),
    ]
    for cp in shards:
        cp.start()
    local = [
        pltpu.make_async_copy(patches, xbuf, loc_sem.at[1]),
        pltpu.make_async_copy(key_w, kw, loc_sem.at[2]),
        pltpu.make_async_copy(value_w, vw, loc_sem.at[3]),
        pltpu.make_async_copy(out_w, ow, loc_sem.at[4]),
    ]

    barrier = pltpu.get_barrier_semaphore()
    place = k * 16 + y * 4 + x

    def in_plane(q):
        return dev(m4(q), m4(lax.div(q, 4)), z, lax.div(q, 16))

    def greet(i, carry):
        q = lax.rem(place + i, PLANE)
        pl.semaphore_signal(barrier, inc=1, device_id=in_plane(q), device_id_type=MESH)
        return carry

    lax.fori_loop(1, PLANE, greet, 0)
    partners = list(zs) + [dev(x, m4(y + 2), m8(z + 4), k)]
    for p in partners:
        pl.semaphore_signal(barrier, inc=1, device_id=p, device_id_type=MESH)

    for cp in shards:
        cp.wait()
    local[0].start()

    source = k == zh

    @pl.when(source)
    def _():
        for part in range(4):
            shard = win if part < 2 else woutt
            if part % 2 == 0:
                a2a_s[part, 0:SHARD, :] = shard[:, 0:HALF]
            else:
                a2a_s[part, :, HALF - LANES:HALF] = jnp.zeros((SLOT_ROWS, LANES), BF16)
                a2a_s[part, 0:SHARD, 0:FF - HALF] = shard[:, HALF:FF]

    text_wide = text[...].astype(F32)
    text_inv = lax.rsqrt(jnp.sum(text_wide * text_wide, axis=1, keepdims=True) + EPSILON)
    text_unit = text_wide * text_inv
    tx_s[...] = jnp.zeros((16, D), BF16)
    tx_s[0:4, :] = text_unit.astype(BF16)
    for j in range(4):
        cn_s[j] = jnp.full((8, LANES), counts[j], I32)

    pl.semaphore_wait(barrier, PLANE - 1 + len(partners))

    def piece_lanes(p):
        return slice(PIECES[p][0] * LANES, PIECES[p][1] * LANES)

    @pl.when(source)
    def _():
        for p in range(len(PIECES)):
            at = piece_lanes(p)
            for i in range(3):
                to_x = m4(x + i + 1)
                rcopy(
                    a2a_s.at[to_x, :, at], a2a_r.at[x, :, at], x_ss.at[p, i], x_rs.at[p, x], xs[i]
                ).start()
        a2a_r[x] = a2a_s[x]

    for i in range(3):
        rcopy(tx_s, tx_r.at[x], tx_ss.at[i], tx_rs.at[x], xs[i]).start()
    tx_r[x] = tx_s[...]
    for j in (1, 2, 3):
        rcopy(cn_s.at[j], cn_r.at[j], cn_ss.at[j], cn_rs.at[j], group_dev[j]).start()
    cn_r[0] = cn_s[0]

    a = jnp.where(k == 0, y, x)
    b = jnp.where(k == 0, x, y)

    def along(axis_is_a, step):
        move_y = jnp.where(k == 0, 1, 0) if axis_is_a else jnp.where(k == 0, 0, 1)
        return dev(m4(x + (1 - move_y) * step), m4(y + move_y * step), z, k)

    a_plus, a_minus = along(True, 1), along(True, 3)
    b_plus, b_minus = along(False, 1), along(False, 3)

    def a_block(c, at):
        return G.at[c, k, b, pl.ds(pl.multiple_of(at * BLOCK, 16), BLOCK), :]

    def b_group(c, at):
        return G.at[c, k, at]

    def take_piece(p):
        at = piece_lanes(p)
        for i in (1, 2, 3):
            s = m4(x + i)
            wait_recv(a2a_r.at[s, :, at], x_rs.at[p, s])
        for s in range(4):
            compact[s * SHARD:(s + 1) * SHARD, at] = a2a_r[s, 0:SHARD, at].astype(F32)
        for c in range(*PIECES[p]):
            own_blocks[c] = compact[:, c * LANES:(c + 1) * LANES].astype(BF16)

    @pl.when(source)
    def _():
        take_piece(0)

    edge = jnp.logical_or(zl == 0, zl == 3)
    outward = jnp.where(zl == 3, 1, 7)
    z_to = dev(x, y, m8(z + jnp.where(source, outward, 8 - outward)), k)

    def t_block(zl_, k_, zh_):
        return T.at[zl_, k_, zh_]

    def z_parts(step):
        zz = m8(z + step)
        return m4(zz), lax.div(zz, 4)

    def text_ring(step):
        zl_, zh_ = z_parts(step)
        return T.at[zl_, k, zh_]

    z_plus, z_minus = zs[0], zs[6]
    own_t = pl.ds(pl.multiple_of(y * 16, 16), 16)

    def gather_line(received, wide):
        for s in range(4):
            wide[4 * s:4 * s + 4, :] = received[s, 0:4, :].astype(F32)
        return wide[...].astype(BF16)

    def label_cols(ids):
        rows = ids.shape[0]
        lanes = lax.broadcasted_iota(I32, (rows, TEXTS), 1)
        row = jnp.broadcast_to(labels[...].astype(F32), (rows, TEXTS))
        return jnp.sum(jnp.where(lanes == ids, row, 0.0), axis=1, keepdims=True)

    parity = lax.rem(zl, 2)
    hand_to = tuple(jnp.where(k == 0, p, m) for p, m in zip(z_plus, z_minus))

    def gathered(i):
        c = i + 2 * SHARED - sum(jnp.where(i > at, 1, 0) for at in SHARED_AT)
        for j, at in enumerate(SHARED_AT):
            c = jnp.where(i == at, 2 * j + parity, c)
        return c

    def part(c, p):
        pieces = [G[c, 0, p]]
        for yy in range(4):
            pieces.append(G[c, 1, yy, p * BLOCK:(p + 1) * BLOCK, :])
        return jnp.concatenate(pieces, axis=0)

    def w1_of(c):
        return jnp.concatenate([part(c, 0), part(c, 1)], axis=1)

    def w2_of(c):
        return jnp.concatenate([part(c, 2), part(c, 3)], axis=1)

    def chunk_at(u):
        at = [tick_ - LAG_E + j + 1 for j, tick_ in enumerate(TWO_AT)]
        later = [jnp.where(u > v, 1, 0) for v in at]
        c = gathered(u - sum(later))
        for j, v in enumerate(at):
            c = jnp.where(u == v, 2 * j + 1 - parity, c)
        return c

    def tick(t, carry):
        for p, at in enumerate(PIECE_TICKS):

            @pl.when(jnp.logical_and(source, t == at))
            def _():
                take_piece(p + 1)

        for q in range(4):

            @pl.when(4 * t + q < CHUNKS)
            def _():
                c = 4 * t + q
                own = own_blocks.at[c]

                @pl.when(jnp.logical_not(source))
                def _():
                    wait_recv(own, g_rs.at[Z, c])

                @pl.when(edge)
                def _():
                    rcopy(own, own, g_ss.at[Z, c], g_rs.at[Z, c], z_to).start()

        @pl.when(t < GATHERED)
        def _():
            c = gathered(t)
            own = own_blocks.at[c]
            there = a_block(c, a)
            rcopy(own, there, g_ss.at[A_MINUS, c], g_rs.at[A_MINUS, c], a_plus).start()
            rcopy(own, there, g_ss.at[A_PLUS, c], g_rs.at[A_PLUS, c], a_minus).start()
            there[...] = own[...]

        @pl.when(jnp.logical_and(t >= LAG_A, t < GATHERED + LAG_A))
        def _():
            even = lax.rem(t - LAG_A, 2) == 0
            c = gathered(t - LAG_A)
            blk = a_block(c, m4(a + jnp.where(even, 3, 1)))
            wait_recv(blk, g_rs.at[jnp.where(even, A_MINUS, A_PLUS), c])
            to = tuple(jnp.where(even, p, m) for p, m in zip(a_plus, a_minus))
            rcopy(blk, blk, g_ss.at[A_FAR, c], g_rs.at[A_FAR, c], to).start()

        @pl.when(jnp.logical_and(t >= LAG_C, t < GATHERED + LAG_C))
        def _():
            even = lax.rem(t - LAG_C, 2) == 0
            c = gathered(t - LAG_C)
            grp = b_group(c, m4(b + jnp.where(even, 3, 1)))
            wait_recv(grp, g_rs.at[jnp.where(even, B_MINUS, B_PLUS), c])
            to = tuple(jnp.where(even, p, m) for p, m in zip(b_plus, b_minus))
            rcopy(grp, grp, g_ss.at[B_FAR, c], g_rs.at[B_FAR, c], to).start()

        @pl.when(jnp.logical_and(t >= LAG_B, t < GATHERED + LAG_B))
        def _():
            even = lax.rem(t - LAG_B, 2) == 0
            c = gathered(t - LAG_B)
            wait_recv(a_block(c, m4(a + jnp.where(even, 1, 3))), g_rs.at[jnp.where(even, A_PLUS, A_MINUS), c])
            wait_recv(a_block(c, m4(a + 2)), g_rs.at[A_FAR, c])
            grp = b_group(c, b)
            rcopy(grp, grp, g_ss.at[B_MINUS, c], g_rs.at[B_MINUS, c], b_plus).start()
            rcopy(grp, grp, g_ss.at[B_PLUS, c], g_rs.at[B_PLUS, c], b_minus).start()

        @pl.when(jnp.logical_and(t >= LAG_D, t < GATHERED + LAG_D))
        def _():
            even = lax.rem(t - LAG_D, 2) == 0
            i = t - LAG_D
            c = gathered(i)
            wait_recv(b_group(c, m4(b + jnp.where(even, 1, 3))), g_rs.at[jnp.where(even, B_PLUS, B_MINUS), c])
            wait_recv(b_group(c, m4(b + 2)), g_rs.at[B_FAR, c])
            half = G.at[c, k]
            rcopy(half, half, g_ss.at[SIB, c], g_rs.at[SIB, c], sib).start()

            @pl.when(sum(jnp.where(i == at, 1, 0) for at in SHARED_AT) == 1)
            def _():
                rcopy(half, half, g_ss.at[HAND, c], g_rs.at[HAND, c], hand_to).start()

        for j, at in enumerate(HANDED_TICKS):

            @pl.when(t == at)
            def _():
                c = 2 * j + 1 - parity
                half = G.at[c, k]
                wait_recv(half, g_rs.at[HAND, c])
                rcopy(half, half, g_ss.at[SIB, c], g_rs.at[SIB, c], sib).start()

        @pl.when(t == TEXT_TICKS[0])
        def _():
            for i in (1, 2, 3):
                s = m4(x + i)
                wait_recv(tx_r.at[s], tx_rs.at[s])
            T[zl, k, zh, own_t, :] = gather_line(tx_r, line_f)
            blk = T.at[zl, k, zh, own_t, :]
            for i in (1, 2, 3):
                rcopy(blk, blk, ty_ss.at[i - 1], ty_rs.at[y], dev(x, m4(y + i), z, k)).start()

        @pl.when(t == TEXT_TICKS[1])
        def _():
            for i in (1, 2, 3):
                yy = m4(y + i)
                wait_recv(T.at[zl, k, zh, pl.ds(pl.multiple_of(yy * 16, 16), 16), :], ty_rs.at[yy])
            blk = text_ring(0)
            rcopy(blk, blk, tz_ss.at[0, 0], tz_rs.at[0, 0], z_plus).start()
            rcopy(blk, blk, tz_ss.at[1, 0], tz_rs.at[1, 0], z_minus).start()

        for hop in (1, 2):

            @pl.when(t == TEXT_TICKS[1 + hop])
            def _():
                low, high = text_ring(8 - hop), text_ring(hop)
                wait_recv(low, tz_rs.at[0, hop - 1])
                wait_recv(high, tz_rs.at[1, hop - 1])
                rcopy(low, low, tz_ss.at[0, hop], tz_rs.at[0, hop], z_plus).start()
                rcopy(high, high, tz_ss.at[1, hop], tz_rs.at[1, hop], z_minus).start()

        @pl.when(t == TEXT_TICKS[4])
        def _():
            low, high = text_ring(5), text_ring(3)
            wait_recv(low, tz_rs.at[0, 2])
            wait_recv(high, tz_rs.at[1, 2])

            @pl.when(k == 0)
            def _():
                rcopy(low, low, tz_ss.at[0, 3], tz_rs.at[0, 3], z_plus).start()

            @pl.when(k == 1)
            def _():
                rcopy(high, high, tz_ss.at[0, 3], tz_rs.at[0, 3], z_minus).start()

        @pl.when(t == TEXT_TICKS[5])
        def _():
            wait_recv(text_ring(4), tz_rs.at[0, 3])
            mine = T.at[:, k]
            rcopy(mine, mine, ts_ss.at[0], ts_rs.at[0], sib).start()

        @pl.when(t == TEXT_TICKS[5] + 1)
        def _():
            for zz in range(8):
                block = T[zz % 4, k, zz // 4, own_t, :].astype(F32)
                mine = jnp.zeros((4, D), F32)
                for s in range(4):
                    mine = mine + jnp.where(x == s, 1.0, 0.0) * block[4 * s:4 * s + 4, :]
                tcol[8 * zz:8 * zz + 4, :] = mine
                tcol[8 * zz + 4:8 * zz + 8, :] = jnp.zeros((4, D), F32)

        @pl.when(t == 0)
        def _():
            local[1].start()

        @pl.when(t == 1)
        def _():
            local[0].wait()

        @pl.when(t == 8)
        def _():
            local[2].start()
            local[3].start()

        @pl.when(jnp.logical_and(t >= 1, t <= PACK // TILE))
        def _():
            sl = pl.ds(pl.multiple_of((t - 1) * TILE, TILE), TILE)
            wide = xbuf[sl, :].astype(F32)
            center = jnp.mean(wide, axis=1, keepdims=True)
            off = wide - center
            spread = jnp.mean(off * off, axis=1, keepdims=True)
            normed[sl, :] = (off * lax.rsqrt(spread + EPSILON) * gain[...].reshape(1, D)).astype(BF16)
            acc[sl, :] = wide
            act[sl, :] = jnp.zeros((TILE, 2 * LANES), BF16)

        @pl.when(t == 7)
        def _():
            local[1].wait()
            head_of = lax.div(lax.broadcasted_iota(I32, (HEADS, D), 1), HEAD_DIM)
            own_head = head_of == lax.broadcasted_iota(I32, (HEADS, D), 0)
            block = jnp.where(own_head, jnp.broadcast_to(probe[...].astype(F32).reshape(1, D), (HEADS, D)), 0.0)
            keys = lax.dot_general(block.astype(BF16), kw[...], NT, preferred_element_type=F32)
            hk[...] = (keys / math.sqrt(HEAD_DIM)).astype(BF16)

            pos = lax.broadcasted_iota(I32, (LANES, 1), 0)
            slot = lax.rem(pos, 4)
            px = lax.rem(lax.div(pos, 4), 4)
            py = lax.rem(lax.div(pos, 16), 4)
            pk = lax.div(pos, 64)
            owner = lax.rem(16 * zh + 4 * py + px + 32 - 8 * slot, 32)
            ids = 4 * ((2 * zl + pk) * 32 + owner) + slot
            hot = lax.broadcasted_iota(I32, (LANES, TEXTS), 1) == ids
            hot = jnp.where(hot, 1.0, 0.0).astype(BF16)
            lab = labels[...]
            high = lax.div(lab, 16)
            low = lab - 16 * high
            pair = jnp.where(
                lax.broadcasted_iota(I32, (16, TEXTS), 0) == 0,
                jnp.broadcast_to(high, (16, TEXTS)),
                jnp.broadcast_to(low, (16, TEXTS)),
            ).astype(F32).astype(BF16)
            rows = lax.dot_general(pair, hot, NT, preferred_element_type=F32)
            ilab[...] = jnp.broadcast_to(16.0 * rows[0:1, :] + rows[1:2, :], (8, LANES))
            tpos = lax.broadcasted_iota(I32, (64, 1), 0)
            tz = lax.div(tpos, 8)
            tid = m4(tz) * 256 + k * 128 + lax.div(tz, 4) * 64 + y * 16 + x * 4 + m4(tpos)
            tlab[...] = jnp.broadcast_to(label_cols(tid), (64, LANES))

        @pl.when(jnp.logical_and(t >= LAG_E, t < GATHERED + LAG_E))
        def _():
            first = t - LAG_E + sum(jnp.where(t > v, 1, 0) for v in TWO_AT)
            many = 1 + sum(jnp.where(t == v, 1, 0) for v in TWO_AT)

            def one(n, carry):
                u = first + n
                c = chunk_at(u)
                before = chunk_at(jnp.maximum(u - 1, 0))
                wait_recv(G.at[c, 1 - k], g_rs.at[SIB, c])
                w1, w2 = w1_of(c), w2_of(before)
                for r in range(PACK // TILE):
                    sl = slice(r * TILE, (r + 1) * TILE)
                    old = act[sl, :]
                    hidden = jnp.dot(normed[sl, :], w1, preferred_element_type=F32)
                    acc[sl, :] += lax.dot_general(old, w2, NT, preferred_element_type=F32)
                    act[sl, :] = gelu(hidden)
                return carry

            lax.fori_loop(0, many, one, 0)

        return carry

    lax.fori_loop(0, TICKS, tick, 0)

    states = normed
    w2 = w2_of(chunk_at(CHUNKS - 1))
    score_tiles = []
    for r in range(PACK // TILE):
        sl = slice(r * TILE, (r + 1) * TILE)
        mixed = lax.dot_general(act[sl, :], w2, NT, preferred_element_type=F32)
        low = (acc[sl, :] + mixed).astype(BF16)
        states[sl, :] = low
        score_tiles.append(lax.dot_general(hk[...], low, NT, preferred_element_type=F32))
    scores = jnp.concatenate(score_tiles, axis=1)
    row = lax.broadcasted_iota(I32, (HEADS, PACK), 1)
    all_weights = []
    for j in range(4):
        if j > 0:
            wait_recv(cn_r.at[j], cn_rs.at[j])
        first = offsets[j]
        count = cn_r[j][0:1, 0:1]
        member = jnp.logical_and(row >= first, row < first + count)
        masked = jnp.where(member, scores, -1e30)
        highest = jnp.max(masked, axis=1, keepdims=True)
        raised = jnp.exp(masked - highest)
        all_weights.append(raised / jnp.sum(raised, axis=1, keepdims=True))
    weights = jnp.concatenate(all_weights, axis=0).astype(BF16)
    mean_states = jnp.dot(weights, states[...], preferred_element_type=F32).astype(BF16)
    local[2].wait()
    local[3].wait()
    full = jnp.dot(mean_states, vw[...], preferred_element_type=F32)
    head_of = lax.div(lax.broadcasted_iota(I32, (HEADS, D), 1), HEAD_DIM)
    own_head = head_of == lax.broadcasted_iota(I32, (HEADS, D), 0)
    values = [
        jnp.sum(jnp.where(own_head, full[HEADS * j:HEADS * (j + 1), :], 0.0), axis=0, keepdims=True)
        for j in range(4)
    ]
    mixed = jnp.concatenate(values + [jnp.zeros((12, D), F32)], axis=0).astype(BF16)
    pooled = jnp.dot(mixed, ow[...], preferred_element_type=F32)[0:8, :]
    image_inv = lax.rsqrt(jnp.sum(pooled * pooled, axis=1, keepdims=True) + EPSILON)
    image_unit = pooled * image_inv
    image_low = jnp.concatenate([image_unit, jnp.zeros((8, D), F32)], axis=0).astype(BF16)
    ix_s[...] = image_unit[0:4].astype(BF16)

    def send_images(i, carry):
        q = lax.rem(place + i, PLANE)
        rcopy(ix_s, ix_r.at[place], ix_ss.at[i], ix_rs.at[place], in_plane(q)).start()
        return carry

    lax.fori_loop(1, PLANE, send_images, 0)
    ix_r[place] = ix_s[...]

    mult = scale[0]
    shift = bias[0]

    wait_recv(T.at[:, 1 - k], ts_rs.at[0])
    texts = T[...].reshape(TEXTS, D)
    own_logits = mult * lax.dot_general(image_low, texts, NT, preferred_element_type=F32) + shift
    slot = lax.broadcasted_iota(I32, (16, 1), 0)
    slot4 = m4(slot)
    own_ids = 4 * (g * 32 + lax.rem(d + 32 - 8 * slot4, 32)) + slot4
    own_lab = label_cols(own_ids)
    sign = jnp.where(own_lab == labels[...].astype(F32), 1.0, -1.0)
    signed = sign * own_logits
    terms = jnp.log1p(jnp.exp(-jnp.abs(signed))) + jnp.maximum(-signed, 0.0)
    terms = jnp.where(slot < 4, terms, 0.0)
    part_loss = jnp.sum(jnp.sum(terms, axis=1, keepdims=True), axis=0, keepdims=True)
    ls_s[0] = jnp.broadcast_to(part_loss, (8, LANES))
    for i in range(3):
        rcopy(ls_s.at[0], ls_r.at[0, x], l1_ss.at[i], l1_rs.at[x], xs[i]).start()
    ls_r[0, x] = ls_s[0]

    others = [(m4(y + i), c_) for i in (1, 2, 3) for c_ in (0, 1)]
    to_plane = [dev(x, yy, z, c_) for yy, c_ in others] + [sib]

    own_slope = (mult * -sign * jax.nn.sigmoid(-signed)).astype(BF16)
    image_push = jnp.dot(own_slope, texts, preferred_element_type=F32)[0:8, :]
    image_grad = (
        image_push - image_unit * jnp.sum(image_unit * image_push, axis=1, keepdims=True)
    ) * image_inv
    for j in range(4):
        ig_s[j] = image_grad[j:j + 1, :]
    for j in (1, 2, 3):
        rcopy(ig_s.at[j], ig_r.at[j], ig_ss.at[j], ig_rs.at[j], group_dev[4 - j]).start()
    ig_r[0] = ig_s[0]

    for i in (1, 2, 3):
        s = m4(x + i)
        wait_recv(ls_r.at[0, s], l1_rs.at[s])
    ls_s[1] = ls_r[0, 0] + ls_r[0, 1] + ls_r[0, 2] + ls_r[0, 3]
    me8 = k * 4 + y
    for i, to in enumerate(to_plane):
        rcopy(ls_s.at[1], ls_r.at[1, me8], l2_ss.at[i], l2_rs.at[me8], to).start()
    ls_r[1, me8] = ls_s[1]

    def take_images(i, carry):
        q = lax.rem(place + i, PLANE)
        wait_recv(ix_r.at[q], ix_rs.at[q])
        return carry

    lax.fori_loop(1, PLANE, take_images, 0)
    for q in range(PLANE):
        plane_f[4 * q:4 * q + 4, :] = ix_r[q].astype(F32)
    plane = plane_f[...].astype(BF16)
    plane_logits = mult * lax.dot_general(
        tcol[...].astype(BF16), plane, NT, preferred_element_type=F32
    ) + shift
    plane_sign = jnp.where(tlab[...] == ilab[0:1, :], 1.0, -1.0)
    plane_slope = (mult * -plane_sign * jax.nn.sigmoid(-plane_sign * plane_logits)).astype(BF16)
    push = jnp.dot(plane_slope, plane, preferred_element_type=F32)
    for zz in range(8):
        ps_s[zz] = push[8 * zz:8 * zz + 4, :]
    for i in (3, 2, 4, 1, 5, 0, 6):
        to_z = m8(z + i + 1)
        rcopy(ps_s.at[to_z], ps_r.at[z], ps_ss.at[i], ps_rs.at[z], zs[i]).start()
    ps_r[z] = ps_s[z]

    for yy, c_ in others + [(y, 1 - k)]:
        wait_recv(ls_r.at[1, c_ * 4 + yy], l2_rs.at[c_ * 4 + yy])
    total = ls_r[1, 0]
    for i in range(1, 8):
        total = total + ls_r[1, i]
    ls_s[2] = total
    for i in range(7):
        rcopy(ls_s.at[2], ls_r.at[2, z], l3_ss.at[i], l3_rs.at[z], zs[i]).start()
    ls_r[2, z] = ls_s[2]

    for j in (1, 2, 3):
        wait_recv(ig_r.at[j], ig_rs.at[j])
    for j in range(4):
        grads_out[j:j + 1, :] = ig_r[j]

    def drain(c, carry):
        own = own_blocks.at[c]

        @pl.when(edge)
        def _():
            wait_send(own, g_ss.at[Z, c])

        wait_send(G.at[c, k], g_ss.at[SIB, c])

        @pl.when(c < GATHERED)
        def _():
            e = gathered(c)
            for kind in (A_MINUS, A_PLUS, A_FAR):
                wait_send(own, g_ss.at[kind, e])
            for kind in (B_MINUS, B_PLUS, B_FAR):
                wait_send(b_group(e, b), g_ss.at[kind, e])

            @pl.when(c < SHARED)
            def _():
                wait_send(G.at[e, k], g_ss.at[HAND, 2 * c + parity])

        return carry

    lax.fori_loop(0, CHUNKS, drain, 0)

    @pl.when(source)
    def _():
        for p in range(len(PIECES)):
            for i in range(3):
                wait_send(a2a_s.at[0, :, piece_lanes(p)], x_ss.at[p, i])

    for i in range(3):
        wait_send(tx_s, tx_ss.at[i])
        wait_send(T.at[zl, k, zh, own_t, :], ty_ss.at[i])
        wait_send(ls_s.at[0], l1_ss.at[i])
        wait_send(cn_s.at[i + 1], cn_ss.at[i + 1])
        wait_send(ig_s.at[i + 1], ig_ss.at[i + 1])
        wait_send(text_ring(0), tz_ss.at[0, i])
        wait_send(text_ring(0), tz_ss.at[1, i])
    wait_send(text_ring(0), tz_ss.at[0, 3])
    wait_send(T.at[:, k], ts_ss.at[0])
    for i in range(1, 8):
        zz = m8(z + i)
        wait_recv(ps_r.at[zz], ps_rs.at[zz])
    text_push = ps_r[0]
    for i in range(1, 8):
        text_push = text_push + ps_r[i]
    grads_out[4:8, :] = (
        text_push - text_unit * jnp.sum(text_unit * text_push, axis=1, keepdims=True)
    ) * text_inv

    for i in range(1, 8):
        zz = m8(z + i)
        wait_recv(ls_r.at[2, zz], l3_rs.at[zz])
    total = ls_r[2, 0]
    for i in range(1, 8):
        total = total + ls_r[2, i]
    loss_out[...] = total[0:1, 0:1] / float(TEXTS)

    def sent_images(i, carry):
        wait_send(ix_s, ix_ss.at[i])
        return carry

    lax.fori_loop(1, PLANE, sent_images, 0)
    for i in range(7):
        wait_send(ls_s.at[1], l2_ss.at[i])
        wait_send(ps_s.at[0], ps_ss.at[i])
        wait_send(ls_s.at[2], l3_ss.at[i])


def per_device(
    patches, patch_counts, pack_offsets, norm_gain, mlp_in, mlp_out, probe_query, key_weight,
    value_weight, out_weight, text_embed, pair_label, logit_scale, logit_bias,
):
    vmem = pl.BlockSpec(memory_space=pltpu.VMEM)
    smem = pl.BlockSpec(memory_space=pltpu.SMEM)
    anywhere = pl.BlockSpec(memory_space=pl.ANY)
    dma = pltpu.SemaphoreType.DMA
    loss, grads = pl.pallas_call(
        kernel,
        out_shape=(
            jax.ShapeDtypeStruct((1, 1), F32),
            jax.ShapeDtypeStruct((8, D), F32),
        ),
        in_specs=[
            anywhere, smem, smem, vmem, anywhere, anywhere, vmem, anywhere, anywhere, anywhere, vmem, vmem, smem, smem,
        ],
        out_specs=(vmem, vmem),
        scratch_shapes=[
            pltpu.VMEM((PACK, D), BF16),
            pltpu.VMEM((PACK, D), BF16),
            pltpu.VMEM((PACK, D), F32),
            pltpu.VMEM((PACK, 2 * LANES), BF16),
            pltpu.VMEM((CHUNKS, 2, 4, GROUP, LANES), BF16),
            pltpu.VMEM((CHUNKS, BLOCK, LANES), BF16),
            pltpu.VMEM((SHARD, FF), BF16),
            pltpu.VMEM((SHARD, FF), BF16),
            pltpu.VMEM((4, SLOT_ROWS, HALF), BF16),
            pltpu.VMEM((4, SLOT_ROWS, HALF), BF16),
            pltpu.VMEM((BLOCK, HALF), F32),
            pltpu.VMEM((4, 2, 2, 64, D), BF16),
            pltpu.VMEM((16, D), F32),
            pltpu.VMEM((16, D), BF16),
            pltpu.VMEM((4, 16, D), BF16),
            pltpu.VMEM((4, D), BF16),
            pltpu.VMEM((PLANE, 4, D), BF16),
            pltpu.VMEM((LANES, D), F32),
            pltpu.VMEM((64, D), F32),
            pltpu.VMEM((8, 4, D), F32),
            pltpu.VMEM((8, 4, D), F32),
            pltpu.VMEM((4, 1, D), F32),
            pltpu.VMEM((4, 1, D), F32),
            pltpu.VMEM((4, 8, LANES), I32),
            pltpu.VMEM((4, 8, LANES), I32),
            pltpu.VMEM((HEADS, D), BF16),
            pltpu.VMEM((D, D), BF16),
            pltpu.VMEM((D, D), BF16),
            pltpu.VMEM((D, D), BF16),
            pltpu.VMEM((8, LANES), F32),
            pltpu.VMEM((64, LANES), F32),
            pltpu.VMEM((3, 8, LANES), F32),
            pltpu.VMEM((3, 8, 8, LANES), F32),
            dma((7,)),
            dma((9, CHUNKS)), dma((9, CHUNKS)),
            dma((3, 3)), dma((3, 4)),
            dma((3,)), dma((4,)),
            dma((3,)), dma((4,)),
            dma((2, 4)), dma((2, 4)),
            dma((1,)), dma((1,)),
            dma((PLANE,)), dma((PLANE,)),
            dma((7,)), dma((8,)),
            dma((4,)), dma((4,)),
            dma((4,)), dma((4,)),
            dma((3,)), dma((4,)),
            dma((7,)), dma((8,)),
            dma((7,)), dma((8,)),
        ],
        compiler_params=pltpu.CompilerParams(
            collective_id=0, has_side_effects=True, vmem_limit_bytes=62 * 2**20
        ),
        cost_estimate=pl.CostEstimate(
            flops=4 * PACK * D * FF, bytes_accessed=12 * 2**20, transcendentals=PACK * FF
        ),
        name="pooled_loss",
    )(
        patches, patch_counts, pack_offsets, norm_gain, mlp_in, mlp_out.T,
        probe_query, key_weight, value_weight, out_weight, text_embed,
        pair_label.reshape(1, TEXTS), logit_scale, logit_bias,
    )
    return loss.reshape(()), grads[0:4], grads[4:8]


def solution(mesh):
    placed = (
        P(("grp", "dp"), None), P(("grp", "dp")), P(("grp", "dp")), P(), P("dp", None), P(None, "dp"),
        P(), P(), P(), P(), P(("grp", "dp"), None), P(), P(), P(),
    )
    return jax.shard_map(
        per_device,
        mesh=mesh,
        in_specs=placed,
        out_specs=(P(), P(("grp", "dp"), None), P(("grp", "dp"), None)),
        check_vma=False,
    )
```
